128 devices in a mesh: dp: 2 (over core), ep: 64 (over z, y, x).
Axes of the slice: x: 4, y: 4, z: 4, core: 2. Of those that a mesh axis runs over, the one named last changes fastest.
Arguments:
- kv_cache: bfloat16 [4096, 36864], P(('dp', 'ep')), may hold values from -6 to 6
- lengths: int32 [4096], P(('dp', 'ep')), may hold values from 1 to 62, as said below
- move_list: int32 [4096, 2], P(('dp', 'ep')), may hold values from 0 to 63, as said below
- queries: bfloat16 [2, 4096, 36864], P(None, ('dp', 'ep')), may hold values from -125 to 125
- new_kv: bfloat16 [2, 4096, 576], P(None, ('dp', 'ep')), may hold values from -6 to 6
- hidden: bfloat16 [2, 4096, 3584], P(None, ('dp', 'ep')), may hold values from -6 to 6
- expert_ids: int32 [2, 4096, 8], P(None, ('dp', 'ep')), may hold values from 0 to 63, all different within a row; in each aligned block of 32 rows (0 to 31, 32 to 63, ..., all dimensions but the last counted through in order) at most 8 rows name the same one
- gate_weights: float32 [2, 4096, 8], P(None, ('dp', 'ep')), may hold values from 0.2 to 1
- expert_gate: bfloat16 [64, 3584, 1024], P('ep', None, 'dp'), may hold values from -0.09375 to 0.09375
- expert_up: bfloat16 [64, 3584, 1024], P('ep', None, 'dp'), may hold values from -0.09375 to 0.09375
- expert_down: bfloat16 [64, 1024, 3584], P('ep', 'dp'), may hold values from -0.1875 to 0.1875
Outputs:
- context: bfloat16 [2, 4096, 32768], P(None, ('dp', 'ep'))
- expert_mix: bfloat16 [2, 4096, 3584], P(None, ('dp', 'ep'))
The draws below stay inside these ranges and needn't reach their ends.
Inputs may be any that keep to these rules, and one draw needn't show every extreme that they name: `lengths`: each slot's count of cached positions; room is left for the 2 new tokens. `move_list`: destinations lie in the same dp index as the source. Each device sends its 32 requests and receives exactly 32, into distinct slots; between two devices move either none or exactly 1 request. `expert_ids`: in each step, among the 32 tokens of one device no expert is named more than 8 times; a token names 8 different experts.
All inputs are finite; a program needn't handle non-finite values.
Results may differ from the reference program's by a relative error of at most 0.0058.
Values may be sent and summed in bfloat16 or wider, within the bound.
No kernel may reach another device: no remote copies, remote signals or barrier semaphores. Data moves between devices by JAX's collectives and lax.ppermute only.
A program may use at most 192 MiB of HBM per device.

```python
import math
import jax
import jax.numpy as jnp
import numpy as np
from jax import lax

D = 3584
H = 64
LAT = 512
FF = 1024
TOPK = 8
STEPS = 2
R_DEV = 32
CTX = 64
KVW = 576
EXPERTS = 64
REQS = 4096
CAP = 1
CAPE = 8
N_DP = 2
N_EP = 64


def shared_draws(key):
    key_query, key_new = jax.random.split(key, 2)
    query_base = jnp.clip(jax.random.normal(key_query, (STEPS, REQS, H, KVW), jnp.float32), -6.0, 6.0)
    new_base = jnp.clip(jax.random.normal(key_new, (STEPS, REQS, KVW), jnp.float32), -6.0, 6.0)
    return (query_base, new_base)


def draw_new_kv(key, part):
    query_base, new_base = shared_draws(key)
    result = new_base
    return result.astype(jnp.bfloat16)


def draw_queries(key, part):
    query_base, new_base = shared_draws(key)
    result = query_base
    return result.reshape(STEPS, REQS, H * KVW).astype(jnp.bfloat16)


def draw_lengths(key, part):
    key = jax.random.fold_in(key, 3)
    values = jax.random.randint(key, (REQS,), 1, CTX - STEPS + 1, dtype=jnp.int32)
    values = values.at[0].set(CTX - STEPS).at[1].set(1)
    return values.astype(jnp.int32)


def permute_rows(key, rows, width):

    def single(row_key):
        return jax.random.permutation(row_key, width).astype(jnp.int32)
    return jax.vmap(single)(jax.random.split(key, rows))


def draw_move_list(key, part):
    key = jax.random.fold_in(key, 5)
    groups_of = R_DEV // CAP

    def one_group(group_key):
        keys = jax.random.split(group_key, 5)
        shifted = jax.random.permutation(keys[0], N_EP).astype(jnp.int32)
        renamed = jax.random.permutation(keys[1], N_EP).astype(jnp.int32)
        chosen_blocks = jax.random.permutation(keys[2], N_EP).astype(jnp.int32)[:groups_of]
        pairing = permute_rows(keys[3], N_EP, R_DEV)
        arrival = permute_rows(keys[4], N_EP, groups_of)
        which = pairing // CAP
        within = pairing % CAP
        landing = (shifted[:, None] + chosen_blocks[which]) % N_EP
        destination = renamed[landing]
        slot_there = arrival[destination, which] * CAP + within
        return jnp.stack([destination, slot_there], axis=-1).reshape(N_EP * R_DEV, 2)
    result = jax.vmap(one_group)(jax.random.split(key, N_DP))
    return result.reshape(REQS, 2).astype(jnp.int32)


def levels(rng, dims, shards, low, top_value):
    factor_of = 1.0
    for dim, parts in shards:
        steps = jax.random.uniform(jax.random.fold_in(jax.random.fold_in(rng, 6), dim), (parts,), jnp.float32, low / len(shards), top_value / len(shards))
        factor_of = factor_of * jnp.repeat(jnp.exp(steps), dims[dim] // parts).reshape((-1,) + (1,) * (len(dims) - 1 - dim))
    return factor_of


def deal_out(rng, own, number, rows, number_of, top, most, skew):
    sequence = jax.random.permutation(rng, number_of)
    heavy_load, usual = shares(number_of, rows * top, most, skew, True), shares(number_of, rows * top, most, skew, False)
    places = jnp.arange(number_of)

    def named(sizes, turn):
        used = int((sizes > 0).sum())
        fixed = max(1, used // 4)
        moved = fixed + (places - fixed + turn * (used - fixed)) % max(1, number_of - fixed)
        return jnp.zeros((number_of,), jnp.int32).at[sequence[jnp.where(places < fixed, places, moved)]].set(jnp.asarray(sizes, jnp.int32))

    sizes = jnp.where(number % 4 == 0, named(heavy_load, number // 4), named(usual, number - number // 4 - 1))
    mixed = jax.random.permutation(jax.random.fold_in(own, 3), number_of)
    source_of, receiver = mixed[0:number_of // 2 * 2:2], mixed[1:number_of // 2 * 2:2]
    slack = jnp.minimum(sizes[source_of] - 1, most - sizes[receiver]) // 2
    slack = jnp.where((source_of == sequence[0]) | (receiver == sequence[0]) | (sizes[receiver] == 0), 0, jnp.maximum(slack, 0))
    moved = jax.random.randint(jax.random.fold_in(own, 4), (number_of // 2,), 0, 1 << 20) % (slack + 1)
    sizes = sizes.at[source_of].add(-moved).at[receiver].add(moved)
    labels = jnp.searchsorted(jnp.cumsum(sizes), jnp.arange(rows * top), side="right").astype(jnp.int32)
    grid = labels.reshape(top, rows).T
    grid = grid[jax.random.permutation(jax.random.fold_in(own, 1), rows)]
    turn = jax.random.randint(jax.random.fold_in(own, 2), (rows, 1), 0, top)
    return jnp.take_along_axis(grid, (jnp.arange(top)[None, :] + turn) % top, axis=1)


def shares(count, total, bound, skew, full):
    loads = [(1 << 20) // math.isqrt(standing ** skew) + 1 for standing in range(1, count + 1)]
    largest = bound if full else min(bound, max(-(-total // count), total * loads[0] // sum(loads)))
    least = 1 if total - largest >= count - 1 else 0
    counts, rest = [largest] + [least] * (count - 1), total - largest - least * (count - 1)
    while rest > 0:
        candidates = [i for i in range(1, count) if counts[i] < largest] or [i for i in range(1, count) if counts[i] < bound]
        pool, budget = sum([loads[i] for i in candidates]), rest
        for i in candidates:
            extra = min(bound - counts[i], max(1, budget * loads[i] // pool), rest)
            counts[i] = counts[i] + extra
            rest = rest - extra
    return np.array(counts)


def normal_values(rng, shape, spread, limit, shards=(), held_as=jnp.bfloat16):
    values = jax.random.normal(rng, shape, jnp.float32) * spread
    if len(shards) > 0:
        values = levels(rng, shape, shards, -0.22, 0.18) * values
    return jnp.clip(values, min=-limit, max=limit).astype(held_as)


def setup_inputs(seed: int = 0) -> dict:
    seeds = jax.random.split(jax.random.key(seed), 12)
    kv_cache = normal_values(seeds[0], (REQS, CTX * KVW), 1.0, 6.0, ((0, 128),))
    lengths = draw_lengths(jax.random.fold_in(seeds[11], 71), 0)
    move_list = draw_move_list(jax.random.fold_in(seeds[11], 71), 0)
    queries = draw_queries(jax.random.fold_in(seeds[11], 71), 0)
    new_kv = draw_new_kv(jax.random.fold_in(seeds[11], 71), 0)
    hidden = normal_values(seeds[5], (STEPS, REQS, D), 1.0, 6.0, ((1, 128),))
    expert_ids_keys = jax.random.split(jax.random.fold_in(seeds[6], 1), STEPS * REQS // R_DEV)
    expert_ids_turns = jax.random.permutation(jax.random.fold_in(seeds[6], 3), STEPS * REQS // R_DEV)
    expert_ids = jax.vmap(lambda own, number: deal_out(jax.random.fold_in(seeds[6], 2), own, number, R_DEV, EXPERTS, TOPK, CAPE, 2))(expert_ids_keys, expert_ids_turns).reshape((STEPS, REQS, TOPK))
    gate_weights = jnp.clip(0.2 + 0.8 * jax.random.uniform(seeds[7], (STEPS, REQS, TOPK), jnp.float32) ** levels(seeds[7], (STEPS, REQS, TOPK), ((1, 128),), -0.2, 0.2), 0.2, 1.0)
    expert_gate = normal_values(seeds[8], (EXPERTS, D, FF), D ** -0.5, 0.09375, ((0, 64), (2, 2)))
    expert_up = normal_values(seeds[9], (EXPERTS, D, FF), D ** -0.5, 0.09375, ((0, 64), (2, 2)))
    expert_down = normal_values(seeds[10], (EXPERTS, FF, D), FF ** -0.5, 0.1875, ((0, 64), (1, 2)))
    return dict(kv_cache=kv_cache, lengths=lengths, move_list=move_list, queries=queries, new_kv=new_kv, hidden=hidden, expert_ids=expert_ids, gate_weights=gate_weights, expert_gate=expert_gate, expert_up=expert_up, expert_down=expert_down)


score_scale = 192.0 ** -0.5


def attend_block(query_block, new_block, cache_rows, cached_len):
    request_count = cache_rows.shape[0]
    cached_keys = cache_rows.reshape(request_count, CTX, KVW).astype(jnp.float32)
    new_keys = new_block.astype(jnp.float32)
    position = jnp.arange(CTX, dtype=jnp.int32)
    cached_live = position[None, :] < cached_len[:, None]
    results = []
    for decode_step in range(STEPS):
        query_rows = query_block[decode_step].reshape(request_count, H, KVW).astype(jnp.float32)
        recent = new_keys[: decode_step + 1]
        cached_score = jnp.einsum("rhc,rpc->rhp", query_rows, cached_keys) * score_scale
        cached_score = jnp.where(cached_live[:, None, :], cached_score, -jnp.inf)
        recent_score = jnp.einsum("rhc,src->rhs", query_rows, recent) * score_scale
        row_max = jnp.maximum(jnp.max(cached_score, axis=-1), jnp.max(recent_score, axis=-1))[..., None]
        cached_exp = jnp.exp(cached_score - row_max)
        recent_exp = jnp.exp(recent_score - row_max)
        denominator = jnp.sum(cached_exp, axis=-1, keepdims=True) + jnp.sum(recent_exp, axis=-1, keepdims=True)
        cached_prob = lax.optimization_barrier((cached_exp / denominator).astype(jnp.bfloat16)).astype(jnp.float32)
        recent_prob = lax.optimization_barrier((recent_exp / denominator).astype(jnp.bfloat16)).astype(jnp.float32)
        mixed = jnp.einsum("rhp,rpl->rhl", cached_prob, cached_keys[:, :, :LAT])
        mixed = mixed + jnp.einsum("rhs,srl->rhl", recent_prob, recent[:, :, :LAT])
        results.append(mixed.astype(jnp.bfloat16).reshape(request_count, H * LAT))
    return jnp.stack(results)


def experts_step(tokens, chosen, weights, expert_gate, expert_up, expert_down):
    half_units = FF // N_DP
    capacity = N_DP * N_EP * CAPE

    def per_expert(running, scanned):
        gate_mat, up_mat, down_mat, expert = scanned
        member = chosen == expert
        picked = jnp.any(member, axis=1)
        row_index = jnp.nonzero(picked, size=capacity, fill_value=0)[0].astype(jnp.int32)
        filled = jnp.arange(capacity, dtype=jnp.int32) < jnp.sum(picked.astype(jnp.int32))
        picked_rows = tokens[row_index]
        summed = jnp.zeros((capacity, D), jnp.float32)
        for portion in range(N_DP):
            low = portion * half_units
            gate_pre = jnp.dot(picked_rows, gate_mat[:, low:low + half_units], preferred_element_type=jnp.float32)
            up_pre = jnp.dot(picked_rows, up_mat[:, low:low + half_units], preferred_element_type=jnp.float32)
            hidden_act = (jax.nn.silu(gate_pre) * up_pre).astype(jnp.bfloat16)
            part_out = jnp.dot(hidden_act, down_mat[low:low + half_units, :], preferred_element_type=jnp.float32)
            summed = summed + lax.optimization_barrier(part_out.astype(jnp.bfloat16)).astype(jnp.float32)
        factor = jnp.sum(jnp.where(member, weights, 0.0), axis=1)[row_index]
        factor = jnp.where(filled, factor, 0.0)
        return running.at[row_index].add(factor[:, None] * summed), None

    start = jnp.zeros((REQS, D), jnp.float32)
    running, _ = lax.scan(per_expert, start, (expert_gate, expert_up, expert_down, jnp.arange(EXPERTS, dtype=jnp.int32)))
    return running.astype(jnp.bfloat16)


def reference(kv_cache, lengths, move_list, queries, new_kv, hidden, expert_ids, gate_weights, expert_gate, expert_up, expert_down):
    group_size = N_EP * R_DEV
    source = jnp.arange(REQS, dtype=jnp.int32)
    target = ((source // group_size) * N_EP + move_list[:, 0]) * R_DEV + move_list[:, 1]
    placed_cache = jnp.zeros_like(kv_cache).at[target].set(kv_cache)
    placed_len = jnp.zeros_like(lengths).at[target].set(lengths)
    blocks = N_DP * N_EP
    query_blocks = queries.reshape(STEPS, blocks, R_DEV, H * KVW).transpose(1, 0, 2, 3)
    new_blocks = new_kv.reshape(STEPS, blocks, R_DEV, KVW).transpose(1, 0, 2, 3)

    def one_block(scanned):
        return attend_block(scanned[0], scanned[1], scanned[2], scanned[3])

    context = lax.map(one_block, (query_blocks, new_blocks, placed_cache.reshape(blocks, R_DEV, CTX * KVW), placed_len.reshape(blocks, R_DEV)))
    context = context.transpose(1, 0, 2, 3).reshape(STEPS, REQS, H * LAT)
    expert_mix = jnp.stack([experts_step(hidden[decode_step], expert_ids[decode_step], gate_weights[decode_step], expert_gate, expert_up, expert_down) for decode_step in range(STEPS)])
    return context, expert_mix
```

```python
import jax
import jax.numpy as jnp
from jax import lax
from jax.sharding import PartitionSpec as P

D = 3584
H = 64
LAT = 512
TOPK = 8
STEPS = 2
CTX = 64
KVW = 576


score_scale = 192.0 ** (-0.5)


def attend(query_all, new_all, cache_rows, cached_len):
    request_count = cache_rows.shape[0]
    cached_keys = cache_rows.reshape(request_count, CTX - STEPS, KVW)
    cached_values = cached_keys[:, :, :LAT]
    cached_live = jnp.arange(CTX - STEPS, dtype=jnp.int32)[None, :] < cached_len[:, None]
    results = []
    for decode_step in range(STEPS):
        query_rows = query_all[decode_step].reshape(request_count, H, KVW)
        recent = new_all[: decode_step + 1]
        cached_score = (
            jnp.einsum("rhc,rpc->rhp", query_rows, cached_keys, preferred_element_type=jnp.float32)
            * score_scale
        )
        cached_score = jnp.where(cached_live[:, None, :], cached_score, -jnp.inf)
        recent_score = (
            jnp.einsum("rhc,src->rhs", query_rows, recent, preferred_element_type=jnp.float32)
            * score_scale
        )
        row_max = jnp.maximum(jnp.max(cached_score, axis=-1), jnp.max(recent_score, axis=-1))[
            ..., None
        ]
        cached_exp = jnp.exp(cached_score - row_max)
        recent_exp = jnp.exp(recent_score - row_max)
        denominator = jnp.sum(cached_exp, axis=-1, keepdims=True) + jnp.sum(
            recent_exp, axis=-1, keepdims=True
        )
        cached_prob = (cached_exp / denominator).astype(jnp.bfloat16)
        recent_prob = (recent_exp / denominator).astype(jnp.bfloat16)
        mixed = jnp.einsum(
            "rhp,rpl->rhl", cached_prob, cached_values, preferred_element_type=jnp.float32
        )
        mixed = mixed + jnp.einsum(
            "rhs,srl->rhl", recent_prob, recent[:, :, :LAT], preferred_element_type=jnp.float32
        )
        results.append(mixed.astype(jnp.bfloat16).reshape(request_count, H * LAT))
    return jnp.stack(results)


def expert_rows(token_rows, halves):
    total = None
    for gate_mat, up_mat, down_mat in halves:
        gate_pre = jnp.dot(token_rows, gate_mat, preferred_element_type=jnp.float32)
        up_pre = jnp.dot(token_rows, up_mat, preferred_element_type=jnp.float32)
        inner = (jax.nn.silu(gate_pre) * up_pre).astype(jnp.bfloat16)
        part = jnp.dot(inner, down_mat, preferred_element_type=jnp.float32)
        total = part if total is None else total + part
    return total.astype(jnp.bfloat16)


def three_parts(weights):
    high = lax.reduce_precision(weights, 8, 7)
    rest = weights - high
    mid = lax.reduce_precision(rest, 8, 7)
    return [part.astype(jnp.bfloat16) for part in (high, mid, rest - mid)]


def on_device(
    kv_cache,
    lengths,
    move_list,
    queries,
    new_kv,
    hidden,
    expert_ids,
    gate_weights,
    expert_gate,
    expert_up,
    expert_down,
):
    ep_count = lax.axis_size("ep")
    slot_count = lengths.shape[0]
    per_expert = 2 * slot_count * TOPK // ep_count
    swap = [(0, 1), (1, 0)]
    own = (expert_gate[0], expert_up[0], expert_down[0])
    other = tuple(lax.ppermute(w, "dp", swap) for w in own)
    halves = (own, other)
    expert_range = jnp.arange(ep_count, dtype=jnp.int32)
    buffer_rank = jnp.arange(ep_count * per_expert, dtype=jnp.int32) % per_expert
    combines = []
    arrivals = []
    for decode_step in range(STEPS):
        tokens = hidden[decode_step]
        chosen = expert_ids[decode_step]
        weights = gate_weights[decode_step]
        member = chosen[:, :, None] == expert_range[None, None, :]
        picked = jnp.any(member, axis=1).astype(jnp.int32)
        factor = jnp.sum(jnp.where(member, weights[:, :, None], 0.0), axis=1)
        earlier = jnp.cumsum(picked, axis=0) - picked
        buffer_hit = (jnp.repeat(picked, per_expert, axis=1) > 0) & (
            jnp.repeat(earlier, per_expert, axis=1) == buffer_rank[None, :]
        )
        packed = jnp.einsum(
            "tb,td->bd", buffer_hit.astype(jnp.bfloat16), tokens, preferred_element_type=jnp.float32
        ).astype(jnp.bfloat16)
        combines.append(jnp.where(buffer_hit, jnp.repeat(factor, per_expert, axis=1), 0.0))
        arrivals.append(
            lax.all_to_all(
                packed.reshape(ep_count, per_expert, D), "ep", split_axis=0, concat_axis=0, tiled=True
            )
        )
    slot_range = jnp.arange(slot_count, dtype=jnp.int32)
    target_dev = move_list[:, 0]
    target_slot = move_list[:, 1]
    send_hit = expert_range[:, None] == target_dev[None, :]
    sent_slot = jnp.sum(jnp.where(send_hit, target_slot[None, :] + 1, 0), axis=1) - 1
    sent_len = jnp.sum(jnp.where(send_hit, lengths[None, :], 0), axis=1)
    tail = jnp.concatenate(
        [sent_slot[:, None], sent_len[:, None], jnp.zeros((ep_count, 126), jnp.int32)], axis=1
    ).astype(jnp.bfloat16)
    live_width = (CTX - STEPS) * KVW
    packed_cache = jnp.dot(
        send_hit.astype(jnp.bfloat16), kv_cache[:, :live_width], preferred_element_type=jnp.float32
    ).astype(jnp.bfloat16)
    packed_cache = jnp.concatenate([packed_cache, tail], axis=1)
    packed_cache, _ = lax.optimization_barrier((packed_cache, arrivals[1]))
    got_cache = lax.all_to_all(packed_cache, "ep", split_axis=0, concat_axis=0, tiled=True)
    got_slot = got_cache[:, live_width].astype(jnp.int32)
    got_len = got_cache[:, live_width + 1].astype(jnp.int32)
    land_hit = got_slot[None, :] == slot_range[:, None]
    placed_len = jnp.sum(jnp.where(land_hit, got_len[None, :], 0), axis=1)
    placed = jnp.dot(
        land_hit.astype(jnp.bfloat16), got_cache[:, :live_width], preferred_element_type=jnp.float32
    ).astype(jnp.bfloat16)
    context = attend(queries, new_kv, placed, placed_len)
    mixtures = []
    for decode_step in range(STEPS):
        produced = expert_rows(arrivals[decode_step].reshape(-1, D), halves)
        produced, _ = lax.optimization_barrier((produced, got_cache))
        answers = lax.all_to_all(
            produced.reshape(ep_count, per_expert, D), "ep", split_axis=0, concat_axis=0, tiled=True
        ).reshape(-1, D)
        parts = jnp.concatenate(three_parts(combines[decode_step]), axis=0)
        mixed = jnp.dot(parts, answers, preferred_element_type=jnp.float32)
        mixed = mixed.reshape(3, slot_count, D)
        mixtures.append((mixed[0] + (mixed[1] + mixed[2])).astype(jnp.bfloat16))
    return context, jnp.stack(mixtures)


def solution(mesh):
    return jax.shard_map(
        on_device,
        mesh=mesh,
        in_specs=(
            P(("dp", "ep"), None),
            P(("dp", "ep")),
            P(("dp", "ep"), None),
            P(None, ("dp", "ep"), None),
            P(None, ("dp", "ep"), None),
            P(None, ("dp", "ep"), None),
            P(None, ("dp", "ep"), None),
            P(None, ("dp", "ep"), None),
            P("ep", None, "dp"),
            P("ep", None, "dp"),
            P("ep", "dp", None),
        ),
        out_specs=(P(None, ("dp", "ep"), None), P(None, ("dp", "ep"), None)),
        check_vma=False,
    )
```

```python
import functools

import jax
import jax.numpy as jnp
from jax import lax
from jax.experimental import pallas as pl
from jax.experimental.pallas import tpu as pltpu
from jax.sharding import PartitionSpec as P

D = 3584
H = 64
LAT = 512
TOPK = 8
STEPS = 2
CTX = 64
KVW = 576
LIVE = CTX - STEPS
SIDE = 4
SLOTS = 32
CAPE = 8
LINE = SIDE * SLOTS
PICKS = SIDE * CAPE

Z, Y, X = SIDE * SIDE, SIDE, 1
PARTS = (
    (0, 1280, (Z, Y, X)),
    (1280, 1152, (Y, X, Z)),
    (2432, 1152, (X, Z, Y)),
)
TURN = (1, -1)
SOURCES = (0, -1, 1, 2)
TARGETS = (0, 1, -1, 2)

score_scale = 192.0 ** (-0.5)


def hop(value, stride, delta):
    pairs = []
    for chip in range(SIDE**3):
        place = chip // stride % SIDE
        pairs.append((chip, chip + ((place + delta) % SIDE - place) * stride))
    return lax.ppermute(value, "ep", pairs)


def spread(block, stride, turn):
    near = hop(block, stride, turn)
    back = hop(block, stride, -turn)
    far = hop(near, stride, turn)
    return [block, near, back, far] if turn == 1 else [block, back, near, far]


def collect(blocks, stride, turn):
    own, near, back, far = blocks if turn == 1 else [blocks[i] for i in (0, 2, 1, 3)]
    passed = hop(far, stride, -turn)
    from_back = hop(back, stride, turn)
    joined = (near.astype(jnp.float32) + passed.astype(jnp.float32)).astype(jnp.bfloat16)
    from_near = hop(joined, stride, -turn)
    return (
        own.astype(jnp.float32) + from_near.astype(jnp.float32) + from_back.astype(jnp.float32)
    ).astype(jnp.bfloat16)


def deal(blocks, stride, turn):
    far = hop(hop(blocks[3], stride, turn), stride, turn)
    return [blocks[0], hop(blocks[1], stride, 1), hop(blocks[2], stride, -1), far]


def undeal(blocks, stride, turn):
    far = hop(hop(blocks[3], stride, -turn), stride, -turn)
    return [blocks[0], hop(blocks[1], stride, -1), hop(blocks[2], stride, 1), far]


def pick_matrix(target_ref, ids):
    hits = [
        jnp.sum((ids == target_ref[j]).astype(jnp.float32), axis=0, keepdims=True)
        for j in range(SIDE)
    ]
    before = lax.broadcasted_iota(jnp.int32, (LINE, LINE), 0)
    after = lax.broadcasted_iota(jnp.int32, (LINE, LINE), 1)
    earlier = ((before // SLOTS == after // SLOTS) & (before < after)).astype(jnp.bfloat16)
    stacked = jnp.concatenate(hits + hits, axis=0)
    ranks = jnp.dot(stacked.astype(jnp.bfloat16), earlier, preferred_element_type=jnp.float32)
    base = (lax.broadcasted_iota(jnp.int32, (1, LINE), 1) // SLOTS * CAPE).astype(jnp.float32)
    rows = lax.broadcasted_iota(jnp.int32, (PICKS, LINE), 0).astype(jnp.float32)
    picks = []
    for j in range(SIDE):
        place = jnp.where(hits[j] > 0.0, base + ranks[j : j + 1], -1.0)
        picks.append((rows == place).astype(jnp.float32))
    return jnp.concatenate(picks, axis=0).astype(jnp.bfloat16)


def select_kernel(target_ref, ids_ref, *refs):
    for line in range(SIDE):
        picks = pick_matrix(target_ref, ids_ref[line])
        rows = jnp.dot(picks, refs[line][...], preferred_element_type=jnp.float32)
        rows = rows.astype(jnp.bfloat16)
        for j in range(SIDE):
            refs[SIDE + j][pl.ds(line * PICKS, PICKS), :] = rows[j * PICKS : (j + 1) * PICKS]


def combine_kernel(target_ref, ids_ref, *refs):
    for line in range(SIDE):
        picks = pick_matrix(target_ref, ids_ref[line])
        rows = jnp.concatenate(
            [refs[j][pl.ds(line * PICKS, PICKS), :] for j in range(SIDE)], axis=0
        )
        total = lax.dot_general(
            picks, rows, (((0,), (0,)), ((), ())), preferred_element_type=jnp.float32
        )
        refs[SIDE + line][...] = total.astype(jnp.bfloat16)


def line_call(kernel, targets, ids, blocks):
    width = blocks[0].shape[1]
    whole = pl.BlockSpec(memory_space=pltpu.VMEM)
    return pl.pallas_call(
        kernel,
        out_shape=[jax.ShapeDtypeStruct((LINE, width), jnp.bfloat16)] * SIDE,
        in_specs=[pl.BlockSpec(memory_space=pltpu.SMEM)] + [whole] * (1 + SIDE),
        out_specs=[whole] * SIDE,
        compiler_params=pltpu.CompilerParams(vmem_limit_bytes=16 * 2**20),
        cost_estimate=pl.CostEstimate(
            flops=2 * SIDE * LINE * LINE * width,
            bytes_accessed=2 * SIDE * LINE * width * 2,
            transcendentals=0,
        ),
    )(targets, ids, *blocks)


def attend(query_all, new_all, cache_rows, cached_len):
    request_count = cache_rows.shape[0]
    cached_keys = cache_rows.reshape(request_count, LIVE, KVW)
    cached_values = cached_keys[:, :, :LAT]
    cached_live = jnp.arange(LIVE, dtype=jnp.int32)[None, :] < cached_len[:, None]
    results = []
    for decode_step in range(STEPS):
        query_rows = query_all[decode_step].reshape(request_count, H, KVW)
        recent = new_all[: decode_step + 1]
        cached_score = (
            jnp.einsum("rhc,rpc->rhp", query_rows, cached_keys, preferred_element_type=jnp.float32)
            * score_scale
        )
        cached_score = jnp.where(cached_live[:, None, :], cached_score, -jnp.inf)
        recent_score = (
            jnp.einsum("rhc,src->rhs", query_rows, recent, preferred_element_type=jnp.float32)
            * score_scale
        )
        row_max = jnp.maximum(jnp.max(cached_score, axis=-1), jnp.max(recent_score, axis=-1))[
            ..., None
        ]
        cached_exp = jnp.exp(cached_score - row_max)
        recent_exp = jnp.exp(recent_score - row_max)
        denominator = jnp.sum(cached_exp, axis=-1, keepdims=True) + jnp.sum(
            recent_exp, axis=-1, keepdims=True
        )
        cached_prob = (cached_exp / denominator).astype(jnp.bfloat16)
        recent_prob = (recent_exp / denominator).astype(jnp.bfloat16)
        mixed = jnp.einsum(
            "rhp,rpl->rhl", cached_prob, cached_values, preferred_element_type=jnp.float32
        )
        mixed = mixed + jnp.einsum(
            "rhs,srl->rhl", recent_prob, recent[:, :, :LAT], preferred_element_type=jnp.float32
        )
        results.append(mixed.astype(jnp.bfloat16).reshape(request_count, H * LAT))
    return jnp.stack(results)


def expert_rows(token_rows, row_weight, halves):
    total = None
    for gate_mat, up_mat, down_mat in halves:
        gate_pre = jnp.dot(token_rows, gate_mat, preferred_element_type=jnp.float32)
        up_pre = jnp.dot(token_rows, up_mat, preferred_element_type=jnp.float32)
        inner = (jax.nn.silu(gate_pre) * up_pre).astype(jnp.bfloat16)
        part = jnp.dot(inner, down_mat, preferred_element_type=jnp.float32)
        total = part if total is None else total + part
    return (total * row_weight).astype(jnp.bfloat16)


def on_device(
    kv_cache,
    lengths,
    move_list,
    queries,
    new_kv,
    hidden,
    expert_ids,
    gate_weights,
    expert_gate,
    expert_up,
    expert_down,
):
    chips = SIDE**3
    me = lax.axis_index("ep")

    def chip_at(stride, delta, start):
        place = start // stride % SIDE
        return start + ((place + delta) % SIDE - place) * stride

    own = (expert_gate[0], expert_up[0], expert_down[0])

    choices = jnp.concatenate([expert_ids.astype(jnp.float32), gate_weights], axis=2)
    choices = jnp.transpose(choices, (2, 0, 1)).reshape(2 * TOPK, STEPS * SLOTS)
    choices = lax.all_gather(choices, "ep")
    order = jnp.stack(
        [
            chip_at(Z, oz, chip_at(Y, oy, chip_at(X, ox, me)))
            for oz in SOURCES
            for oy in SOURCES
            for ox in SOURCES
        ]
    )
    choices = jnp.take(choices, order, axis=0)
    ids_near = choices[:, :TOPK].astype(jnp.int32).reshape(SIDE, SIDE, SIDE, TOPK, STEPS, SLOTS)
    axis_of = {Z: 0, Y: 1, X: 2}
    line_ids = []
    line_targets = []
    for _, _, axes in PARTS:
        first, second, third = (axis_of[a] for a in axes)
        plane = lax.index_in_dim(ids_near, 0, third, keepdims=True)
        plane = jnp.transpose(plane, (third, 4, second, 3, first, 5))
        line_ids.append(plane.reshape(STEPS, SIDE, TOPK, LINE))
        line_targets.append(jnp.stack([chip_at(axes[2], delta, me) for delta in TARGETS]))

    arrived = []
    for decode_step in range(STEPS):
        for part, (start, width, axes) in enumerate(PARTS):
            turn = TURN[decode_step]
            block = hidden[decode_step, :, start : start + width]
            block = jnp.concatenate(spread(block, axes[0], turn), axis=0)
            lines = spread(block, axes[1], turn)
            picked = line_call(
                select_kernel, line_targets[part], line_ids[part][decode_step], lines
            )
            arrived.append(deal(picked, axes[2], turn))

    live_width = LIVE * KVW
    chip_range = jnp.arange(chips, dtype=jnp.int32)
    slot_range = jnp.arange(SLOTS, dtype=jnp.int32)
    send_hit = chip_range[:, None] == move_list[:, 0][None, :]
    sent_slot = jnp.sum(jnp.where(send_hit, move_list[:, 1][None, :] + 1, 0), axis=1) - 1
    sent_len = jnp.sum(jnp.where(send_hit, lengths[None, :], 0), axis=1)
    tail = jnp.concatenate(
        [sent_slot[:, None], sent_len[:, None], jnp.zeros((chips, 126), jnp.int32)], axis=1
    ).astype(jnp.bfloat16)
    packed_cache = jnp.dot(
        send_hit.astype(jnp.bfloat16), kv_cache[:, :live_width], preferred_element_type=jnp.float32
    ).astype(jnp.bfloat16)
    packed_cache = jnp.concatenate([packed_cache, tail], axis=1)
    packed_cache, arrived = lax.optimization_barrier((packed_cache, arrived))
    got_cache = lax.all_to_all(packed_cache, "ep", split_axis=0, concat_axis=0, tiled=True)

    other = tuple(lax.ppermute(w, "dp", [(0, 1), (1, 0)]) for w in own)
    hit = choices[:, :TOPK] == me.astype(jnp.float32)
    factor = jnp.sum(jnp.where(hit, choices[:, TOPK:], 0.0), axis=1)
    factor = factor.reshape(chips, STEPS, SLOTS)
    chosen = jnp.any(hit, axis=1).reshape(chips, STEPS, SLOTS)
    count = chosen.astype(jnp.int32)
    rank = jnp.cumsum(count, axis=2) - count
    row_hit = chosen[..., None] & (rank[..., None] == jnp.arange(CAPE, dtype=jnp.int32))
    row_weight = jnp.sum(jnp.where(row_hit, factor[..., None], 0.0), axis=2)
    row_weight = row_weight.reshape(SIDE, SIDE, SIDE, STEPS, CAPE)
    row_weight = jnp.transpose(row_weight, (3, 2, 1, 0, 4)).reshape(STEPS, chips * CAPE, 1)

    results = []
    for decode_step in range(STEPS):
        turn = TURN[decode_step]
        columns = []
        for part, (start, width, axes) in enumerate(PARTS):
            blocks = jnp.stack(arrived[decode_step * len(PARTS) + part])
            blocks = blocks.reshape(SIDE, SIDE, SIDE, CAPE, width)
            held = (axes[2], axes[1], axes[0])
            blocks = jnp.transpose(blocks, tuple(held.index(a) for a in (X, Y, Z)) + (3, 4))
            columns.append(blocks.reshape(chips * CAPE, width))
        rows = jnp.concatenate(columns, axis=1)
        produced = expert_rows(rows, row_weight[decode_step], (own, other))
        sums = []
        for part, (start, width, axes) in enumerate(PARTS):
            blocks = produced[:, start : start + width].reshape(SIDE, SIDE, SIDE, CAPE, width)
            held = (axes[2], axes[1], axes[0])
            blocks = jnp.transpose(blocks, tuple((X, Y, Z).index(a) for a in held) + (3, 4))
            blocks = blocks.reshape(SIDE, LINE, width)
            returned = undeal([blocks[j] for j in range(SIDE)], axes[2], turn)
            lines = line_call(
                combine_kernel, line_targets[part], line_ids[part][decode_step], returned
            )
            block = collect(lines, axes[1], turn).reshape(SIDE, SLOTS, width)
            sums.append(collect([block[j] for j in range(SIDE)], axes[0], turn))
        results.append(jnp.concatenate(sums, axis=1))
    mixture = jnp.stack(results)

    got_slot = got_cache[:, live_width].astype(jnp.int32)
    got_len = got_cache[:, live_width + 1].astype(jnp.int32)
    land_hit = got_slot[None, :] == slot_range[:, None]
    placed_len = jnp.sum(jnp.where(land_hit, got_len[None, :], 0), axis=1)
    placed = jnp.dot(
        land_hit.astype(jnp.bfloat16), got_cache[:, :live_width], preferred_element_type=jnp.float32
    ).astype(jnp.bfloat16)
    context = attend(queries, new_kv, placed, placed_len)
    return context, mixture


def solution(mesh):
    return jax.shard_map(
        on_device,
        mesh=mesh,
        in_specs=(
            P(("dp", "ep"), None),
            P(("dp", "ep")),
            P(("dp", "ep"), None),
            P(None, ("dp", "ep"), None),
            P(None, ("dp", "ep"), None),
            P(None, ("dp", "ep"), None),
            P(None, ("dp", "ep"), None),
            P(None, ("dp", "ep"), None),
            P("ep", None, "dp"),
            P("ep", None, "dp"),
            P("ep", "dp", None),
        ),
        out_specs=(P(None, ("dp", "ep"), None), P(None, ("dp", "ep"), None)),
        check_vma=False,
    )
```

```python
import jax
import jax.numpy as jnp
from jax import lax
from jax.experimental import pallas as pl
from jax.experimental.pallas import tpu as pltpu
from jax.sharding import PartitionSpec as P

D = 3584
H = 64
LAT = 512
TOPK = 8
STEPS = 2
CTX = 64
KVW = 576
HALF = CTX // 2
GROUP = 16
TOGETHER = 8
WIDE = 640
SIDE = 4
Z, Y, X = SIDE * SIDE, SIDE, 1
MAIN = 2432
MINOR = D - MAIN
MARK = 128
SLOTS = 32
CAPE = 8
ROWS = STEPS * SLOTS
PICKS = STEPS * CAPE
LINE = SIDE * ROWS
PLANE = SIDE * SIDE
CHIPS = SIDE**3
ORDERS = (((Z, Y, X), (Y, X, Z)), ((X, Z, Y), (X, Z, Y)))
TARGETS = (0, 1, -1, 2)
KEYS = GROUP * (CTX + STEPS)


score_scale = 192.0 ** (-0.5)


def attend_kernel(landing_ref, got_ref, len_ref, new_ref, query_ref, out_ref, even_ref, odd_ref, value_ref, bias_ref):
    group = pl.program_id(0)
    pairs = GROUP * HALF

    def lanes(rows):
        return lax.broadcasted_iota(jnp.int32, (rows, WIDE), 1)

    def place(keys, rows, at):
        even_ref[pl.ds(at, rows), :] = keys.astype(jnp.bfloat16)
        odd_ref[pl.ds(at, rows), :] = pltpu.roll(keys, WIDE - KVW, 1).astype(jnp.bfloat16)
        value_ref[pl.ds(at, rows), :] = keys[:, :LAT].astype(jnp.bfloat16)

    def one(slot, carry):
        source = landing_ref[group * GROUP + slot]
        block = got_ref[source]
        first = jnp.where(lanes(HALF) < KVW, block[:, :WIDE].astype(jnp.float32), 0.0)
        at = pl.multiple_of(slot * HALF, HALF)
        place(first, HALF, at)
        second = block[:, LAT:].astype(jnp.float32)
        second = jnp.where(lanes(HALF) < WIDE - KVW, 0.0, second)
        place(pltpu.roll(second, KVW, 1), HALF, pl.multiple_of(pairs + at, HALF))
        return carry

    lax.fori_loop(0, GROUP, one, 0)
    for step in range(STEPS):
        rows = new_ref[step].astype(jnp.float32)
        rows = jnp.concatenate([rows, jnp.zeros((GROUP, WIDE - KVW), jnp.float32)], axis=1)
        place(rows, GROUP, 2 * pairs + step * GROUP)

    column = lax.broadcasted_iota(jnp.int32, (GROUP, KEYS), 1)
    row = lax.broadcasted_iota(jnp.int32, (GROUP, KEYS), 0)
    cached = column < 2 * pairs
    half = (column >= pairs).astype(jnp.int32)
    within = column - half * pairs
    position = 2 * (within % HALF) + half
    recent = column - 2 * pairs
    owner = jnp.where(cached, within // HALF, recent % GROUP)
    live = cached & (position < len_ref[...])
    for step in range(STEPS):
        allowed = (live | (~cached & (recent < (step + 1) * GROUP))) & (owner == row)
        bias_ref[pl.ds(step * GROUP, GROUP), :] = jnp.where(allowed, 0.0, -jnp.inf)

    def heads(index, carry):
        bias = jnp.concatenate([bias_ref[...]] * TOGETHER, axis=0)
        for odd in range(2):
            slabs = []
            for k in range(TOGETHER):
                start = pl.multiple_of((index * TOGETHER + k) * 2 * KVW + odd * LAT, 128)
                for step in range(STEPS):
                    slabs.append(query_ref[step, :, pl.ds(start, WIDE)])
            keys = odd_ref[...] if odd else even_ref[...]
            score = lax.dot_general(
                jnp.concatenate(slabs, axis=0),
                keys,
                (((1,), (1,)), ((), ())),
                preferred_element_type=jnp.float32,
            )
            score = score * score_scale + bias
            weight = jnp.exp(score - jnp.max(score, axis=1, keepdims=True))
            prob = weight * (1.0 / jnp.sum(weight, axis=1, keepdims=True))
            mixed = jnp.dot(
                prob.astype(jnp.bfloat16), value_ref[...], preferred_element_type=jnp.float32
            ).astype(jnp.bfloat16)
            for k in range(TOGETHER):
                start = pl.multiple_of(((index * TOGETHER + k) * 2 + odd) * LAT, LAT)
                for step in range(STEPS):
                    at = (k * STEPS + step) * GROUP
                    out_ref[step, :, pl.ds(start, LAT)] = mixed[at : at + GROUP]
        return carry

    lax.fori_loop(0, H // (2 * TOGETHER), heads, 0)


def attend(queries, new_kv, got, landing, placed_len):
    slots = queries.shape[1]
    return pl.pallas_call(
        attend_kernel,
        grid=(slots // GROUP,),
        out_shape=jax.ShapeDtypeStruct((STEPS, slots, H * LAT), jnp.bfloat16),
        in_specs=[
            pl.BlockSpec(memory_space=pltpu.SMEM),
            pl.BlockSpec(memory_space=pltpu.VMEM),
            pl.BlockSpec((GROUP, 1), lambda g: (g, 0)),
            pl.BlockSpec((STEPS, GROUP, KVW), lambda g: (0, g, 0)),
            pl.BlockSpec((STEPS, GROUP, H * KVW), lambda g: (0, g, 0)),
        ],
        out_specs=pl.BlockSpec((STEPS, GROUP, H * LAT), lambda g: (0, g, 0)),
        scratch_shapes=[
            pltpu.VMEM((KEYS, WIDE), jnp.bfloat16),
            pltpu.VMEM((KEYS, WIDE), jnp.bfloat16),
            pltpu.VMEM((KEYS, LAT), jnp.bfloat16),
            pltpu.VMEM((STEPS * GROUP, KEYS), jnp.float32),
        ],
        compiler_params=pltpu.CompilerParams(vmem_limit_bytes=48 * 2**20),
        cost_estimate=pl.CostEstimate(
            flops=2 * STEPS * slots * H * KEYS * (WIDE + LAT),
            bytes_accessed=2 * STEPS * slots * H * (KVW + LAT),
            transcendentals=STEPS * slots * H * KEYS,
        ),
    )(landing, got, placed_len[:, None], new_kv, queries)


def expert_rows(token_rows, row_weight, halves):
    total = None
    for gate_mat, up_mat, down_mat in halves:
        gate_pre = jnp.dot(token_rows, gate_mat, preferred_element_type=jnp.float32)
        up_pre = jnp.dot(token_rows, up_mat, preferred_element_type=jnp.float32)
        inner = (jax.nn.silu(gate_pre) * up_pre).astype(jnp.bfloat16)
        part = jnp.dot(inner, down_mat, preferred_element_type=jnp.float32)
        total = part if total is None else total + part
    return (total * row_weight).astype(jnp.bfloat16)


def hop(value, strides, delta):
    pairs = []
    for core, stride in enumerate(strides):
        for chip in range(CHIPS):
            place = chip // stride % SIDE
            there = chip + ((place + delta) % SIDE - place) * stride
            pairs.append((core * CHIPS + chip, core * CHIPS + there))
    return lax.ppermute(value, ("dp", "ep"), pairs)


def chip_at(stride, delta, start):
    place = start // stride % SIDE
    return start + ((place + delta) % SIDE - place) * stride


def pick_matrix(targets_ref, ids):
    hits = [
        jnp.sum((ids == targets_ref[j].astype(jnp.float32)).astype(jnp.float32), axis=0, keepdims=True)
        for j in range(SIDE)
    ]
    before = lax.broadcasted_iota(jnp.int32, (LINE, LINE), 0)
    after = lax.broadcasted_iota(jnp.int32, (LINE, LINE), 1)
    earlier = ((before // SLOTS == after // SLOTS) & (before < after)).astype(jnp.bfloat16)
    stacked = jnp.concatenate(hits + hits, axis=0).astype(jnp.bfloat16)
    ranks = jnp.dot(stacked, earlier, preferred_element_type=jnp.float32)
    base = (lax.broadcasted_iota(jnp.int32, (1, LINE), 1) // SLOTS * CAPE).astype(jnp.float32)
    rows = lax.broadcasted_iota(jnp.int32, (SIDE * PICKS, LINE), 0).astype(jnp.float32)
    picks = []
    for j in range(SIDE):
        place = jnp.where(hits[j] > 0.0, base + ranks[j : j + 1], -1.0)
        picks.append((rows == place).astype(jnp.float32))
    return jnp.concatenate(picks, axis=0).astype(jnp.bfloat16)


def select_kernel(targets_ref, own_ref, minus_ref, plus_ref, first_ref, second_ref,
                  here_ref, right_ref, left_ref, ids_ref):
    width = own_ref.shape[1]
    half = SIDE // 2
    for line in range(SIDE):
        if line < SIDE - 1:
            piece = (own_ref, minus_ref, plus_ref)[line][...]
        else:
            piece = jnp.concatenate([first_ref[...], second_ref[...]], axis=0)
        ids = piece[:, width - MARK :].astype(jnp.float32).T[:TOPK]
        ids_ref[line] = ids
        picks = pick_matrix(targets_ref, ids)
        rows = jnp.dot(picks, piece, preferred_element_type=jnp.float32).astype(jnp.bfloat16)
        rows = rows.reshape(SIDE, SIDE, PICKS, width)
        at = pl.ds(line * SIDE, SIDE)
        here_ref[at] = rows[0]
        right_ref[at] = rows[1]
        left_ref[at] = rows[2]
        far = pl.ds(PLANE + line % half * SIDE, SIDE)
        if line < half:
            right_ref[far] = rows[3]
        else:
            left_ref[far] = rows[3]


def select(targets, pieces):
    width = pieces[0].shape[1]
    vmem = pl.BlockSpec(memory_space=pltpu.VMEM)
    shapes = [PLANE, PLANE * 3 // 2, PLANE * 3 // 2]
    return pl.pallas_call(
        select_kernel,
        out_shape=[jax.ShapeDtypeStruct((n, PICKS, width), jnp.bfloat16) for n in shapes]
        + [jax.ShapeDtypeStruct((SIDE, TOPK, LINE), jnp.float32)],
        in_specs=[pl.BlockSpec(memory_space=pltpu.SMEM)] + [vmem] * 5,
        out_specs=[vmem] * 4,
        compiler_params=pltpu.CompilerParams(vmem_limit_bytes=32 * 2**20),
        cost_estimate=pl.CostEstimate(
            flops=2 * SIDE * LINE * LINE * width, bytes_accessed=4 * SIDE * LINE * width, transcendentals=0
        ),
    )(targets, *pieces)


def combine_kernel(targets_ref, ids_ref, here_ref, plus_ref, minus_ref, first_ref, second_ref, *out_refs):
    width = here_ref.shape[2]
    half = SIDE // 2
    for line in range(SIDE):
        picks = pick_matrix(targets_ref, ids_ref[line])
        at = pl.ds(line * SIDE, SIDE)
        far = (first_ref if line < half else second_ref)[pl.ds(line % half * SIDE, SIDE)]
        blocks = [here_ref[at], plus_ref[at], minus_ref[at], far]
        rows = jnp.concatenate([b.reshape(SIDE * PICKS, width) for b in blocks], axis=0)
        total = lax.dot_general(
            picks, rows, (((0,), (0,)), ((), ())), preferred_element_type=jnp.float32
        )
        out_refs[line][...] = total.astype(jnp.bfloat16)


def combine(targets, ids, blocks):
    width = blocks[0].shape[2]
    vmem = pl.BlockSpec(memory_space=pltpu.VMEM)
    return pl.pallas_call(
        combine_kernel,
        out_shape=[jax.ShapeDtypeStruct((LINE, width), jnp.bfloat16)] * SIDE,
        in_specs=[pl.BlockSpec(memory_space=pltpu.SMEM)] + [vmem] * 6,
        out_specs=[vmem] * SIDE,
        compiler_params=pltpu.CompilerParams(vmem_limit_bytes=32 * 2**20),
        cost_estimate=pl.CostEstimate(
            flops=2 * SIDE * LINE * LINE * width, bytes_accessed=4 * SIDE * LINE * width, transcendentals=0
        ),
    )(targets, ids, *blocks)


def spread_plane(block, orders, targets):
    first, second, third = zip(*orders)
    ring = [block] + [hop(block, first, delta) for delta in (1, -1, 2)]
    line = jnp.concatenate(ring, axis=0)
    minus = hop(line, second, 1)
    plus = hop(line, second, -1)
    far = [hop(minus[: LINE // 2], second, 1), hop(plus[LINE // 2 :], second, -1)]
    here, right, left, ids = select(targets, [line, minus, plus] + far)
    minus = hop(right, third, 1)
    plus = hop(left, third, -1)
    far = [hop(minus[PLANE:], third, 1), hop(plus[PLANE:], third, -1)]
    return [here, minus, plus] + far, ids


def collect_plane(here, to_minus, to_plus, orders, targets, ids):
    first, second, third = zip(*orders)
    plus = hop(to_minus, third, -1)
    minus = hop(to_plus, third, 1)
    far = [hop(plus[PLANE:], third, -1), hop(minus[PLANE:], third, 1)]
    own, near, back, away = combine(targets, ids, [here, plus, minus] + far)
    half = LINE // 2
    far = [hop(away[:half], second, -1), hop(away[half:], second, 1)]
    near = jnp.concatenate([add(near[:half], far[0]), near[half:]], axis=0)
    back = jnp.concatenate([back[:half], add(back[half:], far[1])], axis=0)
    line = add(own, hop(near, second, -1), hop(back, second, 1))
    blocks = [line[i * ROWS : (i + 1) * ROWS] for i in range(SIDE)]
    return add(blocks[0], hop(blocks[1], first, -1), hop(blocks[2], first, 1), hop(blocks[3], first, 2))


def add(*terms):
    return sum(t.astype(jnp.float32) for t in terms).astype(jnp.bfloat16)


def join_kernel(order_ref, *refs):
    main, minor, (rows_ref, mark_ref) = refs[:5], refs[5:10], refs[10:]
    half = PLANE // 2

    def fill(group, source):
        rows_ref[group, :, pl.ds(0, MAIN)] = source[:, :MAIN]
        mark_ref[group] = source[:, MAIN:]

    def one(group, carry):
        for j in range(3):
            fill(j * PLANE + group, main[j][group])
        return carry

    def far(group, carry):
        fill(3 * PLANE + group, main[3][group])
        fill(3 * PLANE + half + group, main[4][group])
        return carry

    lax.fori_loop(0, PLANE, one, 0)
    lax.fori_loop(0, half, far, 0)

    def place(group, block):
        rows_ref[order_ref[group], :, pl.ds(MAIN, MINOR)] = block[:, :MINOR]

    def one_minor(group, carry):
        for j in range(3):
            place(j * PLANE + group, minor[j][group])
        return carry

    def far_minor(group, carry):
        place(3 * PLANE + group, minor[3][group])
        place(3 * PLANE + half + group, minor[4][group])
        return carry

    lax.fori_loop(0, PLANE, one_minor, 0)
    lax.fori_loop(0, half, far_minor, 0)


def join_rows(order, main, minor):
    vmem = pl.BlockSpec(memory_space=pltpu.VMEM)
    return pl.pallas_call(
        join_kernel,
        out_shape=[
            jax.ShapeDtypeStruct((CHIPS, PICKS, D), jnp.bfloat16),
            jax.ShapeDtypeStruct((CHIPS, PICKS, MARK), jnp.bfloat16),
        ],
        in_specs=[pl.BlockSpec(memory_space=pltpu.SMEM)] + [vmem] * 10,
        out_specs=[vmem] * 2,
        compiler_params=pltpu.CompilerParams(vmem_limit_bytes=32 * 2**20),
        cost_estimate=pl.CostEstimate(
            flops=0, bytes_accessed=4 * CHIPS * PICKS * D, transcendentals=0
        ),
    )(order, *main, *minor)


def split_kernel(order_ref, rows_ref, *out_refs):
    half = PLANE // 2

    def cut(outs, start, width, number):
        def one(group, carry):
            for j in range(3):
                source = number(j * PLANE + group)
                outs[j][group] = rows_ref[source, :, pl.ds(start, width)]
            return carry

        def far(group, carry):
            for k in range(2):
                source = number(3 * PLANE + k * half + group)
                outs[1 + k][PLANE + group] = rows_ref[source, :, pl.ds(start, width)]
            return carry

        lax.fori_loop(0, PLANE, one, 0)
        lax.fori_loop(0, half, far, 0)

    cut(out_refs[:3], 0, MAIN, lambda group: group)
    cut(out_refs[3:], MAIN, MINOR, lambda group: order_ref[group])


def split_rows(order, rows):
    vmem = pl.BlockSpec(memory_space=pltpu.VMEM)
    shapes = [(n, PICKS, w) for w in (MAIN, MINOR) for n in (PLANE, PLANE * 3 // 2, PLANE * 3 // 2)]
    outs = pl.pallas_call(
        split_kernel,
        out_shape=[jax.ShapeDtypeStruct(shape, jnp.bfloat16) for shape in shapes],
        in_specs=[pl.BlockSpec(memory_space=pltpu.SMEM), vmem],
        out_specs=[vmem] * 6,
        compiler_params=pltpu.CompilerParams(vmem_limit_bytes=32 * 2**20),
        cost_estimate=pl.CostEstimate(
            flops=0, bytes_accessed=4 * CHIPS * PICKS * D, transcendentals=0
        ),
    )(order, rows)
    return outs[:3], outs[3:]


def three_parts(weights):
    high = lax.reduce_precision(weights, 8, 7)
    rest = weights - high
    mid = lax.reduce_precision(rest, 8, 7)
    return [part.astype(jnp.bfloat16) for part in (high, mid, rest - mid)]


def pack_kernel(from_ref, slot_ref, len_ref, cache_ref, out_ref):
    row = lax.broadcasted_iota(jnp.int32, (HALF, 128), 0)
    lane = lax.broadcasted_iota(jnp.int32, (HALF, 128), 1)

    def one(chip, carry):
        block = cache_ref[from_ref[chip]]
        out_ref[chip] = block
        mark = jnp.where(lane == 0, slot_ref[chip], len_ref[chip]).astype(jnp.float32)
        head = jnp.where((row == HALF - 1) & (lane < 2), mark, block[:, :128].astype(jnp.float32))
        out_ref[chip, :, pl.ds(0, 128)] = head.astype(jnp.bfloat16)
        return carry

    lax.fori_loop(0, out_ref.shape[0], one, 0)


def pack_cache(send_from, sent_slot, sent_len, cache):
    chips = send_from.shape[0]
    small = pl.BlockSpec(memory_space=pltpu.SMEM)
    return pl.pallas_call(
        pack_kernel,
        out_shape=jax.ShapeDtypeStruct((chips,) + cache.shape[1:], jnp.bfloat16),
        in_specs=[small, small, small, pl.BlockSpec(memory_space=pltpu.VMEM)],
        out_specs=pl.BlockSpec(memory_space=pltpu.VMEM),
        compiler_params=pltpu.CompilerParams(vmem_limit_bytes=24 * 2**20),
        cost_estimate=pl.CostEstimate(
            flops=0, bytes_accessed=2 * (chips + cache.shape[0]) * CTX * KVW, transcendentals=0
        ),
    )(send_from, sent_slot, sent_len, cache)


def on_device(
    kv_cache,
    lengths,
    move_list,
    queries,
    new_kv,
    hidden,
    expert_ids,
    gate_weights,
    expert_gate,
    expert_up,
    expert_down,
):
    ep_count = lax.axis_size("ep")
    slot_count = lengths.shape[0]
    own = (expert_gate[0], expert_up[0], expert_down[0])
    other = tuple(lax.ppermute(w, "dp", [(0, 1), (1, 0)]) for w in own)
    expert_range = jnp.arange(ep_count, dtype=jnp.int32)
    me = lax.axis_index("ep")
    core = lax.axis_index("dp")

    marks = [expert_ids.astype(jnp.bfloat16)] + three_parts(gate_weights)
    marks = jnp.concatenate(marks, axis=2).reshape(ROWS, 4 * TOPK)
    marks = jnp.pad(marks, ((0, 0), (0, MARK - 4 * TOPK)))
    rows = hidden.reshape(ROWS, D)
    columns = (rows[:, :MAIN], rows[:, MAIN:])
    arrived = []
    returns = []
    for block, orders in zip(columns, ORDERS):
        stride = jnp.where(core == 0, orders[0][2], orders[1][2])
        targets = jnp.stack([chip_at(stride, delta, me) for delta in TARGETS]).astype(jnp.int32)
        blocks, ids = spread_plane(jnp.concatenate([block, marks], axis=1), orders, targets)
        arrived.append(blocks)
        returns.append((orders, targets, ids))

    slot_range = jnp.arange(slot_count, dtype=jnp.int32)
    send_hit = expert_range[:, None] == move_list[:, 0][None, :]
    send_from = jnp.sum(jnp.where(send_hit, slot_range[None, :], 0), axis=1)
    sent_slot = jnp.sum(jnp.where(send_hit, move_list[:, 1][None, :] + 1, 0), axis=1) - 1
    sent_len = jnp.sum(jnp.where(send_hit, lengths[None, :], 0), axis=1)
    packed_cache = pack_cache(
        send_from, sent_slot, sent_len, kv_cache.reshape(slot_count, HALF, 2 * KVW)
    )
    packed_cache, arrived = lax.optimization_barrier((packed_cache, arrived))
    got = lax.all_to_all(packed_cache, "ep", split_axis=0, concat_axis=0, tiled=True)

    tables = []
    for main, minor in zip(*ORDERS):
        table = [0] * CHIPS
        for number in range(CHIPS):
            digits = (number // PLANE, number // SIDE % SIDE, number % SIDE)
            place = dict(zip(main, digits[::-1]))
            index = place[minor[2]] * PLANE + place[minor[1]] * SIDE + place[minor[0]]
            table[index] = number
        tables.append(jnp.array(table, jnp.int32))
    order = jnp.where(core == 0, tables[0], tables[1])
    rows, mark = join_rows(order, arrived[0], arrived[1])
    mark = mark.reshape(CHIPS * PICKS, MARK).astype(jnp.float32)
    weight = mark[:, TOPK : 2 * TOPK] + mark[:, 2 * TOPK : 3 * TOPK] + mark[:, 3 * TOPK : 4 * TOPK]
    weight = jnp.where(mark[:, :TOPK] == me.astype(jnp.float32), weight, 0.0)
    weight = jnp.sum(weight, axis=1, keepdims=True)
    produced = expert_rows(rows.reshape(CHIPS * PICKS, D), weight, (own, other))
    outward = split_rows(order, produced.reshape(CHIPS, PICKS, D))
    outward, got = lax.optimization_barrier((outward, got))
    sums = []
    for (here, to_minus, to_plus), (orders, targets, ids) in zip(outward, returns):
        sums.append(collect_plane(here, to_minus, to_plus, orders, targets, ids))
    mixture = jnp.concatenate(sums, axis=1).reshape(STEPS, SLOTS, D)

    got_slot = got[:, HALF - 1, 0].astype(jnp.int32)
    got_len = got[:, HALF - 1, 1].astype(jnp.int32)
    land_hit = got_slot[None, :] == slot_range[:, None]
    landing = jnp.sum(jnp.where(land_hit, expert_range[None, :], 0), axis=1)
    placed_len = jnp.sum(jnp.where(land_hit, got_len[None, :], 0), axis=1)
    context = attend(queries, new_kv, got, landing, placed_len)

    return context, mixture


def solution(mesh):
    return jax.shard_map(
        on_device,
        mesh=mesh,
        in_specs=(
            P(("dp", "ep"), None),
            P(("dp", "ep")),
            P(("dp", "ep"), None),
            P(None, ("dp", "ep"), None),
            P(None, ("dp", "ep"), None),
            P(None, ("dp", "ep"), None),
            P(None, ("dp", "ep"), None),
            P(None, ("dp", "ep"), None),
            P("ep", None, "dp"),
            P("ep", None, "dp"),
            P("ep", "dp", None),
        ),
        out_specs=(P(None, ("dp", "ep"), None), P(None, ("dp", "ep"), None)),
        check_vma=False,
    )
```

```python
import jax
import jax.numpy as jnp
from jax import lax
from jax.experimental import pallas as pl
from jax.experimental.pallas import tpu as pltpu
from jax.sharding import PartitionSpec as P

D = 3584
H = 64
LAT = 512
TOPK = 8
STEPS = 2
CTX = 64
KVW = 576
HALF = CTX // 2
GROUP = 16
TOGETHER = 8
WIDE = 640
SIDE = 4
Z, Y, X = SIDE * SIDE, SIDE, 1
MAIN = 2432
MINOR = D - MAIN
MARK = 128
SLOTS = 32
CAPE = 8
ROWS = STEPS * SLOTS
PICKS = STEPS * CAPE
LINE = SIDE * ROWS
PLANE = SIDE * SIDE
CHIPS = SIDE**3
ORDERS = (((Z, Y, X), (Y, X, Z)), ((X, Z, Y), (X, Z, Y)))
TARGETS = (0, 1, -1, 2)
KEYS = GROUP * (CTX + STEPS)


score_scale = 192.0 ** (-0.5)


def attend_kernel(landing_ref, got_ref, len_ref, new_ref, query_ref, out_ref, even_ref, odd_ref, value_ref, bias_ref):
    pairs = GROUP * HALF

    def lanes(rows):
        return lax.broadcasted_iota(jnp.int32, (rows, WIDE), 1)

    def place(keys, rows, at):
        even_ref[pl.ds(at, rows), :] = keys.astype(jnp.bfloat16)
        odd_ref[pl.ds(at, rows), :] = pltpu.roll(keys, WIDE - KVW, 1).astype(jnp.bfloat16)
        value_ref[pl.ds(at, rows), :] = keys[:, :LAT].astype(jnp.bfloat16)

    def one(slot, carry):
        source = landing_ref[slot]
        block = got_ref[source]
        first = jnp.where(lanes(HALF) < KVW, block[:, :WIDE].astype(jnp.float32), 0.0)
        at = pl.multiple_of(slot * HALF, HALF)
        place(first, HALF, at)
        second = block[:, LAT:].astype(jnp.float32)
        second = jnp.where(lanes(HALF) < WIDE - KVW, 0.0, second)
        place(pltpu.roll(second, KVW, 1), HALF, pl.multiple_of(pairs + at, HALF))
        return carry

    lax.fori_loop(0, GROUP, one, 0)
    for step in range(STEPS):
        rows = new_ref[step].astype(jnp.float32)
        rows = jnp.concatenate([rows, jnp.zeros((GROUP, WIDE - KVW), jnp.float32)], axis=1)
        place(rows, GROUP, 2 * pairs + step * GROUP)

    column = lax.broadcasted_iota(jnp.int32, (GROUP, KEYS), 1)
    row = lax.broadcasted_iota(jnp.int32, (GROUP, KEYS), 0)
    cached = column < 2 * pairs
    half = (column >= pairs).astype(jnp.int32)
    within = column - half * pairs
    position = 2 * (within % HALF) + half
    recent = column - 2 * pairs
    owner = jnp.where(cached, within // HALF, recent % GROUP)
    live = cached & (position < len_ref[...])
    for step in range(STEPS):
        allowed = (live | (~cached & (recent < (step + 1) * GROUP))) & (owner == row)
        bias_ref[pl.ds(step * GROUP, GROUP), :] = jnp.where(allowed, 0.0, -jnp.inf)

    def heads(index, carry):
        bias = jnp.concatenate([bias_ref[...]] * TOGETHER, axis=0)
        for odd in range(2):
            slabs = []
            for k in range(TOGETHER):
                start = pl.multiple_of((index * TOGETHER + k) * 2 * KVW + odd * LAT, 128)
                for step in range(STEPS):
                    slabs.append(query_ref[step, :, pl.ds(start, WIDE)])
            keys = odd_ref[...] if odd else even_ref[...]
            score = lax.dot_general(
                jnp.concatenate(slabs, axis=0),
                keys,
                (((1,), (1,)), ((), ())),
                preferred_element_type=jnp.float32,
            )
            score = score * score_scale + bias
            weight = jnp.exp(score - jnp.max(score, axis=1, keepdims=True))
            prob = weight * (1.0 / jnp.sum(weight, axis=1, keepdims=True))
            mixed = jnp.dot(
                prob.astype(jnp.bfloat16), value_ref[...], preferred_element_type=jnp.float32
            ).astype(jnp.bfloat16)
            for k in range(TOGETHER):
                start = pl.multiple_of(((index * TOGETHER + k) * 2 + odd) * LAT, LAT)
                for step in range(STEPS):
                    at = (k * STEPS + step) * GROUP
                    out_ref[step, :, pl.ds(start, LAT)] = mixed[at : at + GROUP]
        return carry

    lax.fori_loop(0, H // (2 * TOGETHER), heads, 0)


def attend(queries, new_kv, got, landing, placed_len, earlier):
    slots = queries.shape[1]
    group = 0 if earlier is None else 1
    specs = [
        pl.BlockSpec(memory_space=pltpu.SMEM),
        pl.BlockSpec(memory_space=pltpu.VMEM),
        pl.BlockSpec((GROUP, 1), lambda g: (group, 0)),
        pl.BlockSpec((STEPS, GROUP, KVW), lambda g: (0, group, 0)),
        pl.BlockSpec((STEPS, GROUP, H * KVW), lambda g: (0, group, 0)),
    ]
    operands = [landing[group * GROUP :][:GROUP], got, placed_len[:, None], new_kv, queries]
    kernel = attend_kernel
    if earlier is not None:
        specs.append(pl.BlockSpec(memory_space=pl.ANY))
        operands.append(earlier)

        def kernel(*refs):
            attend_kernel(*refs[:5], *refs[6:])

    return pl.pallas_call(
        kernel,
        grid=(1,),
        out_shape=jax.ShapeDtypeStruct((STEPS, slots, H * LAT), jnp.bfloat16),
        in_specs=specs,
        out_specs=pl.BlockSpec((STEPS, GROUP, H * LAT), lambda g: (0, group, 0)),
        scratch_shapes=[
            pltpu.VMEM((KEYS, WIDE), jnp.bfloat16),
            pltpu.VMEM((KEYS, WIDE), jnp.bfloat16),
            pltpu.VMEM((KEYS, LAT), jnp.bfloat16),
            pltpu.VMEM((STEPS * GROUP, KEYS), jnp.float32),
        ],
        input_output_aliases={} if earlier is None else {5: 0},
        compiler_params=pltpu.CompilerParams(vmem_limit_bytes=32 * 2**20),
        cost_estimate=pl.CostEstimate(
            flops=2 * STEPS * GROUP * H * KEYS * (WIDE + LAT),
            bytes_accessed=2 * STEPS * GROUP * H * (KVW + LAT),
            transcendentals=STEPS * GROUP * H * KEYS,
        ),
    )(*operands)


def expert_rows(token_rows, row_weight, halves):
    total = None
    for gate_mat, up_mat, down_mat in halves:
        gate_pre = jnp.dot(token_rows, gate_mat, preferred_element_type=jnp.float32)
        up_pre = jnp.dot(token_rows, up_mat, preferred_element_type=jnp.float32)
        inner = (jax.nn.silu(gate_pre) * up_pre).astype(jnp.bfloat16)
        part = jnp.dot(inner, down_mat, preferred_element_type=jnp.float32)
        total = part if total is None else total + part
    return (total * row_weight).astype(jnp.bfloat16)


def hop(value, strides, delta):
    pairs = []
    for core, stride in enumerate(strides):
        for chip in range(CHIPS):
            place = chip // stride % SIDE
            there = chip + ((place + delta) % SIDE - place) * stride
            pairs.append((core * CHIPS + chip, core * CHIPS + there))
    return lax.ppermute(value, ("dp", "ep"), pairs)


def chip_at(stride, delta, start):
    place = start // stride % SIDE
    return start + ((place + delta) % SIDE - place) * stride


def pick_matrix(targets_ref, ids):
    hits = [
        jnp.sum((ids == targets_ref[j].astype(jnp.float32)).astype(jnp.float32), axis=0, keepdims=True)
        for j in range(SIDE)
    ]
    before = lax.broadcasted_iota(jnp.int32, (LINE, LINE), 0)
    after = lax.broadcasted_iota(jnp.int32, (LINE, LINE), 1)
    earlier = ((before // SLOTS == after // SLOTS) & (before < after)).astype(jnp.bfloat16)
    stacked = jnp.concatenate(hits + hits, axis=0).astype(jnp.bfloat16)
    ranks = jnp.dot(stacked, earlier, preferred_element_type=jnp.float32)
    base = (lax.broadcasted_iota(jnp.int32, (1, LINE), 1) // SLOTS * CAPE).astype(jnp.float32)
    rows = lax.broadcasted_iota(jnp.int32, (SIDE * PICKS, LINE), 0).astype(jnp.float32)
    picks = []
    for j in range(SIDE):
        place = jnp.where(hits[j] > 0.0, base + ranks[j : j + 1], -1.0)
        picks.append((rows == place).astype(jnp.float32))
    return jnp.concatenate(picks, axis=0).astype(jnp.bfloat16)


def select_kernel(targets_ref, *refs):
    pieces, outs, ids_ref = refs[:SIDE], refs[SIDE : 2 * SIDE], refs[2 * SIDE]
    width = pieces[0].shape[1]
    for line in range(SIDE):
        piece = pieces[line][...]
        ids = piece[:, width - MARK :].astype(jnp.float32).T[:TOPK]
        ids_ref[line] = ids
        picks = pick_matrix(targets_ref, ids)
        rows = jnp.dot(picks, piece, preferred_element_type=jnp.float32).astype(jnp.bfloat16)
        rows = rows.reshape(SIDE, SIDE, PICKS, width)
        for j in range(SIDE):
            outs[j][pl.ds(line * SIDE, SIDE)] = rows[j]


def select(targets, pieces):
    width = pieces[0].shape[1]
    vmem = pl.BlockSpec(memory_space=pltpu.VMEM)
    return pl.pallas_call(
        select_kernel,
        out_shape=[jax.ShapeDtypeStruct((PLANE, PICKS, width), jnp.bfloat16)] * SIDE
        + [jax.ShapeDtypeStruct((SIDE, TOPK, LINE), jnp.float32)],
        in_specs=[pl.BlockSpec(memory_space=pltpu.SMEM)] + [vmem] * SIDE,
        out_specs=[vmem] * (SIDE + 1),
        compiler_params=pltpu.CompilerParams(vmem_limit_bytes=32 * 2**20),
        cost_estimate=pl.CostEstimate(
            flops=2 * SIDE * LINE * LINE * width, bytes_accessed=4 * SIDE * LINE * width, transcendentals=0
        ),
    )(targets, *pieces)


def combine_kernel(targets_ref, ids_ref, *refs):
    width = refs[0].shape[2]
    for line in range(SIDE):
        picks = pick_matrix(targets_ref, ids_ref[line])
        blocks = [ref[pl.ds(line * SIDE, SIDE)] for ref in refs[:SIDE]]
        rows = jnp.concatenate([b.reshape(SIDE * PICKS, width) for b in blocks], axis=0)
        total = lax.dot_general(
            picks, rows, (((0,), (0,)), ((), ())), preferred_element_type=jnp.float32
        )
        refs[SIDE + line][...] = total.astype(jnp.bfloat16)


def combine(targets, ids, blocks):
    width = blocks[0].shape[2]
    vmem = pl.BlockSpec(memory_space=pltpu.VMEM)
    return pl.pallas_call(
        combine_kernel,
        out_shape=[jax.ShapeDtypeStruct((LINE, width), jnp.bfloat16)] * SIDE,
        in_specs=[pl.BlockSpec(memory_space=pltpu.SMEM)] + [vmem] * (1 + SIDE),
        out_specs=[vmem] * SIDE,
        compiler_params=pltpu.CompilerParams(vmem_limit_bytes=32 * 2**20),
        cost_estimate=pl.CostEstimate(
            flops=2 * SIDE * LINE * LINE * width, bytes_accessed=4 * SIDE * LINE * width, transcendentals=0
        ),
    )(targets, ids, *blocks)


def together(*trees):
    return lax.optimization_barrier(trees)


def stage_axes():
    return [[tuple(by_core[n] for by_core in orders) for orders in ORDERS] for n in range(3)]


def exchange(blocks, strides, deltas):
    return [hop(block, strides, delta) for block, delta in zip(blocks, deltas)]


def send_rows(columns, targets):
    first, second, third = stage_axes()
    both = range(len(columns))
    rings = [exchange([columns[i]] * 3, first[i], (1, -1, 2)) for i in both]
    columns, rings = together(columns, rings)
    lines = [jnp.concatenate([columns[i]] + rings[i], axis=0) for i in both]
    rings = [exchange([lines[i]] * 3, second[i], (1, -1, 2)) for i in both]
    lines, rings = together(lines, rings)
    picked = [select(targets[i], [lines[i]] + rings[i]) for i in both]
    rings = [exchange(picked[i][1:SIDE], third[i], TARGETS[1:]) for i in both]
    return [[picked[i][0]] + rings[i] for i in both], [p[SIDE] for p in picked]


def return_rows(outward, targets, ids, contexts):
    first, second, third = stage_axes()
    both = range(len(outward))
    rings = [exchange(outward[i][1:], third[i], (-1, 1, 2)) for i in both]
    context = contexts(None)
    rings, context = together(rings, context)
    lines = [combine(targets[i], ids[i], [outward[i][0]] + rings[i]) for i in both]
    rings = [exchange(lines[i][1:], second[i], (-1, 1, 2)) for i in both]
    context = contexts(context)
    rings, context = together(rings, context)
    sums = []
    for i in both:
        line = add(lines[i][0], *rings[i])
        blocks = [line[k * ROWS : (k + 1) * ROWS] for k in range(SIDE)]
        sums.append([blocks[0]] + exchange(blocks[1:], first[i], (-1, 1, 2)))
    sums, = together(sums)
    return [add(*terms) for terms in sums], context


def add(*terms):
    return sum(t.astype(jnp.float32) for t in terms).astype(jnp.bfloat16)


def join_kernel(order_ref, *refs):
    main, minor, (rows_ref, mark_ref) = refs[:SIDE], refs[SIDE : 2 * SIDE], refs[2 * SIDE :]

    def one(group, carry):
        for j in range(SIDE):
            number = j * PLANE + group
            rows_ref[number, :, pl.ds(0, MAIN)] = main[j][group, :, pl.ds(0, MAIN)]
            mark_ref[number] = main[j][group, :, pl.ds(MAIN, MARK)]
            rows_ref[order_ref[number], :, pl.ds(MAIN, MINOR)] = minor[j][group, :, pl.ds(0, MINOR)]
        return carry

    lax.fori_loop(0, PLANE, one, 0)


def join_rows(order, main, minor):
    vmem = pl.BlockSpec(memory_space=pltpu.VMEM)
    return pl.pallas_call(
        join_kernel,
        out_shape=[
            jax.ShapeDtypeStruct((CHIPS, PICKS, D), jnp.bfloat16),
            jax.ShapeDtypeStruct((CHIPS, PICKS, MARK), jnp.bfloat16),
        ],
        in_specs=[pl.BlockSpec(memory_space=pltpu.SMEM)] + [vmem] * (2 * SIDE),
        out_specs=[vmem] * 2,
        compiler_params=pltpu.CompilerParams(vmem_limit_bytes=32 * 2**20),
        cost_estimate=pl.CostEstimate(
            flops=0, bytes_accessed=4 * CHIPS * PICKS * D, transcendentals=0
        ),
    )(order, *main, *minor)


def split_kernel(order_ref, rows_ref, *refs):
    main, minor = refs[:SIDE], refs[SIDE:]

    def one(group, carry):
        for j in range(SIDE):
            number = j * PLANE + group
            main[j][group] = rows_ref[number, :, pl.ds(0, MAIN)]
            minor[j][group] = rows_ref[order_ref[number], :, pl.ds(MAIN, MINOR)]
        return carry

    lax.fori_loop(0, PLANE, one, 0)


def split_rows(order, rows):
    vmem = pl.BlockSpec(memory_space=pltpu.VMEM)
    shapes = [(PLANE, PICKS, width) for width in (MAIN, MINOR) for _ in range(SIDE)]
    outs = pl.pallas_call(
        split_kernel,
        out_shape=[jax.ShapeDtypeStruct(shape, jnp.bfloat16) for shape in shapes],
        in_specs=[pl.BlockSpec(memory_space=pltpu.SMEM), vmem],
        out_specs=[vmem] * (2 * SIDE),
        compiler_params=pltpu.CompilerParams(vmem_limit_bytes=32 * 2**20),
        cost_estimate=pl.CostEstimate(
            flops=0, bytes_accessed=4 * CHIPS * PICKS * D, transcendentals=0
        ),
    )(order, rows)
    return outs[:SIDE], outs[SIDE:]


def three_parts(weights):
    high = lax.reduce_precision(weights, 8, 7)
    rest = weights - high
    mid = lax.reduce_precision(rest, 8, 7)
    return [part.astype(jnp.bfloat16) for part in (high, mid, rest - mid)]


def pack_kernel(from_ref, slot_ref, len_ref, cache_ref, out_ref):
    row = lax.broadcasted_iota(jnp.int32, (HALF, 128), 0)
    lane = lax.broadcasted_iota(jnp.int32, (HALF, 128), 1)

    def one(chip, carry):
        block = cache_ref[from_ref[chip]]
        out_ref[chip] = block
        mark = jnp.where(lane == 0, slot_ref[chip], len_ref[chip]).astype(jnp.float32)
        head = jnp.where((row == HALF - 1) & (lane < 2), mark, block[:, :128].astype(jnp.float32))
        out_ref[chip, :, pl.ds(0, 128)] = head.astype(jnp.bfloat16)
        return carry

    lax.fori_loop(0, out_ref.shape[0], one, 0)


def pack_cache(send_from, sent_slot, sent_len, cache):
    chips = send_from.shape[0]
    small = pl.BlockSpec(memory_space=pltpu.SMEM)
    return pl.pallas_call(
        pack_kernel,
        out_shape=jax.ShapeDtypeStruct((chips,) + cache.shape[1:], jnp.bfloat16),
        in_specs=[small, small, small, pl.BlockSpec(memory_space=pltpu.VMEM)],
        out_specs=pl.BlockSpec(memory_space=pltpu.VMEM),
        compiler_params=pltpu.CompilerParams(vmem_limit_bytes=24 * 2**20),
        cost_estimate=pl.CostEstimate(
            flops=0, bytes_accessed=2 * (chips + cache.shape[0]) * CTX * KVW, transcendentals=0
        ),
    )(send_from, sent_slot, sent_len, cache)


def on_device(
    kv_cache,
    lengths,
    move_list,
    queries,
    new_kv,
    hidden,
    expert_ids,
    gate_weights,
    expert_gate,
    expert_up,
    expert_down,
):
    ep_count = lax.axis_size("ep")
    slot_count = lengths.shape[0]
    own = (expert_gate[0], expert_up[0], expert_down[0])
    expert_range = jnp.arange(ep_count, dtype=jnp.int32)
    me = lax.axis_index("ep")
    core = lax.axis_index("dp")

    marks = [expert_ids.astype(jnp.bfloat16)] + three_parts(gate_weights)
    marks = jnp.concatenate(marks, axis=2).reshape(ROWS, 4 * TOPK)
    marks = jnp.pad(marks, ((0, 0), (0, MARK - 4 * TOPK)))
    rows = hidden.reshape(ROWS, D)
    columns = [
        jnp.concatenate([block, marks], axis=1) for block in (rows[:, :MAIN], rows[:, MAIN:])
    ]
    targets = []
    for orders in ORDERS:
        stride = jnp.where(core == 0, orders[0][2], orders[1][2])
        targets.append(
            jnp.stack([chip_at(stride, delta, me) for delta in TARGETS]).astype(jnp.int32)
        )
    arrived, ids = send_rows(columns, targets)

    slot_range = jnp.arange(slot_count, dtype=jnp.int32)
    send_hit = expert_range[:, None] == move_list[:, 0][None, :]
    send_from = jnp.sum(jnp.where(send_hit, slot_range[None, :], 0), axis=1)
    sent_slot = jnp.sum(jnp.where(send_hit, move_list[:, 1][None, :] + 1, 0), axis=1) - 1
    sent_len = jnp.sum(jnp.where(send_hit, lengths[None, :], 0), axis=1)
    packed_cache = pack_cache(
        send_from, sent_slot, sent_len, kv_cache.reshape(slot_count, HALF, 2 * KVW)
    )
    packed_cache, arrived, own = together(packed_cache, arrived, own)
    other = tuple(lax.ppermute(w, "dp", [(0, 1), (1, 0)]) for w in own)
    got = lax.all_to_all(packed_cache, "ep", split_axis=0, concat_axis=0, tiled=True)

    tables = []
    for main, minor in zip(*ORDERS):
        table = [0] * CHIPS
        for number in range(CHIPS):
            digits = (number // PLANE, number // SIDE % SIDE, number % SIDE)
            place = dict(zip(main, digits[::-1]))
            index = place[minor[2]] * PLANE + place[minor[1]] * SIDE + place[minor[0]]
            table[index] = number
        tables.append(jnp.array(table, jnp.int32))
    order = jnp.where(core == 0, tables[0], tables[1])
    rows, mark = join_rows(order, arrived[0], arrived[1])
    mark = mark.reshape(CHIPS * PICKS, MARK).astype(jnp.float32)
    weight = mark[:, TOPK : 2 * TOPK] + mark[:, 2 * TOPK : 3 * TOPK] + mark[:, 3 * TOPK : 4 * TOPK]
    weight = jnp.where(mark[:, :TOPK] == me.astype(jnp.float32), weight, 0.0)
    weight = jnp.sum(weight, axis=1, keepdims=True)
    produced = expert_rows(rows.reshape(CHIPS * PICKS, D), weight, (own, other))
    outward = split_rows(order, produced.reshape(CHIPS, PICKS, D))
    outward, got = lax.optimization_barrier((outward, got))
    got_slot = got[:, HALF - 1, 0].astype(jnp.int32)
    got_len = got[:, HALF - 1, 1].astype(jnp.int32)
    land_hit = got_slot[None, :] == slot_range[:, None]
    landing = jnp.sum(jnp.where(land_hit, expert_range[None, :], 0), axis=1)
    placed_len = jnp.sum(jnp.where(land_hit, got_len[None, :], 0), axis=1)

    def contexts(earlier):
        return attend(queries, new_kv, got, landing, placed_len, earlier)

    sums, context = return_rows(outward, targets, ids, contexts)
    mixture = jnp.concatenate(sums, axis=1).reshape(STEPS, SLOTS, D)
    return context, mixture


def solution(mesh):
    return jax.shard_map(
        on_device,
        mesh=mesh,
        in_specs=(
            P(("dp", "ep"), None),
            P(("dp", "ep")),
            P(("dp", "ep"), None),
            P(None, ("dp", "ep"), None),
            P(None, ("dp", "ep"), None),
            P(None, ("dp", "ep"), None),
            P(None, ("dp", "ep"), None),
            P(None, ("dp", "ep"), None),
            P("ep", None, "dp"),
            P("ep", None, "dp"),
            P("ep", "dp", None),
        ),
        out_specs=(P(None, ("dp", "ep"), None), P(None, ("dp", "ep"), None)),
        check_vma=False,
    )
```

```python
import jax
import jax.numpy as jnp
from jax import lax
from jax.experimental import pallas as pl
from jax.experimental.pallas import tpu as pltpu
from jax.sharding import PartitionSpec as P

D = 3584
H = 64
LAT = 512
TOPK = 8
STEPS = 2
CTX = 64
KVW = 576
HALF = CTX // 2
GROUP = 16
TOGETHER = 8
WIDE = 640
SIDE = 4
Z, Y, X = SIDE * SIDE, SIDE, 1
MAIN = 2432
MINOR = D - MAIN
MARK = 128
SLOTS = 32
CAPE = 8
ROWS = STEPS * SLOTS
PICKS = STEPS * CAPE
LINE = SIDE * ROWS
PLANE = SIDE * SIDE
CHIPS = SIDE**3
BLOCK = 32
ORDERS = (((Z, Y, X), (Y, X, Z)), ((X, Z, Y), (X, Z, Y)))
TARGETS = (0, 1, -1, 2)
KEYS = GROUP * (CTX + STEPS)


score_scale = 192.0 ** (-0.5)


def attend_kernel(landing_ref, got_ref, len_ref, new_ref, query_ref, out_ref, even_ref, odd_ref, value_ref, bias_ref):
    group = pl.program_id(0)
    pairs = GROUP * HALF

    def lanes(rows):
        return lax.broadcasted_iota(jnp.int32, (rows, WIDE), 1)

    def place(keys, rows, at):
        even_ref[pl.ds(at, rows), :] = keys.astype(jnp.bfloat16)
        odd_ref[pl.ds(at, rows), :] = pltpu.roll(keys, WIDE - KVW, 1).astype(jnp.bfloat16)
        value_ref[pl.ds(at, rows), :] = keys[:, :LAT].astype(jnp.bfloat16)

    def one(slot, carry):
        source = landing_ref[group * GROUP + slot]
        block = got_ref[source]
        first = jnp.where(lanes(HALF) < KVW, block[:, :WIDE].astype(jnp.float32), 0.0)
        at = pl.multiple_of(slot * HALF, HALF)
        place(first, HALF, at)
        second = block[:, LAT:].astype(jnp.float32)
        second = jnp.where(lanes(HALF) < WIDE - KVW, 0.0, second)
        place(pltpu.roll(second, KVW, 1), HALF, pl.multiple_of(pairs + at, HALF))
        return carry

    lax.fori_loop(0, GROUP, one, 0)
    for step in range(STEPS):
        rows = new_ref[step].astype(jnp.float32)
        rows = jnp.concatenate([rows, jnp.zeros((GROUP, WIDE - KVW), jnp.float32)], axis=1)
        place(rows, GROUP, 2 * pairs + step * GROUP)

    column = lax.broadcasted_iota(jnp.int32, (GROUP, KEYS), 1)
    row = lax.broadcasted_iota(jnp.int32, (GROUP, KEYS), 0)
    cached = column < 2 * pairs
    half = (column >= pairs).astype(jnp.int32)
    within = column - half * pairs
    position = 2 * (within % HALF) + half
    recent = column - 2 * pairs
    owner = jnp.where(cached, within // HALF, recent % GROUP)
    live = cached & (position < len_ref[...])
    for step in range(STEPS):
        allowed = (live | (~cached & (recent < (step + 1) * GROUP))) & (owner == row)
        bias_ref[pl.ds(step * GROUP, GROUP), :] = jnp.where(allowed, 0.0, -jnp.inf)

    def heads(index, carry):
        bias = jnp.concatenate([bias_ref[...]] * TOGETHER, axis=0)
        for odd in range(2):
            slabs = []
            for k in range(TOGETHER):
                start = pl.multiple_of((index * TOGETHER + k) * 2 * KVW + odd * LAT, 128)
                for step in range(STEPS):
                    slabs.append(query_ref[step, :, pl.ds(start, WIDE)])
            keys = odd_ref[...] if odd else even_ref[...]
            score = lax.dot_general(
                jnp.concatenate(slabs, axis=0),
                keys,
                (((1,), (1,)), ((), ())),
                preferred_element_type=jnp.float32,
            )
            score = score * score_scale + bias
            weight = jnp.exp(score - jnp.max(score, axis=1, keepdims=True))
            prob = weight * (1.0 / jnp.sum(weight, axis=1, keepdims=True))
            mixed = jnp.dot(
                prob.astype(jnp.bfloat16), value_ref[...], preferred_element_type=jnp.float32
            ).astype(jnp.bfloat16)
            for k in range(TOGETHER):
                start = pl.multiple_of(((index * TOGETHER + k) * 2 + odd) * LAT, LAT)
                for step in range(STEPS):
                    at = (k * STEPS + step) * GROUP
                    out_ref[step, :, pl.ds(start, LAT)] = mixed[at : at + GROUP]
        return carry

    lax.fori_loop(0, H // (2 * TOGETHER), heads, 0)


def attend(queries, new_kv, got, landing, placed_len):
    slots = queries.shape[1]
    return pl.pallas_call(
        attend_kernel,
        grid=(slots // GROUP,),
        out_shape=jax.ShapeDtypeStruct((STEPS, slots, H * LAT), jnp.bfloat16),
        in_specs=[
            pl.BlockSpec(memory_space=pltpu.SMEM),
            pl.BlockSpec(memory_space=pltpu.VMEM),
            pl.BlockSpec((GROUP, 1), lambda g: (g, 0)),
            pl.BlockSpec((STEPS, GROUP, KVW), lambda g: (0, g, 0)),
            pl.BlockSpec((STEPS, GROUP, H * KVW), lambda g: (0, g, 0)),
        ],
        out_specs=pl.BlockSpec((STEPS, GROUP, H * LAT), lambda g: (0, g, 0)),
        scratch_shapes=[
            pltpu.VMEM((KEYS, WIDE), jnp.bfloat16),
            pltpu.VMEM((KEYS, WIDE), jnp.bfloat16),
            pltpu.VMEM((KEYS, LAT), jnp.bfloat16),
            pltpu.VMEM((STEPS * GROUP, KEYS), jnp.float32),
        ],
        compiler_params=pltpu.CompilerParams(vmem_limit_bytes=48 * 2**20),
        cost_estimate=pl.CostEstimate(
            flops=2 * STEPS * slots * H * KEYS * (WIDE + LAT),
            bytes_accessed=2 * STEPS * slots * H * (KVW + LAT),
            transcendentals=STEPS * slots * H * KEYS,
        ),
    )(landing, got, placed_len[:, None], new_kv, queries)


def hop(value, strides, delta):
    pairs = []
    for core, stride in enumerate(strides):
        for chip in range(CHIPS):
            place = chip // stride % SIDE
            there = chip + ((place + delta) % SIDE - place) * stride
            pairs.append((core * CHIPS + chip, core * CHIPS + there))
    return lax.ppermute(value, ("dp", "ep"), pairs)


def chip_at(stride, delta, start):
    place = start // stride % SIDE
    return start + ((place + delta) % SIDE - place) * stride


def pick_matrix(targets_ref, ids):
    hits = [
        jnp.sum((ids == targets_ref[j].astype(jnp.float32)).astype(jnp.float32), axis=0, keepdims=True)
        for j in range(SIDE)
    ]
    before = lax.broadcasted_iota(jnp.int32, (LINE, LINE), 0)
    after = lax.broadcasted_iota(jnp.int32, (LINE, LINE), 1)
    earlier = ((before // SLOTS == after // SLOTS) & (before < after)).astype(jnp.bfloat16)
    stacked = jnp.concatenate(hits + hits, axis=0).astype(jnp.bfloat16)
    ranks = jnp.dot(stacked, earlier, preferred_element_type=jnp.float32)
    base = (lax.broadcasted_iota(jnp.int32, (1, LINE), 1) // SLOTS * CAPE).astype(jnp.float32)
    rows = lax.broadcasted_iota(jnp.int32, (SIDE * PICKS, LINE), 0).astype(jnp.float32)
    picks = []
    for j in range(SIDE):
        place = jnp.where(hits[j] > 0.0, base + ranks[j : j + 1], -1.0)
        picks.append((rows == place).astype(jnp.float32))
    return jnp.concatenate(picks, axis=0).astype(jnp.bfloat16)


def select_kernel(targets_ref, *refs):
    pieces, outs, ids_ref = refs[:SIDE], refs[SIDE : 2 * SIDE], refs[2 * SIDE]
    width = pieces[0].shape[1]
    for line in range(SIDE):
        piece = pieces[line][...]
        ids = piece[:, width - MARK :].astype(jnp.float32).T[:TOPK]
        ids_ref[line] = ids
        picks = pick_matrix(targets_ref, ids)
        rows = jnp.dot(picks, piece, preferred_element_type=jnp.float32).astype(jnp.bfloat16)
        rows = rows.reshape(SIDE, SIDE, PICKS, width)
        for j in range(SIDE):
            outs[j][pl.ds(line * SIDE, SIDE)] = rows[j]


def select(targets, pieces):
    width = pieces[0].shape[1]
    vmem = pl.BlockSpec(memory_space=pltpu.VMEM)
    return pl.pallas_call(
        select_kernel,
        out_shape=[jax.ShapeDtypeStruct((PLANE, PICKS, width), jnp.bfloat16)] * SIDE
        + [jax.ShapeDtypeStruct((SIDE, TOPK, LINE), jnp.float32)],
        in_specs=[pl.BlockSpec(memory_space=pltpu.SMEM)] + [vmem] * SIDE,
        out_specs=[vmem] * (SIDE + 1),
        compiler_params=pltpu.CompilerParams(vmem_limit_bytes=32 * 2**20),
        cost_estimate=pl.CostEstimate(
            flops=2 * SIDE * LINE * LINE * width, bytes_accessed=4 * SIDE * LINE * width, transcendentals=0
        ),
    )(targets, *pieces)


def combine_kernel(targets_ref, ids_ref, *refs):
    width = refs[0].shape[2]
    for line in range(SIDE):
        picks = pick_matrix(targets_ref, ids_ref[line])
        blocks = [ref[pl.ds(line * SIDE, SIDE)] for ref in refs[:SIDE]]
        rows = jnp.concatenate([b.reshape(SIDE * PICKS, width) for b in blocks], axis=0)
        total = lax.dot_general(
            picks, rows, (((0,), (0,)), ((), ())), preferred_element_type=jnp.float32
        )
        refs[SIDE + line][...] = total.astype(jnp.bfloat16)


def combine(targets, ids, blocks):
    width = blocks[0].shape[2]
    vmem = pl.BlockSpec(memory_space=pltpu.VMEM)
    return pl.pallas_call(
        combine_kernel,
        out_shape=[jax.ShapeDtypeStruct((LINE, width), jnp.bfloat16)] * SIDE,
        in_specs=[pl.BlockSpec(memory_space=pltpu.SMEM)] + [vmem] * (1 + SIDE),
        out_specs=[vmem] * SIDE,
        compiler_params=pltpu.CompilerParams(vmem_limit_bytes=32 * 2**20),
        cost_estimate=pl.CostEstimate(
            flops=2 * SIDE * LINE * LINE * width, bytes_accessed=4 * SIDE * LINE * width, transcendentals=0
        ),
    )(targets, ids, *blocks)


def together(*trees):
    return lax.optimization_barrier(trees)


def stage_axes():
    return [[tuple(by_core[n] for by_core in orders) for orders in ORDERS] for n in range(3)]


def exchange(blocks, strides, deltas):
    return [hop(block, strides, delta) for block, delta in zip(blocks, deltas)]


def send_rows(columns, targets, packed_cache):
    first, second, third = stage_axes()
    both = range(len(columns))
    rings = [exchange([columns[i]] * 3, first[i], (1, -1, 2)) for i in both]
    columns, rings = together(columns, rings)
    lines = [jnp.concatenate([columns[i]] + rings[i], axis=0) for i in both]
    rings = [exchange([lines[i]] * 3, second[i], (1, -1, 2)) for i in both]
    packed_cache, rings[1][0] = together(packed_cache, rings[1][0])
    lines, rings = together(lines, rings)
    picked = [select(targets[i], [lines[i]] + rings[i]) for i in both]
    rings = [exchange(picked[i][1:SIDE], third[i], TARGETS[1:]) for i in both]
    return [[picked[i][0]] + rings[i] for i in both], [p[SIDE] for p in picked], packed_cache


def return_rows(outward, targets, ids, context):
    first, second, third = stage_axes()
    both = range(len(outward))
    rings = [exchange(outward[i][1:], third[i], (-1, 1, 2)) for i in both]
    rings, context = together(rings, context)
    lines = [combine(targets[i], ids[i], [outward[i][0]] + rings[i]) for i in both]
    rings = [exchange(lines[i][1:], second[i], (-1, 1, 2)) for i in both]
    lines, rings = together(lines, rings)
    sums = []
    for i in both:
        line = add(lines[i][0], *rings[i])
        blocks = [line[k * ROWS : (k + 1) * ROWS] for k in range(SIDE)]
        sums.append([blocks[0]] + exchange(blocks[1:], first[i], (-1, 1, 2)))
    sums, = together(sums)
    return [add(*terms) for terms in sums], context


def add(*terms):
    return sum(t.astype(jnp.float32) for t in terms).astype(jnp.bfloat16)


def half_expert(rows, gate_ref, up_ref):
    gate_pre = jnp.dot(rows, gate_ref[...], preferred_element_type=jnp.float32)
    up_pre = jnp.dot(rows, up_ref[...], preferred_element_type=jnp.float32)
    return (gate_pre * (1.0 / (1.0 + jnp.exp(-gate_pre))) * up_pre).astype(jnp.bfloat16)


def first_half_kernel(order_ref, me_ref, *refs):
    main, minor = refs[:SIDE], refs[SIDE : 2 * SIDE]
    gate_ref, up_ref, down_ref, rows_ref, part_ref, weight_ref = refs[2 * SIDE :]

    def one(group, carry):
        for j in range(SIDE):
            number = j * PLANE + group
            rows_ref[number, :, pl.ds(0, MAIN)] = main[j][group, :, pl.ds(0, MAIN)]
            rows_ref[order_ref[number], :, pl.ds(MAIN, MINOR)] = minor[j][group, :, pl.ds(0, MINOR)]
            mark = main[j][group, :, pl.ds(MAIN, MARK)].astype(jnp.float32)
            total = sum(pltpu.roll(mark, MARK - k * TOPK, 1) for k in range(1, 4))
            lane = lax.broadcasted_iota(jnp.int32, mark.shape, 1)
            mine = (lane < TOPK) & (mark == me_ref[0].astype(jnp.float32))
            total = jnp.sum(jnp.where(mine, total, 0.0), axis=1, keepdims=True)
            weight_ref[number] = jnp.broadcast_to(total, mark.shape)
        return carry

    lax.fori_loop(0, PLANE, one, 0)

    def block(index, carry):
        at = pl.ds(index * BLOCK, BLOCK)
        rows = rows_ref[at].reshape(BLOCK * PICKS, D)
        inner = half_expert(rows, gate_ref, up_ref)
        for start in range(0, D, LAT):
            part = jnp.dot(inner, down_ref[:, start : start + LAT], preferred_element_type=jnp.float32)
            part_ref[at, :, pl.ds(start, LAT)] = part.astype(jnp.bfloat16).reshape(BLOCK, PICKS, LAT)
        return carry

    lax.fori_loop(0, CHIPS // BLOCK, block, 0)


def second_half_kernel(order_ref, rows_ref, part_ref, weight_ref, gate_ref, up_ref, down_ref, *refs):
    main, minor, out_ref = refs[:SIDE], refs[SIDE : 2 * SIDE], refs[2 * SIDE]

    def block(index, carry):
        at = pl.ds(index * BLOCK, BLOCK)
        rows = rows_ref[at].reshape(BLOCK * PICKS, D)
        inner = half_expert(rows, gate_ref, up_ref)
        weight = weight_ref[at].reshape(BLOCK * PICKS, MARK)
        weight = jnp.concatenate([weight] * (LAT // MARK), axis=1)
        for start in range(0, D, LAT):
            part = jnp.dot(inner, down_ref[:, start : start + LAT], preferred_element_type=jnp.float32)
            earlier = part_ref[at, :, pl.ds(start, LAT)].reshape(BLOCK * PICKS, LAT)
            total = (earlier.astype(jnp.float32) + part) * weight
            out_ref[at, :, pl.ds(start, LAT)] = total.astype(jnp.bfloat16).reshape(BLOCK, PICKS, LAT)
        return carry

    lax.fori_loop(0, CHIPS // BLOCK, block, 0)

    def one(group, carry):
        for j in range(SIDE):
            number = j * PLANE + group
            main[j][group] = out_ref[number, :, pl.ds(0, MAIN)]
            minor[j][group] = out_ref[order_ref[number], :, pl.ds(MAIN, MINOR)]
        return carry

    lax.fori_loop(0, PLANE, one, 0)


HALF_COST = pl.CostEstimate(
    flops=2 * CHIPS * PICKS * D * 512 * 3, bytes_accessed=2 * (3 * D * 512 + 3 * CHIPS * PICKS * D), transcendentals=CHIPS * PICKS * 512
)


def first_half(order, me, main, minor, matrices):
    vmem, smem = pl.BlockSpec(memory_space=pltpu.VMEM), pl.BlockSpec(memory_space=pltpu.SMEM)
    whole = jax.ShapeDtypeStruct((CHIPS, PICKS, D), jnp.bfloat16)
    return pl.pallas_call(
        first_half_kernel,
        out_shape=[whole, whole, jax.ShapeDtypeStruct((CHIPS, PICKS, MARK), jnp.float32)],
        in_specs=[smem, smem] + [vmem] * (2 * SIDE + 3),
        out_specs=[vmem] * 3,
        compiler_params=pltpu.CompilerParams(vmem_limit_bytes=52 * 2**20),
        cost_estimate=HALF_COST,
    )(order, me[None], *main, *minor, *matrices)


def second_half(order, rows, part, weight, matrices):
    vmem, smem = pl.BlockSpec(memory_space=pltpu.VMEM), pl.BlockSpec(memory_space=pltpu.SMEM)
    shapes = [(PLANE, PICKS, width) for width in (MAIN, MINOR) for _ in range(SIDE)]
    outs = pl.pallas_call(
        second_half_kernel,
        out_shape=[jax.ShapeDtypeStruct(shape, jnp.bfloat16) for shape in shapes],
        in_specs=[smem] + [vmem] * 6,
        out_specs=[vmem] * (2 * SIDE),
        scratch_shapes=[pltpu.VMEM((CHIPS, PICKS, D), jnp.bfloat16)],
        compiler_params=pltpu.CompilerParams(vmem_limit_bytes=52 * 2**20),
        cost_estimate=HALF_COST,
    )(order, rows, part, weight, *matrices)
    return outs[:SIDE], outs[SIDE:]


def three_parts(weights):
    high = lax.reduce_precision(weights, 8, 7)
    rest = weights - high
    mid = lax.reduce_precision(rest, 8, 7)
    return [part.astype(jnp.bfloat16) for part in (high, mid, rest - mid)]


def pack_kernel(from_ref, slot_ref, len_ref, cache_ref, out_ref):
    row = lax.broadcasted_iota(jnp.int32, (HALF, 128), 0)
    lane = lax.broadcasted_iota(jnp.int32, (HALF, 128), 1)

    def one(chip, carry):
        block = cache_ref[from_ref[chip]]
        out_ref[chip] = block
        mark = jnp.where(lane == 0, slot_ref[chip], len_ref[chip]).astype(jnp.float32)
        head = jnp.where((row == HALF - 1) & (lane < 2), mark, block[:, :128].astype(jnp.float32))
        out_ref[chip, :, pl.ds(0, 128)] = head.astype(jnp.bfloat16)
        return carry

    lax.fori_loop(0, out_ref.shape[0], one, 0)


def pack_cache(send_from, sent_slot, sent_len, cache):
    chips = send_from.shape[0]
    small = pl.BlockSpec(memory_space=pltpu.SMEM)
    return pl.pallas_call(
        pack_kernel,
        out_shape=jax.ShapeDtypeStruct((chips,) + cache.shape[1:], jnp.bfloat16),
        in_specs=[small, small, small, pl.BlockSpec(memory_space=pltpu.VMEM)],
        out_specs=pl.BlockSpec(memory_space=pltpu.VMEM),
        compiler_params=pltpu.CompilerParams(vmem_limit_bytes=24 * 2**20),
        cost_estimate=pl.CostEstimate(
            flops=0, bytes_accessed=2 * (chips + cache.shape[0]) * CTX * KVW, transcendentals=0
        ),
    )(send_from, sent_slot, sent_len, cache)


def on_device(
    kv_cache,
    lengths,
    move_list,
    queries,
    new_kv,
    hidden,
    expert_ids,
    gate_weights,
    expert_gate,
    expert_up,
    expert_down,
):
    ep_count = lax.axis_size("ep")
    slot_count = lengths.shape[0]
    own = (expert_gate[0], expert_up[0], expert_down[0])
    expert_range = jnp.arange(ep_count, dtype=jnp.int32)
    me = lax.axis_index("ep")
    core = lax.axis_index("dp")

    marks = [expert_ids.astype(jnp.bfloat16)] + three_parts(gate_weights)
    marks = jnp.concatenate(marks, axis=2).reshape(ROWS, 4 * TOPK)
    marks = jnp.pad(marks, ((0, 0), (0, MARK - 4 * TOPK)))
    rows = hidden.reshape(ROWS, D)
    columns = [
        jnp.concatenate([block, marks], axis=1) for block in (rows[:, :MAIN], rows[:, MAIN:])
    ]
    targets = []
    for orders in ORDERS:
        stride = jnp.where(core == 0, orders[0][2], orders[1][2])
        targets.append(
            jnp.stack([chip_at(stride, delta, me) for delta in TARGETS]).astype(jnp.int32)
        )
    slot_range = jnp.arange(slot_count, dtype=jnp.int32)
    send_hit = expert_range[:, None] == move_list[:, 0][None, :]
    send_from = jnp.sum(jnp.where(send_hit, slot_range[None, :], 0), axis=1)
    sent_slot = jnp.sum(jnp.where(send_hit, move_list[:, 1][None, :] + 1, 0), axis=1) - 1
    sent_len = jnp.sum(jnp.where(send_hit, lengths[None, :], 0), axis=1)
    packed_cache = pack_cache(
        send_from, sent_slot, sent_len, kv_cache.reshape(slot_count, HALF, 2 * KVW)
    )
    arrived, ids, packed_cache = send_rows(columns, targets, packed_cache)
    got = lax.all_to_all(packed_cache, "ep", split_axis=0, concat_axis=0, tiled=True)
    arrived, own = together(arrived, own)
    other = tuple(lax.ppermute(w, "dp", [(0, 1), (1, 0)]) for w in own)

    tables = []
    for main, minor in zip(*ORDERS):
        table = [0] * CHIPS
        for number in range(CHIPS):
            digits = (number // PLANE, number // SIDE % SIDE, number % SIDE)
            place = dict(zip(main, digits[::-1]))
            index = place[minor[2]] * PLANE + place[minor[1]] * SIDE + place[minor[0]]
            table[index] = number
        tables.append(jnp.array(table, jnp.int32))
    order = jnp.where(core == 0, tables[0], tables[1])
    rows, part, weight = first_half(order, me, arrived[0], arrived[1], own)
    outward = second_half(order, rows, part, weight, other)
    outward, got = lax.optimization_barrier((outward, got))
    got_slot = got[:, HALF - 1, 0].astype(jnp.int32)
    got_len = got[:, HALF - 1, 1].astype(jnp.int32)
    land_hit = got_slot[None, :] == slot_range[:, None]
    landing = jnp.sum(jnp.where(land_hit, expert_range[None, :], 0), axis=1)
    placed_len = jnp.sum(jnp.where(land_hit, got_len[None, :], 0), axis=1)

    context = attend(queries, new_kv, got, landing, placed_len)
    sums, context = return_rows(outward, targets, ids, context)
    mixture = jnp.concatenate(sums, axis=1).reshape(STEPS, SLOTS, D)
    return context, mixture


def solution(mesh):
    return jax.shard_map(
        on_device,
        mesh=mesh,
        in_specs=(
            P(("dp", "ep"), None),
            P(("dp", "ep")),
            P(("dp", "ep"), None),
            P(None, ("dp", "ep"), None),
            P(None, ("dp", "ep"), None),
            P(None, ("dp", "ep"), None),
            P(None, ("dp", "ep"), None),
            P(None, ("dp", "ep"), None),
            P("ep", None, "dp"),
            P("ep", None, "dp"),
            P("ep", "dp", None),
        ),
        out_specs=(P(None, ("dp", "ep"), None), P(None, ("dp", "ep"), None)),
        check_vma=False,
    )
```

```python
import jax
import jax.numpy as jnp
from jax import lax
from jax.experimental import pallas as pl
from jax.experimental.pallas import tpu as pltpu
from jax.sharding import PartitionSpec as P

D = 3584
H = 64
LAT = 512
TOPK = 8
STEPS = 2
CTX = 64
KVW = 576
HALF = CTX // 2
GROUP = 16
TOGETHER = 8
WIDE = 640
SIDE = 4
Z, Y, X = SIDE * SIDE, SIDE, 1
MAIN = 2560
MINOR = D - MAIN
MARK = 128
SLOTS = 32
CAPE = 8
ROWS = STEPS * SLOTS
PICKS = STEPS * CAPE
LINE = SIDE * ROWS
PLANE = SIDE * SIDE
CHIPS = SIDE**3
BLOCK = 32
ORDERS = (((Z, Y, X), (Y, X, Z)), ((X, Z, Y), (X, Z, Y)))
SOURCES = (0, -1, 2, 1)
TARGETS = (0, 1, 2, -1)
KEYS = GROUP * (CTX + STEPS)


score_scale = 192.0 ** (-0.5)


def attend_kernel(landing_ref, got_ref, len_ref, new_ref, query_ref, out_ref, even_ref, odd_ref, value_ref, bias_ref):
    pairs = GROUP * HALF

    def lanes(rows):
        return lax.broadcasted_iota(jnp.int32, (rows, WIDE), 1)

    def place(keys, rows, at):
        even_ref[pl.ds(at, rows), :] = keys.astype(jnp.bfloat16)
        odd_ref[pl.ds(at, rows), :] = pltpu.roll(keys, WIDE - KVW, 1).astype(jnp.bfloat16)
        value_ref[pl.ds(at, rows), :] = keys[:, :LAT].astype(jnp.bfloat16)

    def one(slot, carry):
        source = landing_ref[slot]
        block = got_ref[source]
        first = jnp.where(lanes(HALF) < KVW, block[:, :WIDE].astype(jnp.float32), 0.0)
        at = pl.multiple_of(slot * HALF, HALF)
        place(first, HALF, at)
        second = block[:, LAT:].astype(jnp.float32)
        second = jnp.where(lanes(HALF) < WIDE - KVW, 0.0, second)
        place(pltpu.roll(second, KVW, 1), HALF, pl.multiple_of(pairs + at, HALF))
        return carry

    lax.fori_loop(0, GROUP, one, 0)
    for step in range(STEPS):
        rows = new_ref[step].astype(jnp.float32)
        rows = jnp.concatenate([rows, jnp.zeros((GROUP, WIDE - KVW), jnp.float32)], axis=1)
        place(rows, GROUP, 2 * pairs + step * GROUP)

    column = lax.broadcasted_iota(jnp.int32, (GROUP, KEYS), 1)
    row = lax.broadcasted_iota(jnp.int32, (GROUP, KEYS), 0)
    cached = column < 2 * pairs
    half = (column >= pairs).astype(jnp.int32)
    within = column - half * pairs
    position = 2 * (within % HALF) + half
    recent = column - 2 * pairs
    owner = jnp.where(cached, within // HALF, recent % GROUP)
    live = cached & (position < len_ref[...])
    for step in range(STEPS):
        allowed = (live | (~cached & (recent < (step + 1) * GROUP))) & (owner == row)
        bias_ref[pl.ds(step * GROUP, GROUP), :] = jnp.where(allowed, 0.0, -jnp.inf)

    def heads(index, carry):
        bias = jnp.concatenate([bias_ref[...]] * TOGETHER, axis=0)
        for odd in range(2):
            slabs = []
            for k in range(TOGETHER):
                start = pl.multiple_of((index * TOGETHER + k) * 2 * KVW + odd * LAT, 128)
                for step in range(STEPS):
                    slabs.append(query_ref[step, :, pl.ds(start, WIDE)])
            keys = odd_ref[...] if odd else even_ref[...]
            score = lax.dot_general(
                jnp.concatenate(slabs, axis=0),
                keys,
                (((1,), (1,)), ((), ())),
                preferred_element_type=jnp.float32,
            )
            score = score * score_scale + bias
            weight = jnp.exp(score - jnp.max(score, axis=1, keepdims=True))
            prob = weight * (1.0 / jnp.sum(weight, axis=1, keepdims=True))
            mixed = jnp.dot(
                prob.astype(jnp.bfloat16), value_ref[...], preferred_element_type=jnp.float32
            ).astype(jnp.bfloat16)
            for k in range(TOGETHER):
                start = pl.multiple_of(((index * TOGETHER + k) * 2 + odd) * LAT, LAT)
                for step in range(STEPS):
                    at = (k * STEPS + step) * GROUP
                    out_ref[step, :, pl.ds(start, LAT)] = mixed[at : at + GROUP]
        return carry

    lax.fori_loop(0, H // (2 * TOGETHER), heads, 0)


def attend(queries, new_kv, got, landing, placed_len, earlier):
    slots = queries.shape[1]
    group = 0 if earlier is None else 1
    specs = [
        pl.BlockSpec(memory_space=pltpu.SMEM),
        pl.BlockSpec(memory_space=pltpu.VMEM),
        pl.BlockSpec((GROUP, 1), lambda g: (group, 0)),
        pl.BlockSpec((STEPS, GROUP, KVW), lambda g: (0, group, 0)),
        pl.BlockSpec((STEPS, GROUP, H * KVW), lambda g: (0, group, 0)),
    ]
    operands = [landing[group * GROUP :][:GROUP], got, placed_len[:, None], new_kv, queries]
    kernel = attend_kernel
    if earlier is not None:
        specs.append(pl.BlockSpec(memory_space=pl.ANY))
        operands.append(earlier)

        def kernel(*refs):
            attend_kernel(*refs[:5], *refs[6:])

    return pl.pallas_call(
        kernel,
        grid=(1,),
        out_shape=jax.ShapeDtypeStruct((STEPS, slots, H * LAT), jnp.bfloat16),
        in_specs=specs,
        out_specs=pl.BlockSpec((STEPS, GROUP, H * LAT), lambda g: (0, group, 0)),
        scratch_shapes=[
            pltpu.VMEM((KEYS, WIDE), jnp.bfloat16),
            pltpu.VMEM((KEYS, WIDE), jnp.bfloat16),
            pltpu.VMEM((KEYS, LAT), jnp.bfloat16),
            pltpu.VMEM((STEPS * GROUP, KEYS), jnp.float32),
        ],
        input_output_aliases={} if earlier is None else {5: 0},
        compiler_params=pltpu.CompilerParams(vmem_limit_bytes=32 * 2**20),
        cost_estimate=pl.CostEstimate(
            flops=2 * STEPS * GROUP * H * KEYS * (WIDE + LAT),
            bytes_accessed=2 * STEPS * GROUP * H * (KVW + LAT),
            transcendentals=STEPS * GROUP * H * KEYS,
        ),
    )(*operands)


def hop(value, strides, delta):
    pairs = []
    for core, stride in enumerate(strides):
        for chip in range(CHIPS):
            place = chip // stride % SIDE
            there = chip + ((place + delta) % SIDE - place) * stride
            pairs.append((core * CHIPS + chip, core * CHIPS + there))
    return lax.ppermute(value, ("dp", "ep"), pairs)


def chip_at(stride, delta, start):
    place = start // stride % SIDE
    return start + ((place + delta) % SIDE - place) * stride


def pick_matrix(targets_ref, ids):
    hits = [
        jnp.sum((ids == targets_ref[j].astype(jnp.float32)).astype(jnp.float32), axis=0, keepdims=True)
        for j in range(SIDE)
    ]
    before = lax.broadcasted_iota(jnp.int32, (LINE, LINE), 0)
    after = lax.broadcasted_iota(jnp.int32, (LINE, LINE), 1)
    earlier = ((before // SLOTS == after // SLOTS) & (before < after)).astype(jnp.bfloat16)
    stacked = jnp.concatenate(hits + hits, axis=0).astype(jnp.bfloat16)
    ranks = jnp.dot(stacked, earlier, preferred_element_type=jnp.float32)
    base = (lax.broadcasted_iota(jnp.int32, (1, LINE), 1) // SLOTS * CAPE).astype(jnp.float32)
    rows = lax.broadcasted_iota(jnp.int32, (SIDE * PICKS, LINE), 0).astype(jnp.float32)
    picks = []
    for j in range(SIDE):
        place = jnp.where(hits[j] > 0.0, base + ranks[j : j + 1], -1.0)
        picks.append((rows == place).astype(jnp.float32))
    return jnp.concatenate(picks, axis=0).astype(jnp.bfloat16)


def select_kernel(targets_ref, *refs):
    pieces, outs, ids_ref = refs[:SIDE], refs[SIDE : 2 * SIDE], refs[2 * SIDE]
    width = pieces[0].shape[1]
    for line in range(SIDE):
        piece = pieces[line][...]
        ids = piece[:, width - MARK :].astype(jnp.float32).T[:TOPK]
        ids_ref[line] = ids
        picks = pick_matrix(targets_ref, ids)
        rows = jnp.dot(picks, piece, preferred_element_type=jnp.float32).astype(jnp.bfloat16)
        rows = rows.reshape(SIDE, SIDE, PICKS, width)
        for j in range(SIDE):
            outs[j][pl.ds(line * SIDE, SIDE)] = rows[j]


def select(targets, pieces):
    width = pieces[0].shape[1]
    vmem = pl.BlockSpec(memory_space=pltpu.VMEM)
    return pl.pallas_call(
        select_kernel,
        out_shape=[jax.ShapeDtypeStruct((PLANE, PICKS, width), jnp.bfloat16)] * SIDE
        + [jax.ShapeDtypeStruct((SIDE, TOPK, LINE), jnp.float32)],
        in_specs=[pl.BlockSpec(memory_space=pltpu.SMEM)] + [vmem] * SIDE,
        out_specs=[vmem] * (SIDE + 1),
        compiler_params=pltpu.CompilerParams(vmem_limit_bytes=32 * 2**20),
        cost_estimate=pl.CostEstimate(
            flops=2 * SIDE * LINE * LINE * width, bytes_accessed=4 * SIDE * LINE * width, transcendentals=0
        ),
    )(targets, *pieces)


def combine_kernel(targets_ref, ids_ref, *refs):
    width = refs[0].shape[2]
    for line in range(SIDE):
        picks = pick_matrix(targets_ref, ids_ref[line])
        blocks = [ref[pl.ds(line * SIDE, SIDE)] for ref in refs[:SIDE]]
        rows = jnp.concatenate([b.reshape(SIDE * PICKS, width) for b in blocks], axis=0)
        total = lax.dot_general(
            picks, rows, (((0,), (0,)), ((), ())), preferred_element_type=jnp.float32
        )
        refs[SIDE + line][...] = total.astype(jnp.bfloat16)


def combine(targets, ids, blocks):
    width = blocks[0].shape[2]
    vmem = pl.BlockSpec(memory_space=pltpu.VMEM)
    return pl.pallas_call(
        combine_kernel,
        out_shape=[jax.ShapeDtypeStruct((LINE, width), jnp.bfloat16)] * SIDE,
        in_specs=[pl.BlockSpec(memory_space=pltpu.SMEM)] + [vmem] * (1 + SIDE),
        out_specs=[vmem] * SIDE,
        compiler_params=pltpu.CompilerParams(vmem_limit_bytes=32 * 2**20),
        cost_estimate=pl.CostEstimate(
            flops=2 * SIDE * LINE * LINE * width, bytes_accessed=4 * SIDE * LINE * width, transcendentals=0
        ),
    )(targets, ids, *blocks)


def together(*trees):
    return lax.optimization_barrier(trees)


def stage_axes():
    return [[tuple(by_core[n] for by_core in orders) for orders in ORDERS] for n in range(3)]


def exchange(blocks, strides, deltas):
    return [hop(block, strides, delta) for block, delta in zip(blocks, deltas)]


def send_rows(columns, targets, packed_cache):
    first, second, third = stage_axes()
    both = range(len(columns))
    rings = [exchange([columns[i]] * 3, first[i], TARGETS[1:]) for i in both]
    columns, rings = together(columns, rings)
    lines = [jnp.concatenate([columns[i]] + rings[i], axis=0) for i in both]
    rings = [exchange([lines[i]] * 3, second[i], TARGETS[1:]) for i in both]
    packed_cache, rings[1][0] = together(packed_cache, rings[1][0])
    lines, rings = together(lines, rings)
    picked = [list(select(targets[0], [lines[0]] + rings[0]))]
    lines[1], picked[0][SIDE] = together(lines[1], picked[0][SIDE])
    picked.append(select(targets[1], [lines[1]] + rings[1]))
    rings = [exchange(picked[i][1:SIDE], third[i], TARGETS[1:]) for i in both]
    return [[picked[i][0]] + rings[i] for i in both], [p[SIDE] for p in picked], packed_cache


def return_rows(outward, targets, ids, contexts):
    first, second, third = stage_axes()
    both = range(len(outward))
    rings = [exchange(outward[i][1:], third[i], SOURCES[1:]) for i in both]
    context = contexts(None)
    rings, context = together(rings, context)
    lines = [combine(targets[i], ids[i], [outward[i][0]] + rings[i]) for i in both]
    rings = [exchange(lines[i][1:], second[i], SOURCES[1:]) for i in both]
    context = contexts(context)
    rings, context = together(rings, context)
    sums = []
    for i in both:
        line = add(lines[i][0], *rings[i])
        blocks = [line[k * ROWS : (k + 1) * ROWS] for k in range(SIDE)]
        sums.append([blocks[0]] + exchange(blocks[1:], first[i], SOURCES[1:]))
    sums, = together(sums)
    return [add(*terms) for terms in sums], context


def add(*terms):
    return sum(t.astype(jnp.float32) for t in terms).astype(jnp.bfloat16)


def half_expert(rows, gate_ref, up_ref):
    gate_pre = jnp.dot(rows, gate_ref[...], preferred_element_type=jnp.float32)
    up_pre = jnp.dot(rows, up_ref[...], preferred_element_type=jnp.float32)
    return (gate_pre * (1.0 / (1.0 + jnp.exp(-gate_pre))) * up_pre).astype(jnp.bfloat16)


def first_half_kernel(order_ref, me_ref, *refs):
    main, minor = refs[:SIDE], refs[SIDE : 2 * SIDE]
    gate_ref, up_ref, down_ref, rows_ref, part_ref, weight_ref = refs[2 * SIDE :]

    def one(group, carry):
        for j in range(SIDE):
            number = j * PLANE + group
            rows_ref[number, :, pl.ds(0, MAIN)] = main[j][group, :, pl.ds(0, MAIN)]
            rows_ref[order_ref[number], :, pl.ds(MAIN, MINOR)] = minor[j][group, :, pl.ds(0, MINOR)]
            mark = main[j][group, :, pl.ds(MAIN, MARK)].astype(jnp.float32)
            total = sum(pltpu.roll(mark, MARK - k * TOPK, 1) for k in range(1, 4))
            lane = lax.broadcasted_iota(jnp.int32, mark.shape, 1)
            mine = (lane < TOPK) & (mark == me_ref[0].astype(jnp.float32))
            total = jnp.sum(jnp.where(mine, total, 0.0), axis=1, keepdims=True)
            weight_ref[number] = jnp.broadcast_to(total, mark.shape)
        return carry

    lax.fori_loop(0, PLANE, one, 0)

    def block(index, carry):
        at = pl.ds(index * BLOCK, BLOCK)
        rows = rows_ref[at].reshape(BLOCK * PICKS, D)
        inner = half_expert(rows, gate_ref, up_ref)
        for start in range(0, D, LAT):
            part = jnp.dot(inner, down_ref[:, start : start + LAT], preferred_element_type=jnp.float32)
            part_ref[at, :, pl.ds(start, LAT)] = part.astype(jnp.bfloat16).reshape(BLOCK, PICKS, LAT)
        return carry

    lax.fori_loop(0, CHIPS // BLOCK, block, 0)


def second_half_kernel(order_ref, rows_ref, part_ref, weight_ref, gate_ref, up_ref, down_ref, *refs):
    main, minor, out_ref = refs[:SIDE], refs[SIDE : 2 * SIDE], refs[2 * SIDE]

    def block(index, carry):
        at = pl.ds(index * BLOCK, BLOCK)
        rows = rows_ref[at].reshape(BLOCK * PICKS, D)
        inner = half_expert(rows, gate_ref, up_ref)
        weight = weight_ref[at].reshape(BLOCK * PICKS, MARK)
        weight = jnp.concatenate([weight] * (LAT // MARK), axis=1)
        for start in range(0, D, LAT):
            part = jnp.dot(inner, down_ref[:, start : start + LAT], preferred_element_type=jnp.float32)
            earlier = part_ref[at, :, pl.ds(start, LAT)].reshape(BLOCK * PICKS, LAT)
            total = (earlier.astype(jnp.float32) + part) * weight
            out_ref[at, :, pl.ds(start, LAT)] = total.astype(jnp.bfloat16).reshape(BLOCK, PICKS, LAT)
        return carry

    lax.fori_loop(0, CHIPS // BLOCK, block, 0)

    def one(group, carry):
        for j in range(SIDE):
            number = j * PLANE + group
            main[j][group] = out_ref[number, :, pl.ds(0, MAIN)]
            minor[j][group] = out_ref[order_ref[number], :, pl.ds(MAIN, MINOR)]
        return carry

    lax.fori_loop(0, PLANE, one, 0)


HALF_COST = pl.CostEstimate(
    flops=2 * CHIPS * PICKS * D * 512 * 3, bytes_accessed=2 * (3 * D * 512 + 3 * CHIPS * PICKS * D), transcendentals=CHIPS * PICKS * 512
)


def first_half(order, me, main, minor, matrices):
    vmem, smem = pl.BlockSpec(memory_space=pltpu.VMEM), pl.BlockSpec(memory_space=pltpu.SMEM)
    whole = jax.ShapeDtypeStruct((CHIPS, PICKS, D), jnp.bfloat16)
    return pl.pallas_call(
        first_half_kernel,
        out_shape=[whole, whole, jax.ShapeDtypeStruct((CHIPS, PICKS, MARK), jnp.float32)],
        in_specs=[smem, smem] + [vmem] * (2 * SIDE + 3),
        out_specs=[vmem] * 3,
        compiler_params=pltpu.CompilerParams(vmem_limit_bytes=52 * 2**20),
        cost_estimate=HALF_COST,
    )(order, me[None], *main, *minor, *matrices)


def second_half(order, rows, part, weight, matrices):
    vmem, smem = pl.BlockSpec(memory_space=pltpu.VMEM), pl.BlockSpec(memory_space=pltpu.SMEM)
    shapes = [(PLANE, PICKS, width) for width in (MAIN, MINOR) for _ in range(SIDE)]
    outs = pl.pallas_call(
        second_half_kernel,
        out_shape=[jax.ShapeDtypeStruct(shape, jnp.bfloat16) for shape in shapes],
        in_specs=[smem] + [vmem] * 6,
        out_specs=[vmem] * (2 * SIDE),
        scratch_shapes=[pltpu.VMEM((CHIPS, PICKS, D), jnp.bfloat16)],
        compiler_params=pltpu.CompilerParams(vmem_limit_bytes=52 * 2**20),
        cost_estimate=HALF_COST,
    )(order, rows, part, weight, *matrices)
    return outs[:SIDE], outs[SIDE:]


def three_parts(weights):
    high = lax.reduce_precision(weights, 8, 7)
    rest = weights - high
    mid = lax.reduce_precision(rest, 8, 7)
    return [part.astype(jnp.bfloat16) for part in (high, mid, rest - mid)]


def pack_kernel(from_ref, slot_ref, len_ref, cache_ref, out_ref):
    row = lax.broadcasted_iota(jnp.int32, (HALF, 128), 0)
    lane = lax.broadcasted_iota(jnp.int32, (HALF, 128), 1)

    def one(chip, carry):
        block = cache_ref[from_ref[chip]]
        out_ref[chip] = block
        mark = jnp.where(lane == 0, slot_ref[chip], len_ref[chip]).astype(jnp.float32)
        head = jnp.where((row == HALF - 1) & (lane < 2), mark, block[:, :128].astype(jnp.float32))
        out_ref[chip, :, pl.ds(0, 128)] = head.astype(jnp.bfloat16)
        return carry

    lax.fori_loop(0, out_ref.shape[0], one, 0)


def pack_cache(send_from, sent_slot, sent_len, cache):
    chips = send_from.shape[0]
    small = pl.BlockSpec(memory_space=pltpu.SMEM)
    return pl.pallas_call(
        pack_kernel,
        out_shape=jax.ShapeDtypeStruct((chips,) + cache.shape[1:], jnp.bfloat16),
        in_specs=[small, small, small, pl.BlockSpec(memory_space=pltpu.VMEM)],
        out_specs=pl.BlockSpec(memory_space=pltpu.VMEM),
        compiler_params=pltpu.CompilerParams(vmem_limit_bytes=24 * 2**20),
        cost_estimate=pl.CostEstimate(
            flops=0, bytes_accessed=2 * (chips + cache.shape[0]) * CTX * KVW, transcendentals=0
        ),
    )(send_from, sent_slot, sent_len, cache)


def on_device(
    kv_cache,
    lengths,
    move_list,
    queries,
    new_kv,
    hidden,
    expert_ids,
    gate_weights,
    expert_gate,
    expert_up,
    expert_down,
):
    ep_count = lax.axis_size("ep")
    slot_count = lengths.shape[0]
    own = (expert_gate[0], expert_up[0], expert_down[0])
    expert_range = jnp.arange(ep_count, dtype=jnp.int32)
    me = lax.axis_index("ep")
    core = lax.axis_index("dp")

    marks = [expert_ids.astype(jnp.bfloat16)] + three_parts(gate_weights)
    marks = jnp.concatenate(marks, axis=2).reshape(ROWS, 4 * TOPK)
    marks = jnp.pad(marks, ((0, 0), (0, MARK - 4 * TOPK)))
    rows = hidden.reshape(ROWS, D)
    columns = [
        jnp.concatenate([block, marks], axis=1) for block in (rows[:, :MAIN], rows[:, MAIN:])
    ]
    targets = []
    for orders in ORDERS:
        stride = jnp.where(core == 0, orders[0][2], orders[1][2])
        targets.append(
            jnp.stack([chip_at(stride, delta, me) for delta in TARGETS]).astype(jnp.int32)
        )
    slot_range = jnp.arange(slot_count, dtype=jnp.int32)
    send_hit = expert_range[:, None] == move_list[:, 0][None, :]
    send_from = jnp.sum(jnp.where(send_hit, slot_range[None, :], 0), axis=1)
    sent_slot = jnp.sum(jnp.where(send_hit, move_list[:, 1][None, :] + 1, 0), axis=1) - 1
    sent_len = jnp.sum(jnp.where(send_hit, lengths[None, :], 0), axis=1)
    packed_cache = pack_cache(
        send_from, sent_slot, sent_len, kv_cache.reshape(slot_count, HALF, 2 * KVW)
    )
    arrived, ids, packed_cache = send_rows(columns, targets, packed_cache)
    got = lax.all_to_all(packed_cache, "ep", split_axis=0, concat_axis=0, tiled=True)
    arrived, own = together(arrived, own)
    other = tuple(lax.ppermute(w, "dp", [(0, 1), (1, 0)]) for w in own)

    tables = []
    for main, minor in zip(*ORDERS):
        table = [0] * CHIPS
        for number in range(CHIPS):
            digits = (number // PLANE, number // SIDE % SIDE, number % SIDE)
            place = dict(zip(main, digits[::-1]))
            index = place[minor[2]] * PLANE + place[minor[1]] * SIDE + place[minor[0]]
            table[index] = number
        tables.append(jnp.array(table, jnp.int32))
    order = jnp.where(core == 0, tables[0], tables[1])
    rows, part, weight = first_half(order, me, arrived[0], arrived[1], own)
    outward = second_half(order, rows, part, weight, other)
    got_mark = lax.optimization_barrier(got[:, HALF - 1, :128]).astype(jnp.int32)
    got_slot, got_len = got_mark[:, 0], got_mark[:, 1]
    land_hit = got_slot[None, :] == slot_range[:, None]
    landing = jnp.sum(jnp.where(land_hit, expert_range[None, :], 0), axis=1)
    placed_len = jnp.sum(jnp.where(land_hit, got_len[None, :], 0), axis=1)

    def contexts(earlier):
        return attend(queries, new_kv, got, landing, placed_len, earlier)

    sums, context = return_rows(outward, targets, ids, contexts)
    mixture = jnp.concatenate(sums, axis=1).reshape(STEPS, SLOTS, D)
    return context, mixture


def solution(mesh):
    return jax.shard_map(
        on_device,
        mesh=mesh,
        in_specs=(
            P(("dp", "ep"), None),
            P(("dp", "ep")),
            P(("dp", "ep"), None),
            P(None, ("dp", "ep"), None),
            P(None, ("dp", "ep"), None),
            P(None, ("dp", "ep"), None),
            P(None, ("dp", "ep"), None),
            P(None, ("dp", "ep"), None),
            P("ep", None, "dp"),
            P("ep", None, "dp"),
            P("ep", "dp", None),
        ),
        out_specs=(P(None, ("dp", "ep"), None), P(None, ("dp", "ep"), None)),
        check_vma=False,
    )
```

```python
import jax
import jax.numpy as jnp
from jax import lax
from jax.experimental import pallas as pl
from jax.experimental.pallas import tpu as pltpu
from jax.sharding import PartitionSpec as P

D = 3584
H = 64
LAT = 512
TOPK = 8
STEPS = 2
CTX = 64
KVW = 576
LIVE = CTX - STEPS
HALF = CTX // 2
GROUP = 16
TOGETHER = 8
WIDE = 640
SIDE = 4
Z, Y, X = SIDE * SIDE, SIDE, 1
MAIN = 2432
MINOR = D - MAIN
MARK = 128
SLOTS = 32
CAPE = 8
ROWS = STEPS * SLOTS
PICKS = STEPS * CAPE
LINE = SIDE * ROWS
PLANE = SIDE * SIDE
CHIPS = SIDE**3
BLOCK = 32
ORDERS = (((Z, Y, X), (Y, X, Z)), ((X, Z, Y), (X, Z, Y)))
TARGETS = (0, 1, -1, 2)
KEYS = GROUP * CTX


score_scale = 192.0 ** (-0.5)
base_two_scale = score_scale * 1.4426950408889634


def attend_kernel(
    landing_ref, got_ref, len_ref, new_ref, query_ref, out_ref,
    even_ref, odd_ref, value_ref, bias_ref, recent_ref,
):
    pairs = GROUP * HALF
    lane = lax.broadcasted_iota(jnp.int32, (HALF, WIDE), 1)
    last = lax.broadcasted_iota(jnp.int32, (HALF, WIDE), 0) == HALF - 1
    for step in range(STEPS):
        rows = new_ref[step].astype(jnp.float32)
        recent_ref[step] = jnp.concatenate(
            [rows, jnp.zeros((GROUP, WIDE - KVW), jnp.float32)], axis=1
        )

    def place(keys, at):
        even_ref[pl.ds(at, HALF), :] = keys.astype(jnp.bfloat16)
        odd_ref[pl.ds(at, HALF), :] = pltpu.roll(keys, WIDE - KVW, 1).astype(jnp.bfloat16)
        value_ref[pl.ds(at, HALF), :] = keys[:, :LAT].astype(jnp.bfloat16)

    def one(slot, carry):
        block = got_ref[landing_ref[slot]]
        first = jnp.where(lane < KVW, block[:, :WIDE].astype(jnp.float32), 0.0)
        first = jnp.where(last, recent_ref[0, pl.ds(slot, 1), :], first)
        at = pl.multiple_of(slot * HALF, HALF)
        place(first, at)
        second = block[:, LAT:].astype(jnp.float32)
        second = pltpu.roll(jnp.where(lane < WIDE - KVW, 0.0, second), KVW, 1)
        second = jnp.where(last, recent_ref[1, pl.ds(slot, 1), :], second)
        place(second, pl.multiple_of(pairs + at, HALF))
        return carry

    lax.fori_loop(0, GROUP, one, 0)

    column = lax.broadcasted_iota(jnp.int32, (GROUP, KEYS), 1)
    row = lax.broadcasted_iota(jnp.int32, (GROUP, KEYS), 0)
    half = (column >= pairs).astype(jnp.int32)
    within = column - half * pairs
    position = 2 * (within % HALF) + half
    cached = position < len_ref[...]
    for step in range(STEPS):
        recent = (position >= LIVE) & (position <= LIVE + step)
        allowed = (cached | recent) & (within // HALF == row)
        bias_ref[pl.ds(step * GROUP, GROUP), :] = jnp.where(allowed, 0.0, -jnp.inf)

    def heads(index, carry):
        bias = jnp.concatenate([bias_ref[...]] * TOGETHER, axis=0)
        for odd in range(2):
            slabs = []
            for k in range(TOGETHER):
                start = pl.multiple_of((index * TOGETHER + k) * 2 * KVW + odd * LAT, 128)
                for step in range(STEPS):
                    slabs.append(query_ref[step, :, pl.ds(start, WIDE)])
            keys = odd_ref[...] if odd else even_ref[...]
            score = lax.dot_general(
                jnp.concatenate(slabs, axis=0),
                keys,
                (((1,), (1,)), ((), ())),
                preferred_element_type=jnp.float32,
            )
            score = score + bias
            weight = jnp.exp2((score - jnp.max(score, axis=1, keepdims=True)) * base_two_scale)
            total = jnp.sum(weight, axis=1, keepdims=True)
            mixed = jnp.dot(
                weight.astype(jnp.bfloat16), value_ref[...], preferred_element_type=jnp.float32
            )
            mixed = (mixed * (1.0 / total)).astype(jnp.bfloat16)
            for k in range(TOGETHER):
                start = pl.multiple_of(((index * TOGETHER + k) * 2 + odd) * LAT, LAT)
                for step in range(STEPS):
                    at = (k * STEPS + step) * GROUP
                    out_ref[step, :, pl.ds(start, LAT)] = mixed[at : at + GROUP]
        return carry

    lax.fori_loop(0, H // (2 * TOGETHER), heads, 0)


def attend(queries, new_kv, got, landing, placed_len, earlier):
    slots = queries.shape[1]
    group = 0 if earlier is None else 1
    specs = [
        pl.BlockSpec(memory_space=pltpu.SMEM),
        pl.BlockSpec(memory_space=pltpu.VMEM),
        pl.BlockSpec((GROUP, 1), lambda g: (group, 0)),
        pl.BlockSpec((STEPS, GROUP, KVW), lambda g: (0, group, 0)),
        pl.BlockSpec((STEPS, GROUP, H * KVW), lambda g: (0, group, 0)),
    ]
    operands = [landing[group * GROUP :][:GROUP], got, placed_len[:, None], new_kv, queries]
    kernel = attend_kernel
    if earlier is not None:
        specs.append(pl.BlockSpec(memory_space=pl.ANY))
        operands.append(earlier)

        def kernel(*refs):
            attend_kernel(*refs[:5], *refs[6:])

    return pl.pallas_call(
        kernel,
        grid=(1,),
        out_shape=jax.ShapeDtypeStruct((STEPS, slots, H * LAT), jnp.bfloat16),
        in_specs=specs,
        out_specs=pl.BlockSpec((STEPS, GROUP, H * LAT), lambda g: (0, group, 0)),
        scratch_shapes=[
            pltpu.VMEM((KEYS, WIDE), jnp.bfloat16),
            pltpu.VMEM((KEYS, WIDE), jnp.bfloat16),
            pltpu.VMEM((KEYS, LAT), jnp.bfloat16),
            pltpu.VMEM((STEPS * GROUP, KEYS), jnp.float32),
            pltpu.VMEM((STEPS, GROUP, WIDE), jnp.float32),
        ],
        input_output_aliases={} if earlier is None else {5: 0},
        compiler_params=pltpu.CompilerParams(vmem_limit_bytes=32 * 2**20),
        cost_estimate=pl.CostEstimate(
            flops=2 * STEPS * GROUP * H * KEYS * (WIDE + LAT),
            bytes_accessed=2 * STEPS * GROUP * H * (KVW + LAT),
            transcendentals=STEPS * GROUP * H * KEYS,
        ),
    )(*operands)


def hop(value, strides, delta):
    pairs = []
    for core, stride in enumerate(strides):
        for chip in range(CHIPS):
            place = chip // stride % SIDE
            there = chip + ((place + delta) % SIDE - place) * stride
            pairs.append((core * CHIPS + chip, core * CHIPS + there))
    return lax.ppermute(value, ("dp", "ep"), pairs)


def chip_at(stride, delta, start):
    place = start // stride % SIDE
    return start + ((place + delta) % SIDE - place) * stride


def pick_matrix(targets_ref, ids):
    hits = [
        jnp.sum((ids == targets_ref[j].astype(jnp.float32)).astype(jnp.float32), axis=0, keepdims=True)
        for j in range(SIDE)
    ]
    before = lax.broadcasted_iota(jnp.int32, (LINE, LINE), 0)
    after = lax.broadcasted_iota(jnp.int32, (LINE, LINE), 1)
    earlier = ((before // SLOTS == after // SLOTS) & (before < after)).astype(jnp.bfloat16)
    stacked = jnp.concatenate(hits + hits, axis=0).astype(jnp.bfloat16)
    ranks = jnp.dot(stacked, earlier, preferred_element_type=jnp.float32)
    base = (lax.broadcasted_iota(jnp.int32, (1, LINE), 1) // SLOTS * CAPE).astype(jnp.float32)
    rows = lax.broadcasted_iota(jnp.int32, (SIDE * PICKS, LINE), 0).astype(jnp.float32)
    picks = []
    for j in range(SIDE):
        place = jnp.where(hits[j] > 0.0, base + ranks[j : j + 1], -1.0)
        picks.append((rows == place).astype(jnp.float32))
    return jnp.concatenate(picks, axis=0).astype(jnp.bfloat16)


def select_kernel(targets_ref, *refs):
    pieces, outs, ids_ref = refs[:SIDE], refs[SIDE : 2 * SIDE], refs[2 * SIDE]
    width = pieces[0].shape[1]
    for line in range(SIDE):
        piece = pieces[line][...]
        ids = piece[:, width - MARK :].astype(jnp.float32).T[:TOPK]
        ids_ref[line] = ids
        picks = pick_matrix(targets_ref, ids)
        rows = jnp.dot(picks, piece, preferred_element_type=jnp.float32).astype(jnp.bfloat16)
        rows = rows.reshape(SIDE, SIDE, PICKS, width)
        for j in range(SIDE):
            outs[j][pl.ds(line * SIDE, SIDE)] = rows[j]


def select(targets, pieces):
    width = pieces[0].shape[1]
    vmem = pl.BlockSpec(memory_space=pltpu.VMEM)
    return pl.pallas_call(
        select_kernel,
        out_shape=[jax.ShapeDtypeStruct((PLANE, PICKS, width), jnp.bfloat16)] * SIDE
        + [jax.ShapeDtypeStruct((SIDE, TOPK, LINE), jnp.float32)],
        in_specs=[pl.BlockSpec(memory_space=pltpu.SMEM)] + [vmem] * SIDE,
        out_specs=[vmem] * (SIDE + 1),
        compiler_params=pltpu.CompilerParams(vmem_limit_bytes=32 * 2**20),
        cost_estimate=pl.CostEstimate(
            flops=2 * SIDE * LINE * LINE * width, bytes_accessed=4 * SIDE * LINE * width, transcendentals=0
        ),
    )(targets, *pieces)


def combine_kernel(targets_ref, ids_ref, *refs):
    width = refs[0].shape[2]
    for line in range(SIDE):
        picks = pick_matrix(targets_ref, ids_ref[line])
        blocks = [ref[pl.ds(line * SIDE, SIDE)] for ref in refs[:SIDE]]
        rows = jnp.concatenate([b.reshape(SIDE * PICKS, width) for b in blocks], axis=0)
        total = lax.dot_general(
            picks, rows, (((0,), (0,)), ((), ())), preferred_element_type=jnp.float32
        )
        refs[SIDE + line][...] = total.astype(jnp.bfloat16)


def combine(targets, ids, blocks):
    width = blocks[0].shape[2]
    vmem = pl.BlockSpec(memory_space=pltpu.VMEM)
    return pl.pallas_call(
        combine_kernel,
        out_shape=[jax.ShapeDtypeStruct((LINE, width), jnp.bfloat16)] * SIDE,
        in_specs=[pl.BlockSpec(memory_space=pltpu.SMEM)] + [vmem] * (1 + SIDE),
        out_specs=[vmem] * SIDE,
        compiler_params=pltpu.CompilerParams(vmem_limit_bytes=32 * 2**20),
        cost_estimate=pl.CostEstimate(
            flops=2 * SIDE * LINE * LINE * width, bytes_accessed=4 * SIDE * LINE * width, transcendentals=0
        ),
    )(targets, ids, *blocks)


def together(*trees):
    return lax.optimization_barrier(trees)


def stage_axes():
    return [[tuple(by_core[n] for by_core in orders) for orders in ORDERS] for n in range(3)]


def exchange(blocks, strides, deltas):
    return [hop(block, strides, delta) for block, delta in zip(blocks, deltas)]


def send_rows(columns, targets, packed_cache):
    first, second, third = stage_axes()
    both = range(len(columns))
    rings = [exchange([columns[i]] * 3, first[i], (1, -1, 2)) for i in both]
    columns, rings = together(columns, rings)
    lines = [jnp.concatenate([columns[i]] + rings[i], axis=0) for i in both]
    rings = [exchange([lines[i]] * 3, second[i], (1, -1, 2)) for i in both]
    packed_cache, rings[1][0] = together(packed_cache, rings[1][0])
    lines, rings = together(lines, rings)
    picked = [select(targets[i], [lines[i]] + rings[i]) for i in both]
    rings = [exchange(picked[i][1:SIDE], third[i], TARGETS[1:]) for i in both]
    return [[picked[i][0]] + rings[i] for i in both], [p[SIDE] for p in picked], packed_cache


def return_rows(outward, targets, ids, contexts):
    first, second, third = stage_axes()
    both = range(len(outward))
    rings = [exchange(outward[i][1:], third[i], (-1, 1, 2)) for i in both]
    context = contexts(None)
    rings, context = together(rings, context)
    lines = [combine(targets[i], ids[i], [outward[i][0]] + rings[i]) for i in both]
    rings = [exchange(lines[i][1:], second[i], (-1, 1, 2)) for i in both]
    context = contexts(context)
    rings, context = together(rings, context)
    sums = []
    for i in both:
        line = add(lines[i][0], *rings[i])
        blocks = [line[k * ROWS : (k + 1) * ROWS] for k in range(SIDE)]
        sums.append([blocks[0]] + exchange(blocks[1:], first[i], (-1, 1, 2)))
    sums, = together(sums)
    return [add(*terms) for terms in sums], context


def add(*terms):
    return sum(t.astype(jnp.float32) for t in terms).astype(jnp.bfloat16)


def half_expert(rows, gate_ref, up_ref):
    gate_pre = jnp.dot(rows, gate_ref[...], preferred_element_type=jnp.float32)
    up_pre = jnp.dot(rows, up_ref[...], preferred_element_type=jnp.float32)
    return (gate_pre * (1.0 / (1.0 + jnp.exp(-gate_pre))) * up_pre).astype(jnp.bfloat16)


def first_half_kernel(order_ref, me_ref, *refs):
    main, minor = refs[:SIDE], refs[SIDE : 2 * SIDE]
    gate_ref, up_ref, down_ref, rows_ref, part_ref, weight_ref = refs[2 * SIDE :]

    def one(group, carry):
        for j in range(SIDE):
            number = j * PLANE + group
            rows_ref[number, :, pl.ds(0, MAIN)] = main[j][group, :, pl.ds(0, MAIN)]
            rows_ref[order_ref[number], :, pl.ds(MAIN, MINOR)] = minor[j][group, :, pl.ds(0, MINOR)]
            mark = main[j][group, :, pl.ds(MAIN, MARK)].astype(jnp.float32)
            total = sum(pltpu.roll(mark, MARK - k * TOPK, 1) for k in range(1, 4))
            lane = lax.broadcasted_iota(jnp.int32, mark.shape, 1)
            mine = (lane < TOPK) & (mark == me_ref[0].astype(jnp.float32))
            total = jnp.sum(jnp.where(mine, total, 0.0), axis=1, keepdims=True)
            weight_ref[number] = jnp.broadcast_to(total, mark.shape)
        return carry

    lax.fori_loop(0, PLANE, one, 0)

    def block(index, carry):
        at = pl.ds(index * BLOCK, BLOCK)
        rows = rows_ref[at].reshape(BLOCK * PICKS, D)
        inner = half_expert(rows, gate_ref, up_ref)
        for start in range(0, D, LAT):
            part = jnp.dot(inner, down_ref[:, start : start + LAT], preferred_element_type=jnp.float32)
            part_ref[at, :, pl.ds(start, LAT)] = part.astype(jnp.bfloat16).reshape(BLOCK, PICKS, LAT)
        return carry

    lax.fori_loop(0, CHIPS // BLOCK, block, 0)


def second_half_kernel(order_ref, rows_ref, part_ref, weight_ref, gate_ref, up_ref, down_ref, *refs):
    main, minor, out_ref = refs[:SIDE], refs[SIDE : 2 * SIDE], refs[2 * SIDE]

    def block(index, carry):
        at = pl.ds(index * BLOCK, BLOCK)
        rows = rows_ref[at].reshape(BLOCK * PICKS, D)
        inner = half_expert(rows, gate_ref, up_ref)
        weight = weight_ref[at].reshape(BLOCK * PICKS, MARK)
        weight = jnp.concatenate([weight] * (LAT // MARK), axis=1)
        for start in range(0, D, LAT):
            part = jnp.dot(inner, down_ref[:, start : start + LAT], preferred_element_type=jnp.float32)
            earlier = part_ref[at, :, pl.ds(start, LAT)].reshape(BLOCK * PICKS, LAT)
            total = (earlier.astype(jnp.float32) + part) * weight
            out_ref[at, :, pl.ds(start, LAT)] = total.astype(jnp.bfloat16).reshape(BLOCK, PICKS, LAT)
        return carry

    lax.fori_loop(0, CHIPS // BLOCK, block, 0)

    def one(group, carry):
        for j in range(SIDE):
            number = j * PLANE + group
            main[j][group] = out_ref[number, :, pl.ds(0, MAIN)]
            minor[j][group] = out_ref[order_ref[number], :, pl.ds(MAIN, MINOR)]
        return carry

    lax.fori_loop(0, PLANE, one, 0)


HALF_COST = pl.CostEstimate(
    flops=2 * CHIPS * PICKS * D * 512 * 3, bytes_accessed=2 * (3 * D * 512 + 3 * CHIPS * PICKS * D), transcendentals=CHIPS * PICKS * 512
)


def first_half(order, me, main, minor, matrices):
    vmem, smem = pl.BlockSpec(memory_space=pltpu.VMEM), pl.BlockSpec(memory_space=pltpu.SMEM)
    whole = jax.ShapeDtypeStruct((CHIPS, PICKS, D), jnp.bfloat16)
    return pl.pallas_call(
        first_half_kernel,
        out_shape=[whole, whole, jax.ShapeDtypeStruct((CHIPS, PICKS, MARK), jnp.float32)],
        in_specs=[smem, smem] + [vmem] * (2 * SIDE + 3),
        out_specs=[vmem] * 3,
        compiler_params=pltpu.CompilerParams(vmem_limit_bytes=52 * 2**20),
        cost_estimate=HALF_COST,
    )(order, me[None], *main, *minor, *matrices)


def second_half(order, rows, part, weight, matrices):
    vmem, smem = pl.BlockSpec(memory_space=pltpu.VMEM), pl.BlockSpec(memory_space=pltpu.SMEM)
    shapes = [(PLANE, PICKS, width) for width in (MAIN, MINOR) for _ in range(SIDE)]
    outs = pl.pallas_call(
        second_half_kernel,
        out_shape=[jax.ShapeDtypeStruct(shape, jnp.bfloat16) for shape in shapes],
        in_specs=[smem] + [vmem] * 6,
        out_specs=[vmem] * (2 * SIDE),
        scratch_shapes=[pltpu.VMEM((CHIPS, PICKS, D), jnp.bfloat16)],
        compiler_params=pltpu.CompilerParams(vmem_limit_bytes=52 * 2**20),
        cost_estimate=HALF_COST,
    )(order, rows, part, weight, *matrices)
    return outs[:SIDE], outs[SIDE:]


def three_parts(weights):
    high = lax.reduce_precision(weights, 8, 7)
    rest = weights - high
    mid = lax.reduce_precision(rest, 8, 7)
    return [part.astype(jnp.bfloat16) for part in (high, mid, rest - mid)]


def pack_kernel(from_ref, slot_ref, len_ref, cache_ref, out_ref):
    row = lax.broadcasted_iota(jnp.int32, (HALF, 128), 0)
    lane = lax.broadcasted_iota(jnp.int32, (HALF, 128), 1)

    def one(chip, carry):
        block = cache_ref[from_ref[chip]]
        out_ref[chip] = block
        mark = jnp.where(lane == 0, slot_ref[chip], len_ref[chip]).astype(jnp.float32)
        head = jnp.where((row == HALF - 1) & (lane < 2), mark, block[:, :128].astype(jnp.float32))
        out_ref[chip, :, pl.ds(0, 128)] = head.astype(jnp.bfloat16)
        return carry

    lax.fori_loop(0, out_ref.shape[0], one, 0)


def pack_cache(send_from, sent_slot, sent_len, cache):
    chips = send_from.shape[0]
    small = pl.BlockSpec(memory_space=pltpu.SMEM)
    return pl.pallas_call(
        pack_kernel,
        out_shape=jax.ShapeDtypeStruct((chips,) + cache.shape[1:], jnp.bfloat16),
        in_specs=[small, small, small, pl.BlockSpec(memory_space=pltpu.VMEM)],
        out_specs=pl.BlockSpec(memory_space=pltpu.VMEM),
        compiler_params=pltpu.CompilerParams(vmem_limit_bytes=24 * 2**20),
        cost_estimate=pl.CostEstimate(
            flops=0, bytes_accessed=2 * (chips + cache.shape[0]) * CTX * KVW, transcendentals=0
        ),
    )(send_from, sent_slot, sent_len, cache)


def on_device(
    kv_cache,
    lengths,
    move_list,
    queries,
    new_kv,
    hidden,
    expert_ids,
    gate_weights,
    expert_gate,
    expert_up,
    expert_down,
):
    ep_count = lax.axis_size("ep")
    slot_count = lengths.shape[0]
    own = (expert_gate[0], expert_up[0], expert_down[0])
    expert_range = jnp.arange(ep_count, dtype=jnp.int32)
    me = lax.axis_index("ep")
    core = lax.axis_index("dp")

    marks = [expert_ids.astype(jnp.bfloat16)] + three_parts(gate_weights)
    marks = jnp.concatenate(marks, axis=2).reshape(ROWS, 4 * TOPK)
    marks = jnp.pad(marks, ((0, 0), (0, MARK - 4 * TOPK)))
    rows = hidden.reshape(ROWS, D)
    columns = [
        jnp.concatenate([block, marks], axis=1) for block in (rows[:, :MAIN], rows[:, MAIN:])
    ]
    targets = []
    for orders in ORDERS:
        stride = jnp.where(core == 0, orders[0][2], orders[1][2])
        targets.append(
            jnp.stack([chip_at(stride, delta, me) for delta in TARGETS]).astype(jnp.int32)
        )
    slot_range = jnp.arange(slot_count, dtype=jnp.int32)
    send_hit = expert_range[:, None] == move_list[:, 0][None, :]
    send_from = jnp.sum(jnp.where(send_hit, slot_range[None, :], 0), axis=1)
    sent_slot = jnp.sum(jnp.where(send_hit, move_list[:, 1][None, :] + 1, 0), axis=1) - 1
    sent_len = jnp.sum(jnp.where(send_hit, lengths[None, :], 0), axis=1)
    packed_cache = pack_cache(
        send_from, sent_slot, sent_len, kv_cache.reshape(slot_count, HALF, 2 * KVW)
    )
    arrived, ids, packed_cache = send_rows(columns, targets, packed_cache)
    got = lax.all_to_all(packed_cache, "ep", split_axis=0, concat_axis=0, tiled=True)
    arrived, own = together(arrived, own)
    other = tuple(lax.ppermute(w, "dp", [(0, 1), (1, 0)]) for w in own)

    tables = []
    for main, minor in zip(*ORDERS):
        table = [0] * CHIPS
        for number in range(CHIPS):
            digits = (number // PLANE, number // SIDE % SIDE, number % SIDE)
            place = dict(zip(main, digits[::-1]))
            index = place[minor[2]] * PLANE + place[minor[1]] * SIDE + place[minor[0]]
            table[index] = number
        tables.append(jnp.array(table, jnp.int32))
    order = jnp.where(core == 0, tables[0], tables[1])
    rows, part, weight = first_half(order, me, arrived[0], arrived[1], own)
    outward = second_half(order, rows, part, weight, other)
    outward, got = lax.optimization_barrier((outward, got))
    got_mark = lax.optimization_barrier(got[:, HALF - 1, :128]).astype(jnp.int32)
    got_slot, got_len = got_mark[:, 0], got_mark[:, 1]
    land_hit = got_slot[None, :] == slot_range[:, None]
    landing = jnp.sum(jnp.where(land_hit, expert_range[None, :], 0), axis=1)
    placed_len = jnp.sum(jnp.where(land_hit, got_len[None, :], 0), axis=1)

    def contexts(earlier):
        return attend(queries, new_kv, got, landing, placed_len, earlier)

    sums, context = return_rows(outward, targets, ids, contexts)
    mixture = jnp.concatenate(sums, axis=1).reshape(STEPS, SLOTS, D)
    return context, mixture


def solution(mesh):
    return jax.shard_map(
        on_device,
        mesh=mesh,
        in_specs=(
            P(("dp", "ep"), None),
            P(("dp", "ep")),
            P(("dp", "ep"), None),
            P(None, ("dp", "ep"), None),
            P(None, ("dp", "ep"), None),
            P(None, ("dp", "ep"), None),
            P(None, ("dp", "ep"), None),
            P(None, ("dp", "ep"), None),
            P("ep", None, "dp"),
            P("ep", None, "dp"),
            P("ep", "dp", None),
        ),
        out_specs=(P(None, ("dp", "ep"), None), P(None, ("dp", "ep"), None)),
        check_vma=False,
    )
```

```python
import jax
import jax.numpy as jnp
from jax import lax
from jax.experimental import pallas as pl
from jax.experimental.pallas import tpu as pltpu
from jax.sharding import PartitionSpec as P

D = 3584
H = 64
LAT = 512
TOPK = 8
STEPS = 2
CTX = 64
KVW = 576
LIVE = CTX - STEPS
HALF = CTX // 2
GROUP = 16
TOGETHER = 8
WIDE = 640
SIDE = 4
Z, Y, X = SIDE * SIDE, SIDE, 1
MAIN = 2432
MINOR = D - MAIN
MARK = 128
SLOTS = 32
CAPE = 8
ROWS = STEPS * SLOTS
PICKS = STEPS * CAPE
LINE = SIDE * ROWS
PLANE = SIDE * SIDE
CHIPS = SIDE**3
BLOCK = 32
ORDERS = (((Z, Y, X), (Y, X, Z)), ((X, Z, Y), (X, Z, Y)))
TARGETS = (0, 1, -1, 2)
KEYS = GROUP * CTX


score_scale = 192.0 ** (-0.5)
base_two_scale = score_scale * 1.4426950408889634


def attend_kernel(
    landing_ref, got_ref, len_ref, new_ref, query_ref, out_ref,
    even_ref, odd_ref, value_ref, bias_ref, recent_ref,
):
    pairs = GROUP * HALF
    lane = lax.broadcasted_iota(jnp.int32, (HALF, WIDE), 1)
    last = lax.broadcasted_iota(jnp.int32, (HALF, WIDE), 0) == HALF - 1
    for step in range(STEPS):
        rows = new_ref[step].astype(jnp.float32)
        recent_ref[step] = jnp.concatenate(
            [rows, jnp.zeros((GROUP, WIDE - KVW), jnp.float32)], axis=1
        )

    def place(keys, at):
        even_ref[pl.ds(at, HALF), :] = keys.astype(jnp.bfloat16)
        odd_ref[pl.ds(at, HALF), :] = pltpu.roll(keys, WIDE - KVW, 1).astype(jnp.bfloat16)
        value_ref[pl.ds(at, HALF), :] = keys[:, :LAT].astype(jnp.bfloat16)

    def one(slot, carry):
        block = got_ref[landing_ref[slot]]
        first = jnp.where(lane < KVW, block[:, :WIDE].astype(jnp.float32), 0.0)
        first = jnp.where(last, recent_ref[0, pl.ds(slot, 1), :], first)
        at = pl.multiple_of(slot * HALF, HALF)
        place(first, at)
        second = block[:, LAT:].astype(jnp.float32)
        second = pltpu.roll(jnp.where(lane < WIDE - KVW, 0.0, second), KVW, 1)
        second = jnp.where(last, recent_ref[1, pl.ds(slot, 1), :], second)
        place(second, pl.multiple_of(pairs + at, HALF))
        return carry

    lax.fori_loop(0, GROUP, one, 0)

    column = lax.broadcasted_iota(jnp.int32, (GROUP, KEYS), 1)
    row = lax.broadcasted_iota(jnp.int32, (GROUP, KEYS), 0)
    half = (column >= pairs).astype(jnp.int32)
    within = column - half * pairs
    position = 2 * (within % HALF) + half
    cached = position < len_ref[...]
    for step in range(STEPS):
        recent = (position >= LIVE) & (position <= LIVE + step)
        allowed = (cached | recent) & (within // HALF == row)
        bias_ref[pl.ds(step * GROUP, GROUP), :] = jnp.where(allowed, 0.0, -jnp.inf)

    def heads(index, carry):
        bias = jnp.concatenate([bias_ref[...]] * TOGETHER, axis=0)
        for odd in range(2):
            slabs = []
            for k in range(TOGETHER):
                start = pl.multiple_of((index * TOGETHER + k) * 2 * KVW + odd * LAT, 128)
                for step in range(STEPS):
                    slabs.append(query_ref[step, :, pl.ds(start, WIDE)])
            keys = odd_ref[...] if odd else even_ref[...]
            score = lax.dot_general(
                jnp.concatenate(slabs, axis=0),
                keys,
                (((1,), (1,)), ((), ())),
                preferred_element_type=jnp.float32,
            )
            score = score + bias
            weight = jnp.exp2((score - jnp.max(score, axis=1, keepdims=True)) * base_two_scale)
            total = jnp.sum(weight, axis=1, keepdims=True)
            mixed = jnp.dot(
                weight.astype(jnp.bfloat16), value_ref[...], preferred_element_type=jnp.float32
            )
            mixed = (mixed * (1.0 / total)).astype(jnp.bfloat16)
            for k in range(TOGETHER):
                start = pl.multiple_of(((index * TOGETHER + k) * 2 + odd) * LAT, LAT)
                for step in range(STEPS):
                    at = (k * STEPS + step) * GROUP
                    out_ref[step, :, pl.ds(start, LAT)] = mixed[at : at + GROUP]
        return carry

    lax.fori_loop(0, H // (2 * TOGETHER), heads, 0)


def attend(queries, new_kv, got, landing, placed_len, earlier):
    slots = queries.shape[1]
    group = 0 if earlier is None else 1
    specs = [
        pl.BlockSpec(memory_space=pltpu.SMEM),
        pl.BlockSpec(memory_space=pltpu.VMEM),
        pl.BlockSpec((GROUP, 1), lambda g: (group, 0)),
        pl.BlockSpec((STEPS, GROUP, KVW), lambda g: (0, group, 0)),
        pl.BlockSpec((STEPS, GROUP, H * KVW), lambda g: (0, group, 0)),
    ]
    operands = [landing[group * GROUP :][:GROUP], got, placed_len[:, None], new_kv, queries]
    kernel = attend_kernel
    if earlier is not None:
        specs.append(pl.BlockSpec(memory_space=pl.ANY))
        operands.append(earlier)

        def kernel(*refs):
            attend_kernel(*refs[:5], *refs[6:])

    return pl.pallas_call(
        kernel,
        grid=(1,),
        out_shape=jax.ShapeDtypeStruct((STEPS, slots, H * LAT), jnp.bfloat16),
        in_specs=specs,
        out_specs=pl.BlockSpec((STEPS, GROUP, H * LAT), lambda g: (0, group, 0)),
        scratch_shapes=[
            pltpu.VMEM((KEYS, WIDE), jnp.bfloat16),
            pltpu.VMEM((KEYS, WIDE), jnp.bfloat16),
            pltpu.VMEM((KEYS, LAT), jnp.bfloat16),
            pltpu.VMEM((STEPS * GROUP, KEYS), jnp.float32),
            pltpu.VMEM((STEPS, GROUP, WIDE), jnp.float32),
        ],
        input_output_aliases={} if earlier is None else {5: 0},
        compiler_params=pltpu.CompilerParams(vmem_limit_bytes=32 * 2**20),
        cost_estimate=pl.CostEstimate(
            flops=2 * STEPS * GROUP * H * KEYS * (WIDE + LAT),
            bytes_accessed=2 * STEPS * GROUP * H * (KVW + LAT),
            transcendentals=STEPS * GROUP * H * KEYS,
        ),
    )(*operands)


def hop(value, strides, delta):
    pairs = []
    for core, stride in enumerate(strides):
        for chip in range(CHIPS):
            place = chip // stride % SIDE
            there = chip + ((place + delta) % SIDE - place) * stride
            pairs.append((core * CHIPS + chip, core * CHIPS + there))
    return lax.ppermute(value, ("dp", "ep"), pairs)


def chip_at(stride, delta, start):
    place = start // stride % SIDE
    return start + ((place + delta) % SIDE - place) * stride


def pick_matrix(targets_ref, ids):
    hits = [
        jnp.sum((ids == targets_ref[j].astype(jnp.float32)).astype(jnp.float32), axis=0, keepdims=True)
        for j in range(SIDE)
    ]
    before = lax.broadcasted_iota(jnp.int32, (LINE, LINE), 0)
    after = lax.broadcasted_iota(jnp.int32, (LINE, LINE), 1)
    earlier = ((before // SLOTS == after // SLOTS) & (before < after)).astype(jnp.bfloat16)
    stacked = jnp.concatenate(hits + hits, axis=0).astype(jnp.bfloat16)
    ranks = jnp.dot(stacked, earlier, preferred_element_type=jnp.float32)
    base = (lax.broadcasted_iota(jnp.int32, (1, LINE), 1) // SLOTS * CAPE).astype(jnp.float32)
    rows = lax.broadcasted_iota(jnp.int32, (SIDE * PICKS, LINE), 0).astype(jnp.float32)
    picks = []
    for j in range(SIDE):
        place = jnp.where(hits[j] > 0.0, base + ranks[j : j + 1], -1.0)
        picks.append((rows == place).astype(jnp.float32))
    return jnp.concatenate(picks, axis=0).astype(jnp.bfloat16)


def select_kernel(targets_ref, *refs):
    pieces, outs, ids_ref = refs[:SIDE], refs[SIDE : 2 * SIDE], refs[2 * SIDE]
    width = pieces[0].shape[1]
    for line in range(SIDE):
        piece = pieces[line][...]
        ids = piece[:, width - MARK :].astype(jnp.float32).T[:TOPK]
        ids_ref[line] = ids
        picks = pick_matrix(targets_ref, ids)
        rows = jnp.dot(picks, piece, preferred_element_type=jnp.float32).astype(jnp.bfloat16)
        rows = rows.reshape(SIDE, SIDE, PICKS, width)
        for j in range(SIDE):
            outs[j][pl.ds(line * SIDE, SIDE)] = rows[j]


def select(targets, pieces):
    width = pieces[0].shape[1]
    vmem = pl.BlockSpec(memory_space=pltpu.VMEM)
    return pl.pallas_call(
        select_kernel,
        out_shape=[jax.ShapeDtypeStruct((PLANE, PICKS, width), jnp.bfloat16)] * SIDE
        + [jax.ShapeDtypeStruct((SIDE, TOPK, LINE), jnp.float32)],
        in_specs=[pl.BlockSpec(memory_space=pltpu.SMEM)] + [vmem] * SIDE,
        out_specs=[vmem] * (SIDE + 1),
        compiler_params=pltpu.CompilerParams(vmem_limit_bytes=32 * 2**20),
        cost_estimate=pl.CostEstimate(
            flops=2 * SIDE * LINE * LINE * width, bytes_accessed=4 * SIDE * LINE * width, transcendentals=0
        ),
    )(targets, *pieces)


def combine_kernel(targets_ref, ids_ref, *refs):
    width = refs[0].shape[2]
    for line in range(SIDE):
        picks = pick_matrix(targets_ref, ids_ref[line])
        blocks = [ref[pl.ds(line * SIDE, SIDE)] for ref in refs[:SIDE]]
        rows = jnp.concatenate([b.reshape(SIDE * PICKS, width) for b in blocks], axis=0)
        total = lax.dot_general(
            picks, rows, (((0,), (0,)), ((), ())), preferred_element_type=jnp.float32
        )
        refs[SIDE + line][...] = total.astype(jnp.bfloat16)


def combine(targets, ids, blocks):
    width = blocks[0].shape[2]
    vmem = pl.BlockSpec(memory_space=pltpu.VMEM)
    return pl.pallas_call(
        combine_kernel,
        out_shape=[jax.ShapeDtypeStruct((LINE, width), jnp.bfloat16)] * SIDE,
        in_specs=[pl.BlockSpec(memory_space=pltpu.SMEM)] + [vmem] * (1 + SIDE),
        out_specs=[vmem] * SIDE,
        compiler_params=pltpu.CompilerParams(vmem_limit_bytes=32 * 2**20),
        cost_estimate=pl.CostEstimate(
            flops=2 * SIDE * LINE * LINE * width, bytes_accessed=4 * SIDE * LINE * width, transcendentals=0
        ),
    )(targets, ids, *blocks)


def together(*trees):
    return lax.optimization_barrier(trees)


def stage_axes():
    return [[tuple(by_core[n] for by_core in orders) for orders in ORDERS] for n in range(3)]


def exchange(blocks, strides, deltas):
    return [hop(block, strides, delta) for block, delta in zip(blocks, deltas)]


def send_rows(columns, targets, packed_cache):
    first, second, third = stage_axes()
    both = range(len(columns))
    rings = [exchange([columns[i]] * 3, first[i], (1, -1, 2)) for i in both]
    columns, rings = together(columns, rings)
    lines = [jnp.concatenate([columns[i]] + rings[i], axis=0) for i in both]
    rings = [exchange([lines[i]] * 3, second[i], (1, -1, 2)) for i in both]
    lines, rings = together(lines, rings)
    picked = [select(targets[i], [lines[i]] + rings[i]) for i in both]
    rings = [exchange(picked[i][1:SIDE], third[i], TARGETS[1:]) for i in both]
    packed_cache, rings[1][0] = together(packed_cache, rings[1][0])
    return [[picked[i][0]] + rings[i] for i in both], [p[SIDE] for p in picked], packed_cache


def return_rows(outward, targets, ids, contexts):
    first, second, third = stage_axes()
    both = range(len(outward))
    rings = [exchange(outward[i][1:], third[i], (-1, 1, 2)) for i in both]
    context = contexts(None)
    rings, context = together(rings, context)
    lines = [combine(targets[i], ids[i], [outward[i][0]] + rings[i]) for i in both]
    rings = [exchange(lines[i][1:], second[i], (-1, 1, 2)) for i in both]
    context = contexts(context)
    rings, context = together(rings, context)
    sums = []
    for i in both:
        line = add(lines[i][0], *rings[i])
        blocks = [line[k * ROWS : (k + 1) * ROWS] for k in range(SIDE)]
        sums.append([blocks[0]] + exchange(blocks[1:], first[i], (-1, 1, 2)))
    sums, = together(sums)
    return [add(*terms) for terms in sums], context


def add(*terms):
    return sum(t.astype(jnp.float32) for t in terms).astype(jnp.bfloat16)


def half_expert(rows, gate_ref, up_ref):
    gate_pre = jnp.dot(rows, gate_ref[...], preferred_element_type=jnp.float32)
    up_pre = jnp.dot(rows, up_ref[...], preferred_element_type=jnp.float32)
    return (gate_pre * (1.0 / (1.0 + jnp.exp(-gate_pre))) * up_pre).astype(jnp.bfloat16)


def first_half_kernel(order_ref, me_ref, *refs):
    main, minor = refs[:SIDE], refs[SIDE : 2 * SIDE]
    gate_ref, up_ref, down_ref, rows_ref, part_ref, weight_ref = refs[2 * SIDE :]

    def one(group, carry):
        for j in range(SIDE):
            number = j * PLANE + group
            rows_ref[number, :, pl.ds(0, MAIN)] = main[j][group, :, pl.ds(0, MAIN)]
            rows_ref[order_ref[number], :, pl.ds(MAIN, MINOR)] = minor[j][group, :, pl.ds(0, MINOR)]
            mark = main[j][group, :, pl.ds(MAIN, MARK)].astype(jnp.float32)
            total = sum(pltpu.roll(mark, MARK - k * TOPK, 1) for k in range(1, 4))
            lane = lax.broadcasted_iota(jnp.int32, mark.shape, 1)
            mine = (lane < TOPK) & (mark == me_ref[0].astype(jnp.float32))
            total = jnp.sum(jnp.where(mine, total, 0.0), axis=1, keepdims=True)
            weight_ref[number] = jnp.broadcast_to(total, mark.shape)
        return carry

    lax.fori_loop(0, PLANE, one, 0)

    def block(index, carry):
        at = pl.ds(index * BLOCK, BLOCK)
        rows = rows_ref[at].reshape(BLOCK * PICKS, D)
        inner = half_expert(rows, gate_ref, up_ref)
        for start in range(0, D, LAT):
            part = jnp.dot(inner, down_ref[:, start : start + LAT], preferred_element_type=jnp.float32)
            part_ref[at, :, pl.ds(start, LAT)] = part.astype(jnp.bfloat16).reshape(BLOCK, PICKS, LAT)
        return carry

    lax.fori_loop(0, CHIPS // BLOCK, block, 0)


def second_half_kernel(order_ref, rows_ref, part_ref, weight_ref, gate_ref, up_ref, down_ref, *refs):
    main, minor, out_ref = refs[:SIDE], refs[SIDE : 2 * SIDE], refs[2 * SIDE]

    def block(index, carry):
        at = pl.ds(index * BLOCK, BLOCK)
        rows = rows_ref[at].reshape(BLOCK * PICKS, D)
        inner = half_expert(rows, gate_ref, up_ref)
        weight = weight_ref[at].reshape(BLOCK * PICKS, MARK)
        weight = jnp.concatenate([weight] * (LAT // MARK), axis=1)
        for start in range(0, D, LAT):
            part = jnp.dot(inner, down_ref[:, start : start + LAT], preferred_element_type=jnp.float32)
            earlier = part_ref[at, :, pl.ds(start, LAT)].reshape(BLOCK * PICKS, LAT)
            total = (earlier.astype(jnp.float32) + part) * weight
            out_ref[at, :, pl.ds(start, LAT)] = total.astype(jnp.bfloat16).reshape(BLOCK, PICKS, LAT)
        return carry

    lax.fori_loop(0, CHIPS // BLOCK, block, 0)

    def one(group, carry):
        for j in range(SIDE):
            number = j * PLANE + group
            main[j][group] = out_ref[number, :, pl.ds(0, MAIN)]
            minor[j][group] = out_ref[order_ref[number], :, pl.ds(MAIN, MINOR)]
        return carry

    lax.fori_loop(0, PLANE, one, 0)


HALF_COST = pl.CostEstimate(
    flops=2 * CHIPS * PICKS * D * 512 * 3, bytes_accessed=2 * (3 * D * 512 + 3 * CHIPS * PICKS * D), transcendentals=CHIPS * PICKS * 512
)


def first_half(order, me, main, minor, matrices):
    vmem, smem = pl.BlockSpec(memory_space=pltpu.VMEM), pl.BlockSpec(memory_space=pltpu.SMEM)
    whole = jax.ShapeDtypeStruct((CHIPS, PICKS, D), jnp.bfloat16)
    return pl.pallas_call(
        first_half_kernel,
        out_shape=[whole, whole, jax.ShapeDtypeStruct((CHIPS, PICKS, MARK), jnp.float32)],
        in_specs=[smem, smem] + [vmem] * (2 * SIDE + 3),
        out_specs=[vmem] * 3,
        compiler_params=pltpu.CompilerParams(vmem_limit_bytes=52 * 2**20),
        cost_estimate=HALF_COST,
    )(order, me[None], *main, *minor, *matrices)


def second_half(order, rows, part, weight, matrices):
    vmem, smem = pl.BlockSpec(memory_space=pltpu.VMEM), pl.BlockSpec(memory_space=pltpu.SMEM)
    shapes = [(PLANE, PICKS, width) for width in (MAIN, MINOR) for _ in range(SIDE)]
    outs = pl.pallas_call(
        second_half_kernel,
        out_shape=[jax.ShapeDtypeStruct(shape, jnp.bfloat16) for shape in shapes],
        in_specs=[smem] + [vmem] * 6,
        out_specs=[vmem] * (2 * SIDE),
        scratch_shapes=[pltpu.VMEM((CHIPS, PICKS, D), jnp.bfloat16)],
        compiler_params=pltpu.CompilerParams(vmem_limit_bytes=52 * 2**20),
        cost_estimate=HALF_COST,
    )(order, rows, part, weight, *matrices)
    return outs[:SIDE], outs[SIDE:]


def three_parts(weights):
    high = lax.reduce_precision(weights, 8, 7)
    rest = weights - high
    mid = lax.reduce_precision(rest, 8, 7)
    return [part.astype(jnp.bfloat16) for part in (high, mid, rest - mid)]


def pack_kernel(from_ref, slot_ref, len_ref, cache_ref, out_ref):
    row = lax.broadcasted_iota(jnp.int32, (HALF, 128), 0)
    lane = lax.broadcasted_iota(jnp.int32, (HALF, 128), 1)

    def one(chip, carry):
        block = cache_ref[from_ref[chip]]
        out_ref[chip] = block
        mark = jnp.where(lane == 0, slot_ref[chip], len_ref[chip]).astype(jnp.float32)
        head = jnp.where((row == HALF - 1) & (lane < 2), mark, block[:, :128].astype(jnp.float32))
        out_ref[chip, :, pl.ds(0, 128)] = head.astype(jnp.bfloat16)
        return carry

    lax.fori_loop(0, out_ref.shape[0], one, 0)


def pack_cache(send_from, sent_slot, sent_len, cache):
    chips = send_from.shape[0]
    small = pl.BlockSpec(memory_space=pltpu.SMEM)
    return pl.pallas_call(
        pack_kernel,
        out_shape=jax.ShapeDtypeStruct((chips,) + cache.shape[1:], jnp.bfloat16),
        in_specs=[small, small, small, pl.BlockSpec(memory_space=pltpu.VMEM)],
        out_specs=pl.BlockSpec(memory_space=pltpu.VMEM),
        compiler_params=pltpu.CompilerParams(vmem_limit_bytes=24 * 2**20),
        cost_estimate=pl.CostEstimate(
            flops=0, bytes_accessed=2 * (chips + cache.shape[0]) * CTX * KVW, transcendentals=0
        ),
    )(send_from, sent_slot, sent_len, cache)


def on_device(
    kv_cache,
    lengths,
    move_list,
    queries,
    new_kv,
    hidden,
    expert_ids,
    gate_weights,
    expert_gate,
    expert_up,
    expert_down,
):
    ep_count = lax.axis_size("ep")
    slot_count = lengths.shape[0]
    own = (expert_gate[0], expert_up[0], expert_down[0])
    expert_range = jnp.arange(ep_count, dtype=jnp.int32)
    me = lax.axis_index("ep")
    core = lax.axis_index("dp")

    marks = [expert_ids.astype(jnp.bfloat16)] + three_parts(gate_weights)
    marks = jnp.concatenate(marks, axis=2).reshape(ROWS, 4 * TOPK)
    marks = jnp.pad(marks, ((0, 0), (0, MARK - 4 * TOPK)))
    rows = hidden.reshape(ROWS, D)
    columns = [
        jnp.concatenate([block, marks], axis=1) for block in (rows[:, :MAIN], rows[:, MAIN:])
    ]
    targets = []
    for orders in ORDERS:
        stride = jnp.where(core == 0, orders[0][2], orders[1][2])
        targets.append(
            jnp.stack([chip_at(stride, delta, me) for delta in TARGETS]).astype(jnp.int32)
        )
    slot_range = jnp.arange(slot_count, dtype=jnp.int32)
    send_hit = expert_range[:, None] == move_list[:, 0][None, :]
    send_from = jnp.sum(jnp.where(send_hit, slot_range[None, :], 0), axis=1)
    sent_slot = jnp.sum(jnp.where(send_hit, move_list[:, 1][None, :] + 1, 0), axis=1) - 1
    sent_len = jnp.sum(jnp.where(send_hit, lengths[None, :], 0), axis=1)
    packed_cache = pack_cache(
        send_from, sent_slot, sent_len, kv_cache.reshape(slot_count, HALF, 2 * KVW)
    )
    arrived, ids, packed_cache = send_rows(columns, targets, packed_cache)
    got = lax.all_to_all(packed_cache, "ep", split_axis=0, concat_axis=0, tiled=True)
    arrived, own = together(arrived, own)
    other = tuple(lax.ppermute(w, "dp", [(0, 1), (1, 0)]) for w in own)

    tables = []
    for main, minor in zip(*ORDERS):
        table = [0] * CHIPS
        for number in range(CHIPS):
            digits = (number // PLANE, number // SIDE % SIDE, number % SIDE)
            place = dict(zip(main, digits[::-1]))
            index = place[minor[2]] * PLANE + place[minor[1]] * SIDE + place[minor[0]]
            table[index] = number
        tables.append(jnp.array(table, jnp.int32))
    order = jnp.where(core == 0, tables[0], tables[1])
    rows, part, weight = first_half(order, me, arrived[0], arrived[1], own)
    outward = second_half(order, rows, part, weight, other)
    outward, got = lax.optimization_barrier((outward, got))
    got_mark = lax.optimization_barrier(got[:, HALF - 1, :128]).astype(jnp.int32)
    got_slot, got_len = got_mark[:, 0], got_mark[:, 1]
    land_hit = got_slot[None, :] == slot_range[:, None]
    landing = jnp.sum(jnp.where(land_hit, expert_range[None, :], 0), axis=1)
    placed_len = jnp.sum(jnp.where(land_hit, got_len[None, :], 0), axis=1)

    def contexts(earlier):
        return attend(queries, new_kv, got, landing, placed_len, earlier)

    sums, context = return_rows(outward, targets, ids, contexts)
    mixture = jnp.concatenate(sums, axis=1).reshape(STEPS, SLOTS, D)
    return context, mixture


def solution(mesh):
    return jax.shard_map(
        on_device,
        mesh=mesh,
        in_specs=(
            P(("dp", "ep"), None),
            P(("dp", "ep")),
            P(("dp", "ep"), None),
            P(None, ("dp", "ep"), None),
            P(None, ("dp", "ep"), None),
            P(None, ("dp", "ep"), None),
            P(None, ("dp", "ep"), None),
            P(None, ("dp", "ep"), None),
            P("ep", None, "dp"),
            P("ep", None, "dp"),
            P("ep", "dp", None),
        ),
        out_specs=(P(None, ("dp", "ep"), None), P(None, ("dp", "ep"), None)),
        check_vma=False,
    )
```

```python
import jax
import jax.numpy as jnp
from jax import lax
from jax.experimental import pallas as pl
from jax.experimental.pallas import tpu as pltpu
from jax.sharding import PartitionSpec as P

D = 3584
H = 64
LAT = 512
TOPK = 8
STEPS = 2
CTX = 64
KVW = 576
LIVE = CTX - STEPS
HALF = CTX // 2
GROUP = 16
TOGETHER = 8
WIDE = 640
SIDE = 4
Z, Y, X = SIDE * SIDE, SIDE, 1
MAIN = 2432
MINOR = D - MAIN
MARK = 128
SLOTS = 32
CAPE = 8
ROWS = STEPS * SLOTS
PICKS = STEPS * CAPE
LINE = SIDE * ROWS
PLANE = SIDE * SIDE
CHIPS = SIDE**3
BLOCK = 32
ORDERS = (((Z, Y, X), (Y, X, Z)), ((X, Z, Y), (X, Z, Y)))
TARGETS = (0, 1, -1, 2)
KEYS = GROUP * CTX


score_scale = 192.0 ** (-0.5)
base_two_scale = score_scale * 1.4426950408889634


def attend_kernel(
    landing_ref, got_ref, len_ref, new_ref, query_ref, out_ref,
    even_ref, odd_ref, value_ref, bias_ref, recent_ref,
):
    pairs = GROUP * HALF
    lane = lax.broadcasted_iota(jnp.int32, (HALF, WIDE), 1)
    last = lax.broadcasted_iota(jnp.int32, (HALF, WIDE), 0) == HALF - 1
    for step in range(STEPS):
        rows = new_ref[step].astype(jnp.float32)
        recent_ref[step] = jnp.concatenate(
            [rows, jnp.zeros((GROUP, WIDE - KVW), jnp.float32)], axis=1
        )

    def place(keys, at):
        even_ref[pl.ds(at, HALF), :] = keys.astype(jnp.bfloat16)
        odd_ref[pl.ds(at, HALF), :] = pltpu.roll(keys, WIDE - KVW, 1).astype(jnp.bfloat16)
        value_ref[pl.ds(at, HALF), :] = keys[:, :LAT].astype(jnp.bfloat16)

    def one(slot, carry):
        block = got_ref[landing_ref[slot]]
        first = jnp.where(lane < KVW, block[:, :WIDE].astype(jnp.float32), 0.0)
        first = jnp.where(last, recent_ref[0, pl.ds(slot, 1), :], first)
        at = pl.multiple_of(slot * HALF, HALF)
        place(first, at)
        second = block[:, LAT:].astype(jnp.float32)
        second = pltpu.roll(jnp.where(lane < WIDE - KVW, 0.0, second), KVW, 1)
        second = jnp.where(last, recent_ref[1, pl.ds(slot, 1), :], second)
        place(second, pl.multiple_of(pairs + at, HALF))
        return carry

    lax.fori_loop(0, GROUP, one, 0, unroll=4)

    column = lax.broadcasted_iota(jnp.int32, (GROUP, KEYS), 1)
    row = lax.broadcasted_iota(jnp.int32, (GROUP, KEYS), 0)
    half = (column >= pairs).astype(jnp.int32)
    within = column - half * pairs
    position = 2 * (within % HALF) + half
    cached = position < len_ref[...]
    for step in range(STEPS):
        recent = (position >= LIVE) & (position <= LIVE + step)
        allowed = (cached | recent) & (within // HALF == row)
        bias_ref[pl.ds(step * GROUP, GROUP), :] = jnp.where(allowed, 0.0, -jnp.inf)

    def heads(index, carry):
        bias = jnp.concatenate([bias_ref[...]] * TOGETHER, axis=0)
        for odd in range(2):
            slabs = []
            for k in range(TOGETHER):
                start = pl.multiple_of((index * TOGETHER + k) * 2 * KVW + odd * LAT, 128)
                for step in range(STEPS):
                    slabs.append(query_ref[step, :, pl.ds(start, WIDE)])
            keys = odd_ref[...] if odd else even_ref[...]
            score = lax.dot_general(
                jnp.concatenate(slabs, axis=0),
                keys,
                (((1,), (1,)), ((), ())),
                preferred_element_type=jnp.float32,
            )
            score = score + bias
            weight = jnp.exp2((score - jnp.max(score, axis=1, keepdims=True)) * base_two_scale)
            total = jnp.sum(weight, axis=1, keepdims=True)
            mixed = jnp.dot(
                weight.astype(jnp.bfloat16), value_ref[...], preferred_element_type=jnp.float32
            )
            mixed = (mixed * (1.0 / total)).astype(jnp.bfloat16)
            for k in range(TOGETHER):
                start = pl.multiple_of(((index * TOGETHER + k) * 2 + odd) * LAT, LAT)
                for step in range(STEPS):
                    at = (k * STEPS + step) * GROUP
                    out_ref[step, :, pl.ds(start, LAT)] = mixed[at : at + GROUP]
        return carry

    lax.fori_loop(0, H // (2 * TOGETHER), heads, 0, unroll=2)


def attend(queries, new_kv, got, landing, placed_len, earlier):
    slots = queries.shape[1]
    group = 0 if earlier is None else 1
    specs = [
        pl.BlockSpec(memory_space=pltpu.SMEM),
        pl.BlockSpec(memory_space=pltpu.VMEM),
        pl.BlockSpec((GROUP, 1), lambda g: (group, 0)),
        pl.BlockSpec((STEPS, GROUP, KVW), lambda g: (0, group, 0)),
        pl.BlockSpec((STEPS, GROUP, H * KVW), lambda g: (0, group, 0)),
    ]
    operands = [landing[group * GROUP :][:GROUP], got, placed_len[:, None], new_kv, queries]
    kernel = attend_kernel
    if earlier is not None:
        specs.append(pl.BlockSpec(memory_space=pl.ANY))
        operands.append(earlier)

        def kernel(*refs):
            attend_kernel(*refs[:5], *refs[6:])

    return pl.pallas_call(
        kernel,
        grid=(1,),
        out_shape=jax.ShapeDtypeStruct((STEPS, slots, H * LAT), jnp.bfloat16),
        in_specs=specs,
        out_specs=pl.BlockSpec((STEPS, GROUP, H * LAT), lambda g: (0, group, 0)),
        scratch_shapes=[
            pltpu.VMEM((KEYS, WIDE), jnp.bfloat16),
            pltpu.VMEM((KEYS, WIDE), jnp.bfloat16),
            pltpu.VMEM((KEYS, LAT), jnp.bfloat16),
            pltpu.VMEM((STEPS * GROUP, KEYS), jnp.float32),
            pltpu.VMEM((STEPS, GROUP, WIDE), jnp.float32),
        ],
        input_output_aliases={} if earlier is None else {5: 0},
        compiler_params=pltpu.CompilerParams(vmem_limit_bytes=32 * 2**20),
        cost_estimate=pl.CostEstimate(
            flops=2 * STEPS * GROUP * H * KEYS * (WIDE + LAT),
            bytes_accessed=2 * STEPS * GROUP * H * (KVW + LAT),
            transcendentals=STEPS * GROUP * H * KEYS,
        ),
    )(*operands)


def hop(value, strides, delta):
    pairs = []
    for core, stride in enumerate(strides):
        for chip in range(CHIPS):
            place = chip // stride % SIDE
            there = chip + ((place + delta) % SIDE - place) * stride
            pairs.append((core * CHIPS + chip, core * CHIPS + there))
    return lax.ppermute(value, ("dp", "ep"), pairs)


def chip_at(stride, delta, start):
    place = start // stride % SIDE
    return start + ((place + delta) % SIDE - place) * stride


def pick_matrix(targets_ref, ids):
    hits = [
        jnp.sum((ids == targets_ref[j].astype(jnp.float32)).astype(jnp.float32), axis=0, keepdims=True)
        for j in range(SIDE)
    ]
    before = lax.broadcasted_iota(jnp.int32, (LINE, LINE), 0)
    after = lax.broadcasted_iota(jnp.int32, (LINE, LINE), 1)
    earlier = ((before // SLOTS == after // SLOTS) & (before < after)).astype(jnp.bfloat16)
    stacked = jnp.concatenate(hits + hits, axis=0).astype(jnp.bfloat16)
    ranks = jnp.dot(stacked, earlier, preferred_element_type=jnp.float32)
    base = (lax.broadcasted_iota(jnp.int32, (1, LINE), 1) // SLOTS * CAPE).astype(jnp.float32)
    rows = lax.broadcasted_iota(jnp.int32, (SIDE * PICKS, LINE), 0).astype(jnp.float32)
    picks = []
    for j in range(SIDE):
        place = jnp.where(hits[j] > 0.0, base + ranks[j : j + 1], -1.0)
        picks.append((rows == place).astype(jnp.float32))
    return jnp.concatenate(picks, axis=0).astype(jnp.bfloat16)


def select_kernel(targets_ref, *refs):
    pieces, outs, ids_ref = refs[:SIDE], refs[SIDE : 2 * SIDE], refs[2 * SIDE]
    width = pieces[0].shape[1]
    for line in range(SIDE):
        piece = pieces[line][...]
        ids = piece[:, width - MARK :].astype(jnp.float32).T[:TOPK]
        ids_ref[line] = ids
        picks = pick_matrix(targets_ref, ids)
        rows = jnp.dot(picks, piece, preferred_element_type=jnp.float32).astype(jnp.bfloat16)
        rows = rows.reshape(SIDE, SIDE, PICKS, width)
        for j in range(SIDE):
            outs[j][pl.ds(line * SIDE, SIDE)] = rows[j]


def select(targets, pieces):
    width = pieces[0].shape[1]
    vmem = pl.BlockSpec(memory_space=pltpu.VMEM)
    return pl.pallas_call(
        select_kernel,
        out_shape=[jax.ShapeDtypeStruct((PLANE, PICKS, width), jnp.bfloat16)] * SIDE
        + [jax.ShapeDtypeStruct((SIDE, TOPK, LINE), jnp.float32)],
        in_specs=[pl.BlockSpec(memory_space=pltpu.SMEM)] + [vmem] * SIDE,
        out_specs=[vmem] * (SIDE + 1),
        compiler_params=pltpu.CompilerParams(vmem_limit_bytes=32 * 2**20),
        cost_estimate=pl.CostEstimate(
            flops=2 * SIDE * LINE * LINE * width, bytes_accessed=4 * SIDE * LINE * width, transcendentals=0
        ),
    )(targets, *pieces)


def combine_kernel(targets_ref, ids_ref, *refs):
    width = refs[0].shape[2]
    for line in range(SIDE):
        picks = pick_matrix(targets_ref, ids_ref[line])
        blocks = [ref[pl.ds(line * SIDE, SIDE)] for ref in refs[:SIDE]]
        rows = jnp.concatenate([b.reshape(SIDE * PICKS, width) for b in blocks], axis=0)
        total = lax.dot_general(
            picks, rows, (((0,), (0,)), ((), ())), preferred_element_type=jnp.float32
        )
        refs[SIDE + line][...] = total.astype(jnp.bfloat16)


def combine(targets, ids, blocks):
    width = blocks[0].shape[2]
    vmem = pl.BlockSpec(memory_space=pltpu.VMEM)
    return pl.pallas_call(
        combine_kernel,
        out_shape=[jax.ShapeDtypeStruct((LINE, width), jnp.bfloat16)] * SIDE,
        in_specs=[pl.BlockSpec(memory_space=pltpu.SMEM)] + [vmem] * (1 + SIDE),
        out_specs=[vmem] * SIDE,
        compiler_params=pltpu.CompilerParams(vmem_limit_bytes=32 * 2**20),
        cost_estimate=pl.CostEstimate(
            flops=2 * SIDE * LINE * LINE * width, bytes_accessed=4 * SIDE * LINE * width, transcendentals=0
        ),
    )(targets, ids, *blocks)


def together(*trees):
    return lax.optimization_barrier(trees)


def stage_axes():
    return [[tuple(by_core[n] for by_core in orders) for orders in ORDERS] for n in range(3)]


def exchange(blocks, strides, deltas):
    return [hop(block, strides, delta) for block, delta in zip(blocks, deltas)]


def send_rows(columns, targets, packed_cache):
    first, second, third = stage_axes()
    both = range(len(columns))
    rings = [exchange([columns[i]] * 3, first[i], (1, -1, 2)) for i in both]
    columns, rings = together(columns, rings)
    lines = [jnp.concatenate([columns[i]] + rings[i], axis=0) for i in both]
    rings = [exchange([lines[i]] * 3, second[i], (1, -1, 2)) for i in both]
    lines, rings = together(lines, rings)
    picked = [select(targets[i], [lines[i]] + rings[i]) for i in both]
    rings = [exchange(picked[i][1:SIDE], third[i], TARGETS[1:]) for i in both]
    packed_cache, rings[1][0] = together(packed_cache, rings[1][0])
    return [[picked[i][0]] + rings[i] for i in both], [p[SIDE] for p in picked], packed_cache


def return_rows(outward, targets, ids, contexts):
    first, second, third = stage_axes()
    both = range(len(outward))
    rings = [exchange(outward[i][1:], third[i], (-1, 1, 2)) for i in both]
    context = contexts(None)
    rings, context = together(rings, context)
    lines = [combine(targets[i], ids[i], [outward[i][0]] + rings[i]) for i in both]
    rings = [exchange(lines[i][1:], second[i], (-1, 1, 2)) for i in both]
    context = contexts(context)
    rings, context = together(rings, context)
    sums = []
    for i in both:
        line = add(lines[i][0], *rings[i])
        blocks = [line[k * ROWS : (k + 1) * ROWS] for k in range(SIDE)]
        sums.append([blocks[0]] + exchange(blocks[1:], first[i], (-1, 1, 2)))
    sums, = together(sums)
    return [add(*terms) for terms in sums], context


def add(*terms):
    return sum(t.astype(jnp.float32) for t in terms).astype(jnp.bfloat16)


def half_expert(rows, gate_ref, up_ref):
    gate_pre = jnp.dot(rows, gate_ref[...], preferred_element_type=jnp.float32)
    up_pre = jnp.dot(rows, up_ref[...], preferred_element_type=jnp.float32)
    return (gate_pre * (1.0 / (1.0 + jnp.exp(-gate_pre))) * up_pre).astype(jnp.bfloat16)


def first_half_kernel(order_ref, me_ref, *refs):
    main, minor = refs[:SIDE], refs[SIDE : 2 * SIDE]
    gate_ref, up_ref, down_ref, rows_ref, part_ref, weight_ref = refs[2 * SIDE :]

    def one(group, carry):
        for j in range(SIDE):
            number = j * PLANE + group
            rows_ref[number, :, pl.ds(0, MAIN)] = main[j][group, :, pl.ds(0, MAIN)]
            rows_ref[order_ref[number], :, pl.ds(MAIN, MINOR)] = minor[j][group, :, pl.ds(0, MINOR)]
            mark = main[j][group, :, pl.ds(MAIN, MARK)].astype(jnp.float32)
            total = sum(pltpu.roll(mark, MARK - k * TOPK, 1) for k in range(1, 4))
            lane = lax.broadcasted_iota(jnp.int32, mark.shape, 1)
            mine = (lane < TOPK) & (mark == me_ref[0].astype(jnp.float32))
            total = jnp.sum(jnp.where(mine, total, 0.0), axis=1, keepdims=True)
            weight_ref[number] = jnp.broadcast_to(total, mark.shape)
        return carry

    lax.fori_loop(0, PLANE, one, 0)

    def block(index, carry):
        at = pl.ds(index * BLOCK, BLOCK)
        rows = rows_ref[at].reshape(BLOCK * PICKS, D)
        inner = half_expert(rows, gate_ref, up_ref)
        for start in range(0, D, LAT):
            part = jnp.dot(inner, down_ref[:, start : start + LAT], preferred_element_type=jnp.float32)
            part_ref[at, :, pl.ds(start, LAT)] = part.astype(jnp.bfloat16).reshape(BLOCK, PICKS, LAT)
        return carry

    lax.fori_loop(0, CHIPS // BLOCK, block, 0)


def second_half_kernel(order_ref, rows_ref, part_ref, weight_ref, gate_ref, up_ref, down_ref, *refs):
    main, minor, out_ref = refs[:SIDE], refs[SIDE : 2 * SIDE], refs[2 * SIDE]

    def block(index, carry):
        at = pl.ds(index * BLOCK, BLOCK)
        rows = rows_ref[at].reshape(BLOCK * PICKS, D)
        inner = half_expert(rows, gate_ref, up_ref)
        weight = weight_ref[at].reshape(BLOCK * PICKS, MARK)
        weight = jnp.concatenate([weight] * (LAT // MARK), axis=1)
        for start in range(0, D, LAT):
            part = jnp.dot(inner, down_ref[:, start : start + LAT], preferred_element_type=jnp.float32)
            earlier = part_ref[at, :, pl.ds(start, LAT)].reshape(BLOCK * PICKS, LAT)
            total = (earlier.astype(jnp.float32) + part) * weight
            out_ref[at, :, pl.ds(start, LAT)] = total.astype(jnp.bfloat16).reshape(BLOCK, PICKS, LAT)
        return carry

    lax.fori_loop(0, CHIPS // BLOCK, block, 0)

    def one(group, carry):
        for j in range(SIDE):
            number = j * PLANE + group
            main[j][group] = out_ref[number, :, pl.ds(0, MAIN)]
            minor[j][group] = out_ref[order_ref[number], :, pl.ds(MAIN, MINOR)]
        return carry

    lax.fori_loop(0, PLANE, one, 0)


HALF_COST = pl.CostEstimate(
    flops=2 * CHIPS * PICKS * D * 512 * 3, bytes_accessed=2 * (3 * D * 512 + 3 * CHIPS * PICKS * D), transcendentals=CHIPS * PICKS * 512
)


def first_half(order, me, main, minor, matrices):
    vmem, smem = pl.BlockSpec(memory_space=pltpu.VMEM), pl.BlockSpec(memory_space=pltpu.SMEM)
    whole = jax.ShapeDtypeStruct((CHIPS, PICKS, D), jnp.bfloat16)
    return pl.pallas_call(
        first_half_kernel,
        out_shape=[whole, whole, jax.ShapeDtypeStruct((CHIPS, PICKS, MARK), jnp.float32)],
        in_specs=[smem, smem] + [vmem] * (2 * SIDE + 3),
        out_specs=[vmem] * 3,
        compiler_params=pltpu.CompilerParams(vmem_limit_bytes=52 * 2**20),
        cost_estimate=HALF_COST,
    )(order, me[None], *main, *minor, *matrices)


def second_half(order, rows, part, weight, matrices):
    vmem, smem = pl.BlockSpec(memory_space=pltpu.VMEM), pl.BlockSpec(memory_space=pltpu.SMEM)
    shapes = [(PLANE, PICKS, width) for width in (MAIN, MINOR) for _ in range(SIDE)]
    outs = pl.pallas_call(
        second_half_kernel,
        out_shape=[jax.ShapeDtypeStruct(shape, jnp.bfloat16) for shape in shapes],
        in_specs=[smem] + [vmem] * 6,
        out_specs=[vmem] * (2 * SIDE),
        scratch_shapes=[pltpu.VMEM((CHIPS, PICKS, D), jnp.bfloat16)],
        compiler_params=pltpu.CompilerParams(vmem_limit_bytes=52 * 2**20),
        cost_estimate=HALF_COST,
    )(order, rows, part, weight, *matrices)
    return outs[:SIDE], outs[SIDE:]


def three_parts(weights):
    high = lax.reduce_precision(weights, 8, 7)
    rest = weights - high
    mid = lax.reduce_precision(rest, 8, 7)
    return [part.astype(jnp.bfloat16) for part in (high, mid, rest - mid)]


def pack_kernel(from_ref, slot_ref, len_ref, cache_ref, out_ref):
    row = lax.broadcasted_iota(jnp.int32, (HALF, 128), 0)
    lane = lax.broadcasted_iota(jnp.int32, (HALF, 128), 1)

    def one(chip, carry):
        block = cache_ref[from_ref[chip]]
        out_ref[chip] = block
        mark = jnp.where(lane == 0, slot_ref[chip], len_ref[chip]).astype(jnp.float32)
        head = jnp.where((row == HALF - 1) & (lane < 2), mark, block[:, :128].astype(jnp.float32))
        out_ref[chip, :, pl.ds(0, 128)] = head.astype(jnp.bfloat16)
        return carry

    lax.fori_loop(0, out_ref.shape[0], one, 0)


def pack_cache(send_from, sent_slot, sent_len, cache):
    chips = send_from.shape[0]
    small = pl.BlockSpec(memory_space=pltpu.SMEM)
    return pl.pallas_call(
        pack_kernel,
        out_shape=jax.ShapeDtypeStruct((chips,) + cache.shape[1:], jnp.bfloat16),
        in_specs=[small, small, small, pl.BlockSpec(memory_space=pltpu.VMEM)],
        out_specs=pl.BlockSpec(memory_space=pltpu.VMEM),
        compiler_params=pltpu.CompilerParams(vmem_limit_bytes=24 * 2**20),
        cost_estimate=pl.CostEstimate(
            flops=0, bytes_accessed=2 * (chips + cache.shape[0]) * CTX * KVW, transcendentals=0
        ),
    )(send_from, sent_slot, sent_len, cache)


def on_device(
    kv_cache,
    lengths,
    move_list,
    queries,
    new_kv,
    hidden,
    expert_ids,
    gate_weights,
    expert_gate,
    expert_up,
    expert_down,
):
    ep_count = lax.axis_size("ep")
    slot_count = lengths.shape[0]
    own = (expert_gate[0], expert_up[0], expert_down[0])
    expert_range = jnp.arange(ep_count, dtype=jnp.int32)
    me = lax.axis_index("ep")
    core = lax.axis_index("dp")

    marks = [expert_ids.astype(jnp.bfloat16)] + three_parts(gate_weights)
    marks = jnp.concatenate(marks, axis=2).reshape(ROWS, 4 * TOPK)
    marks = jnp.pad(marks, ((0, 0), (0, MARK - 4 * TOPK)))
    rows = hidden.reshape(ROWS, D)
    columns = [
        jnp.concatenate([block, marks], axis=1) for block in (rows[:, :MAIN], rows[:, MAIN:])
    ]
    targets = []
    for orders in ORDERS:
        stride = jnp.where(core == 0, orders[0][2], orders[1][2])
        targets.append(
            jnp.stack([chip_at(stride, delta, me) for delta in TARGETS]).astype(jnp.int32)
        )
    slot_range = jnp.arange(slot_count, dtype=jnp.int32)
    send_hit = expert_range[:, None] == move_list[:, 0][None, :]
    send_from = jnp.sum(jnp.where(send_hit, slot_range[None, :], 0), axis=1)
    sent_slot = jnp.sum(jnp.where(send_hit, move_list[:, 1][None, :] + 1, 0), axis=1) - 1
    sent_len = jnp.sum(jnp.where(send_hit, lengths[None, :], 0), axis=1)
    packed_cache = pack_cache(
        send_from, sent_slot, sent_len, kv_cache.reshape(slot_count, HALF, 2 * KVW)
    )
    arrived, ids, packed_cache = send_rows(columns, targets, packed_cache)
    got = lax.all_to_all(packed_cache, "ep", split_axis=0, concat_axis=0, tiled=True)
    arrived, own = together(arrived, own)
    other = tuple(lax.ppermute(w, "dp", [(0, 1), (1, 0)]) for w in own)

    tables = []
    for main, minor in zip(*ORDERS):
        table = [0] * CHIPS
        for number in range(CHIPS):
            digits = (number // PLANE, number // SIDE % SIDE, number % SIDE)
            place = dict(zip(main, digits[::-1]))
            index = place[minor[2]] * PLANE + place[minor[1]] * SIDE + place[minor[0]]
            table[index] = number
        tables.append(jnp.array(table, jnp.int32))
    order = jnp.where(core == 0, tables[0], tables[1])
    rows, part, weight = first_half(order, me, arrived[0], arrived[1], own)
    outward = second_half(order, rows, part, weight, other)
    outward, got = lax.optimization_barrier((outward, got))
    got_mark = lax.optimization_barrier(got[:, HALF - 1, :128]).astype(jnp.int32)
    got_slot, got_len = got_mark[:, 0], got_mark[:, 1]
    land_hit = got_slot[None, :] == slot_range[:, None]
    landing = jnp.sum(jnp.where(land_hit, expert_range[None, :], 0), axis=1)
    placed_len = jnp.sum(jnp.where(land_hit, got_len[None, :], 0), axis=1)

    def contexts(earlier):
        return attend(queries, new_kv, got, landing, placed_len, earlier)

    sums, context = return_rows(outward, targets, ids, contexts)
    mixture = jnp.concatenate(sums, axis=1).reshape(STEPS, SLOTS, D)
    return context, mixture


def solution(mesh):
    return jax.shard_map(
        on_device,
        mesh=mesh,
        in_specs=(
            P(("dp", "ep"), None),
            P(("dp", "ep")),
            P(("dp", "ep"), None),
            P(None, ("dp", "ep"), None),
            P(None, ("dp", "ep"), None),
            P(None, ("dp", "ep"), None),
            P(None, ("dp", "ep"), None),
            P(None, ("dp", "ep"), None),
            P("ep", None, "dp"),
            P("ep", None, "dp"),
            P("ep", "dp", None),
        ),
        out_specs=(P(None, ("dp", "ep"), None), P(None, ("dp", "ep"), None)),
        check_vma=False,
    )
```
